512 devices in a mesh: gx: 8 (over y), gy: 8 (over z_lo, core), gz: 8 (over x, z_hi).
Axes of the slice: x: 4, y: 8, z: 8 (z_hi: 2, z_lo: 4; z = z_hi * 4 + z_lo), core: 2. Of those that a mesh axis runs over, the one named last changes fastest.
Arguments:
- coords: float32 [8, 8, 8, 3, 128], P('gx', 'gy', 'gz'), may hold values from 0 to 16, as said below
- species: int32 [8, 8, 8, 128], P('gx', 'gy', 'gz'), may hold values from 0 to 1
- pair_ids: int32 [8, 8, 8, 2, 256], P('gx', 'gy', 'gz'), may hold values from 0 to 3455, as said below
- live_counts: int32 [8, 8, 8, 2], P('gx', 'gy', 'gz'), may hold values from 4 to 128, as said below
- w_two_in: bfloat16 [512, 12], replicated, may hold values from -1.75 to 1.75
- w_two_hid: bfloat16 [512, 512], replicated, may hold values from -0.25 to 0.25
- w_env: bfloat16 [64, 512], replicated, may hold values from -0.25 to 0.25
- w_latent: bfloat16 [512, 704], replicated, may hold values from -0.21875 to 0.21875
- w_out: bfloat16 [1, 512], replicated, may hold values from -0.25 to 0.25
Outputs:
- forces: float32 [8, 8, 8, 3, 128], P('gx', 'gy', 'gz')
- energy: float32 [], replicated
The draws below stay inside these ranges and needn't reach their ends.
Inputs may be any that keep to these rules, and one draw needn't show every extreme that they name: `coords`: each atom lies inside its domain: x and y below 16, z below 4. `pair_ids`: row 0 holds centres: slots of the first 128 of a domain's list name atoms below 64, the others atoms at or above it. Row 1 is s * 128 + a for atom a of slot s, never the centre itself in slot 13; every neighbour lies within 6 Angstrom of its centre. `live_counts`: slots of a half at or beyond its count are padding and carry no weight.
All inputs are finite; a program needn't handle non-finite values.
Results may differ from the reference program's by a relative error of at most 0.017.
Values sent between devices are 32-bit elements; how exact they have to be, the bound alone decides.
No kernel may reach another device: no remote copies, remote signals or barrier semaphores. Data moves between devices by JAX's collectives and lax.ppermute only.
A program may use at most 64 MiB of HBM per device.

```python
import math
import jax
import jax.numpy as jnp
import numpy as np
from jax import lax

ATOMS = 128
SIDE = 8
PAIRS = 256
LAT = 512
CH = 64
NB = 8
NS = 2
HALF = 128
N_GX = 8
N_GY = 8
N_GZ = 8


def offset_table():
    rows = []
    for step_x in range(-2, 3):
        for step_y in range(-2, 3):
            for step_z in range(-2, 3):
                square = step_x * step_x + step_y * step_y + step_z * step_z
                if square >= 1 and square <= 6:
                    rows.append([step_x, step_y, step_z])
    return np.array(rows, dtype=np.int32)


def draw_coords(key, part):
    key = jax.random.fold_in(key, 5)
    key_amount = jax.random.fold_in(key, 0)
    leading = (N_GX, N_GY, N_GZ)
    atom_index = jnp.arange(ATOMS)
    lattice = jnp.stack([atom_index % SIDE, atom_index // SIDE % SIDE, atom_index // (SIDE * SIDE)], axis=0).astype(jnp.float32)
    centres = 2.0 * lattice + 1.0
    jitter = jax.random.uniform(key_amount, leading + (3, ATOMS), jnp.float32, -0.25, 0.25)
    return (centres + jitter).astype(jnp.float32)


def draw_pair_ids(key, part):
    key = jax.random.fold_in(key, 11)
    key_lower, key_upper, key_pick = jax.random.split(key, 3)
    leading = (N_GX, N_GY, N_GZ)
    lower = jax.random.randint(key_lower, leading + (PAIRS // 2,), 0, ATOMS // 2)
    upper = jax.random.randint(key_upper, leading + (PAIRS // 2,), ATOMS // 2, ATOMS)
    centre = jnp.concatenate([lower, upper], axis=-1).astype(jnp.int32)
    table = jnp.asarray(offset_table(), dtype=jnp.int32)
    pick = jax.random.randint(key_pick, leading + (PAIRS,), 0, table.shape[0])
    moves = table[pick]
    planes = ATOMS // (SIDE * SIDE)
    along_x = centre % SIDE + moves[..., 0]
    along_y = centre // SIDE % SIDE + moves[..., 1]
    along_z = centre // (SIDE * SIDE) + moves[..., 2]
    shift_x = jnp.floor_divide(along_x, SIDE)
    shift_y = jnp.floor_divide(along_y, SIDE)
    shift_z = jnp.floor_divide(along_z, planes)
    member = along_x - shift_x * SIDE + SIDE * (along_y - shift_y * SIDE) + SIDE * SIDE * (along_z - shift_z * planes)
    slot = 9 * (shift_x + 1) + 3 * (shift_y + 1) + (shift_z + 1)
    return jnp.stack([centre, slot * ATOMS + member], axis=3).astype(jnp.int32)


def draw_live_counts(key, part):
    key = jax.random.fold_in(key, 23)
    key_mode, key_sx, key_sy, key_sz, key_sparse = jax.random.split(key, 5)
    wide = jax.random.randint(key_mode, (), 0, 10) < 3
    span_x = jnp.where(wide, N_GX - max(1, N_GX // 8), max(1, N_GX // 2))
    span_y = jnp.where(wide, max(1, 5 * N_GY // 8), max(1, N_GY // 2))
    span_z = jnp.where(wide, N_GZ // 2, max(1, N_GZ // 4))
    start_x = jax.random.randint(key_sx, (), 0, N_GX)
    start_y = jax.random.randint(key_sy, (), 0, N_GY)
    start_z = jax.random.randint(key_sz, (), 0, N_GZ)
    inside_x = (jnp.arange(N_GX) - start_x) % N_GX < span_x
    inside_y = (jnp.arange(N_GY) - start_y) % N_GY < span_y
    inside_z = (jnp.arange(N_GZ) - start_z) % N_GZ < span_z
    liquid = inside_x[:, None, None] & inside_y[None, :, None] & inside_z[None, None, :]
    half_slots = PAIRS // 2
    sparse = jax.random.randint(key_sparse, (N_GX, N_GY, N_GZ, 2), half_slots // 32, half_slots // 16 + 1)
    filled = jnp.full((N_GX, N_GY, N_GZ, 2), half_slots, jnp.int32)
    return jnp.where(liquid[:, :, :, None], filled, sparse).astype(jnp.int32)


def place_ends(values, key, least, top_value):
    index_at = [jax.random.randint(jax.random.fold_in(key, axis), (), 0, length) for axis, length in enumerate(values.shape)]
    main_axis = values.shape.index(max(values.shape))
    beside = index_at[:main_axis] + [(index_at[main_axis] + 1) % values.shape[main_axis]] + index_at[main_axis + 1:]
    return values.at[tuple(index_at)].set(least).at[tuple(beside)].set(top_value)


def bell_draw(key, shape, spread, bound, kind=jnp.bfloat16):
    values = jax.random.normal(key, shape, jnp.float32) * spread
    return jnp.minimum(jnp.maximum(values, -bound), bound).astype(kind)


def setup_inputs(seed: int = 0) -> dict:
    seeds = jax.random.split(jax.random.key(seed), 10)
    coords = draw_coords(jax.random.fold_in(seeds[9], 71), 0)
    species = place_ends(jax.random.randint(seeds[1], (N_GX, N_GY, N_GZ, ATOMS), 0, NS), jax.random.fold_in(seeds[1], 1), 0, NS - 1).astype(jnp.int32)
    pair_ids = draw_pair_ids(jax.random.fold_in(seeds[9], 71), 0)
    live_counts = draw_live_counts(jax.random.fold_in(seeds[9], 71), 0)
    w_two_in = bell_draw(seeds[4], (LAT, NB + 2 * NS), (NB + 2 * NS) ** -0.5, 1.75)
    w_two_hid = bell_draw(seeds[5], (LAT, LAT), LAT ** -0.5, 0.25)
    w_env = bell_draw(seeds[6], (CH, LAT), LAT ** -0.5, 0.25)
    w_latent = bell_draw(seeds[7], (LAT, LAT + 3 * CH), (LAT + 3 * CH) ** -0.5, 0.21875)
    w_out = bell_draw(seeds[8], (1, LAT), LAT ** -0.5, 0.25)
    return dict(coords=coords, species=species, pair_ids=pair_ids, live_counts=live_counts, w_two_in=w_two_in, w_two_hid=w_two_hid, w_env=w_env, w_latent=w_latent, w_out=w_out)


cutoff_radius = 6.0
spacing = 2.0
soften = 0.01
env_norm = 0.25

def envelope(ratio):
    poly = 1.0 - 28.0 * ratio ** 6 + 48.0 * ratio ** 7 - 21.0 * ratio ** 8
    return jnp.where(ratio < 1.0, poly, 0.0 * ratio)

def harmonics(direction):
    along_x, along_y, along_z = (direction[0], direction[1], direction[2])
    root3 = math.sqrt(3.0)
    root15 = math.sqrt(15.0)
    root5 = math.sqrt(5.0)
    rows = [jnp.ones_like(along_x), root3 * along_x, root3 * along_y, root3 * along_z, root15 * along_x * along_y, root15 * along_y * along_z, 0.5 * root5 * (2.0 * along_z * along_z - along_x * along_x - along_y * along_y), root15 * along_x * along_z, 0.5 * root15 * (along_x * along_x - along_y * along_y)]
    return jnp.stack(rows, axis=0)

def placed(coords_block):
    atoms = coords_block.shape[-1]
    planes = atoms // (SIDE * SIDE)
    slots = jnp.arange(27)
    steps_grid = jnp.stack([slots // 9 - 1, slots // 3 % 3 - 1, slots % 3 - 1], axis=1).astype(jnp.float32)
    extent = jnp.array([spacing * SIDE, spacing * SIDE, spacing * planes], jnp.float32)
    moved = coords_block + (steps_grid * extent[None, :])[:, :, None]
    return jnp.transpose(moved, (1, 0, 2)).reshape(3, 27 * atoms)

def edge_terms(coords_flat, species_flat, centre, neighbour, live_mask, w_two_in, w_two_hid, w_env):
    atoms = species_flat.shape[0] // 27
    own_coords = coords_flat[:, 13 * atoms:14 * atoms]
    own_species = species_flat[13 * atoms:14 * atoms]
    delta = jnp.take(coords_flat, neighbour, axis=1) - jnp.take(own_coords, centre, axis=1)
    radius = jnp.sqrt(lax.optimization_barrier(jnp.sum(delta * delta, axis=0)) + soften)
    weight_cut = envelope(radius / cutoff_radius) * live_mask
    orders = jnp.arange(1, NB + 1).astype(jnp.float32)[:, None]
    bessel = math.sqrt(2.0 / cutoff_radius) * jnp.sin(orders * (math.pi / cutoff_radius) * radius[None, :]) / radius[None, :]
    kinds = jnp.arange(NS).astype(jnp.float32)[:, None]
    centre_kind = (jnp.take(own_species, centre)[None, :] == kinds).astype(jnp.float32)
    neighbour_kind = (jnp.take(species_flat, neighbour)[None, :] == kinds).astype(jnp.float32)
    features = jnp.concatenate([bessel * weight_cut[None, :], centre_kind, neighbour_kind], axis=0).astype(jnp.bfloat16)
    first_hidden = jax.nn.silu(jnp.dot(w_two_in, features, preferred_element_type=jnp.float32)).astype(jnp.bfloat16)
    latent = (jax.nn.silu(jnp.dot(w_two_hid, first_hidden, preferred_element_type=jnp.float32)) * weight_cut[None, :]).astype(jnp.bfloat16)
    env_weight = jnp.dot(w_env, latent, preferred_element_type=jnp.float32)
    vectors = env_weight[:, None, :] * harmonics(delta / radius[None, :])[None, :, :]
    return (latent, vectors, weight_cut)

def pair_energy(latent, vectors, weight_cut, env_at, w_latent, w_out):
    product = env_at * vectors
    invariants = jnp.concatenate([lax.optimization_barrier(jnp.sum(product[:, 0:1], axis=1)), lax.optimization_barrier(jnp.sum(product[:, 1:4], axis=1)), lax.optimization_barrier(jnp.sum(product[:, 4:9], axis=1))], axis=0).astype(jnp.bfloat16)
    joined = jnp.concatenate([latent, invariants], axis=0)
    update = jax.nn.silu(jnp.dot(w_latent, joined, preferred_element_type=jnp.float32)) * weight_cut[None, :]
    updated = (latent.astype(jnp.float32) + update).astype(jnp.bfloat16)
    return jnp.sum(jnp.dot(w_out, updated, preferred_element_type=jnp.float32))

def domain_energy(coords_block, species_flat, ids, counts, weights):
    w_two_in, w_two_hid, w_env, w_latent, w_out = weights
    coords_flat = placed(coords_block)
    channels = w_env.shape[0]
    total = jnp.zeros((), jnp.float32)
    for which in range(2):
        centre = ids[0, which * HALF:(which + 1) * HALF]
        neighbour = ids[1, which * HALF:(which + 1) * HALF]
        live_mask = (jnp.arange(HALF) < counts[which]).astype(jnp.float32)
        latent, vectors, weight_cut = edge_terms(coords_flat, species_flat, centre, neighbour, live_mask, w_two_in, w_two_hid, w_env)
        environment = env_norm * jax.ops.segment_sum(vectors.reshape(channels * 9, HALF).T, centre, num_segments=ATOMS)
        env_at = jnp.take(environment, centre, axis=0).T.reshape(channels, 9, HALF)
        total = total + pair_energy(latent, vectors, weight_cut, env_at, w_latent, w_out)
    return total

def frames(field):
    blocks = []
    for off_x in (-1, 0, 1):
        for off_y in (-1, 0, 1):
            for off_z in (-1, 0, 1):
                blocks.append(jnp.roll(field, (-off_x, -off_y, -off_z), axis=(0, 1, 2)))
    return jnp.stack(blocks, axis=3)

def reference(coords, species, pair_ids, live_counts, w_two_in, w_two_hid, w_env, w_latent, w_out):
    domains = N_GX * N_GY * N_GZ
    weights = (w_two_in, w_two_hid, w_env, w_latent, w_out)
    species_ext = frames(species.astype(jnp.float32)).reshape(domains, 27 * ATOMS)
    ids = pair_ids.reshape(domains, 2, PAIRS)
    counts = live_counts.reshape(domains, 2)

    def whole(coords_all):
        coords_ext = frames(coords_all).reshape(domains, 27, 3, ATOMS)

        def single(operands):
            return domain_energy(operands[0], operands[1], operands[2], operands[3], weights)
        energies = lax.map(single, (coords_ext, species_ext, ids, counts))
        return jnp.sum(energies)
    total, gradient = jax.value_and_grad(whole)(coords)
    return (-gradient, total / (ATOMS * domains))
```

```python
import math

import jax
import jax.numpy as jnp
from jax import lax
from jax.experimental import pallas as pl
from jax.experimental.pallas import tpu as pltpu
from jax.sharding import PartitionSpec as P

F32 = jnp.float32
BF16 = jnp.bfloat16
CUTOFF = 6.0
SOFTEN = 0.01
ENV_NORM = 0.25
EXTENT = (16.0, 16.0, 4.0)
ROOT3 = math.sqrt(3.0)
ROOT5 = math.sqrt(5.0)
ROOT15 = math.sqrt(15.0)
DEGREE = (0, 1, 1, 1, 2, 2, 2, 2, 2)
RING = 8
LAT = 512
CH = 64
PAIRS = 256
ATOMS = 128
ROWS = 64
ENERGY_ROW = 27


def column_sum(block):
    return jnp.sum(block, axis=0, keepdims=True)


def folded(block):
    return jnp.sum(block.reshape(block.shape[0] // 8, 8, block.shape[1]), axis=0)


def silu_parts(z):
    gate = 0.5 * jnp.tanh(0.5 * z) + 0.5
    value = z * gate
    return value, gate + value * (1.0 - gate)


def split_dot(block, square):
    high = block.astype(BF16)
    low = (block - high.astype(F32)).astype(BF16)
    return jnp.dot(high, square, preferred_element_type=F32) + jnp.dot(
        low, square, preferred_element_type=F32
    )


def split_dot_nt(block, other):
    dims = (((1,), (1,)), ((), ()))
    high = block.astype(BF16)
    low = (block - high.astype(F32)).astype(BF16)
    return lax.dot_general(high, other, dims, preferred_element_type=F32) + lax.dot_general(
        low, other, dims, preferred_element_type=F32
    )


def force_kernel(
    place_ref,
    counts_ref,
    ids_ref,
    below_ref,
    level_ref,
    above_ref,
    same_ref,
    w_in_ref,
    w_in_t_ref,
    w_hid_ref,
    w_hid_t_ref,
    w_env_ref,
    w_env_t_ref,
    w_lat_ref,
    w_lat_t_ref,
    w_out_ref,
    out_ref,
    z1_ref,
    z2_ref,
    z3_ref,
    hidden_ref,
    joined_ref,
    grad_ref,
    dz_ref,
    vec_ref,
    env_ref,
    dvec_ref,
    dlat_ref,
):
    centre = ids_ref[0:1, :]
    neighbour = ids_ref[1:2, :]
    slot = neighbour >> 7
    atom = neighbour & 127
    step_x = (slot * 57) >> 9
    rest = slot - 9 * step_x
    step_y = (rest * 11) >> 5
    step_z = rest - 3 * step_y

    near, own = [], []
    for half in range(2):
        lanes = slice(half * ATOMS, (half + 1) * ATOMS)
        pick = jnp.broadcast_to(atom[:, lanes], (4, ATOMS))
        slot_half = jnp.broadcast_to(slot[:, lanes], (4, ATOMS))
        total = jnp.zeros((4, ATOMS), F32)
        for at_y, slab in enumerate((below_ref, level_ref, above_ref)):
            for at_x in range(3):
                for at_z in range(3):
                    rows = jnp.take_along_axis(slab[at_x * 3 + at_z], pick, axis=1)
                    number = 9 * at_x + 3 * at_y + at_z
                    total = jnp.where(slot_half == number, rows, total)
        near.append(total)
        pick = jnp.broadcast_to(centre[:, lanes], (4, ATOMS))
        own.append(jnp.take_along_axis(level_ref[4], pick, axis=1))
    near = jnp.concatenate(near, axis=1)
    own = jnp.concatenate(own, axis=1)
    delta = [
        near[axis : axis + 1, :]
        + (step - 1).astype(F32) * EXTENT[axis]
        - own[axis : axis + 1, :]
        for axis, step in enumerate((step_x, step_y, step_z))
    ]

    lane = lax.broadcasted_iota(jnp.int32, (1, PAIRS), 1)
    half_live = jnp.where(lane < ATOMS, counts_ref[0], counts_ref[1] + ATOMS)
    live = jnp.where(lane < half_live, 1.0, 0.0)
    radius = jnp.sqrt(delta[0] * delta[0] + delta[1] * delta[1] + delta[2] * delta[2] + SOFTEN)
    inverse = 1.0 / radius
    ratio = radius * (1.0 / CUTOFF)
    inside = jnp.where(ratio < 1.0, live, 0.0)
    square = ratio * ratio
    fifth = square * square * ratio
    sixth = fifth * ratio
    cut = inside * (1.0 + sixth * (-28.0 + 48.0 * ratio - 21.0 * square))
    slope = inside * (-168.0 / CUTOFF) * fifth * (1.0 - ratio) * (1.0 - ratio)

    row8 = lax.broadcasted_iota(jnp.int32, (8, PAIRS), 0)
    order = (row8 + 1).astype(F32)
    turns = order * ratio
    whole = jnp.floor(turns + 0.5)
    sign = 1.0 - 2.0 * (whole.astype(jnp.int32) & 1).astype(F32)
    angle = (turns - whole) * math.pi
    angle2 = angle * angle
    sine = jnp.zeros_like(angle)
    for power in (11, 9, 7, 5, 3, 1):
        sine = sine * angle2 + (-1.0) ** (power // 2) / math.factorial(power)
    sine = sine * angle * sign
    cosine = jnp.zeros_like(angle)
    for power in (12, 10, 8, 6, 4, 2, 0):
        cosine = cosine * angle2 + (-1.0) ** (power // 2) / math.factorial(power)
    cosine = cosine * sign
    front = math.sqrt(2.0 / CUTOFF)
    bessel = front * sine * inverse
    bessel_slope = (front * math.pi / CUTOFF) * order * cosine * inverse - bessel * inverse

    kind_at = jnp.where(row8 < 2, own[3:4, :], near[3:4, :])
    kind = jnp.where((row8 < 4) & (kind_at == (row8 & 1).astype(F32)), 1.0, 0.0)
    features = jnp.concatenate([bessel * cut, kind], axis=0).astype(BF16)

    z1_ref[...] = jnp.dot(w_in_ref[...], features, preferred_element_type=F32)
    for start in range(0, LAT, ROWS):
        rows = pl.ds(start, ROWS)
        value, gate = silu_parts(z1_ref[rows, :])
        hidden_ref[rows, :] = value.astype(BF16)
        z1_ref[rows, :] = gate
    z2_ref[...] = jnp.dot(w_hid_ref[...], hidden_ref[...], preferred_element_type=F32)
    for start in range(0, LAT, ROWS):
        rows = pl.ds(start, ROWS)
        value, unused = silu_parts(z2_ref[rows, :])
        joined_ref[rows, :] = (value * cut).astype(BF16)

    unit = [part * inverse for part in delta]
    along_x, along_y, along_z = unit
    shapes = [
        None,
        ROOT3 * along_x,
        ROOT3 * along_y,
        ROOT3 * along_z,
        ROOT15 * along_x * along_y,
        ROOT15 * along_y * along_z,
        0.5 * ROOT5 * (2.0 * along_z * along_z - along_x * along_x - along_y * along_y),
        ROOT15 * along_x * along_z,
        0.5 * ROOT15 * (along_x * along_x - along_y * along_y),
    ]
    same = same_ref[...]
    weight = jnp.dot(w_env_ref[...], joined_ref[0:LAT, :], preferred_element_type=F32)
    for m in range(9):
        vec_ref[m * CH : (m + 1) * CH, :] = weight if m == 0 else weight * shapes[m]
    env_ref[...] = split_dot(vec_ref[...], same)
    for degree in range(3):
        total = None
        for m in range(9):
            if DEGREE[m] == degree:
                rows = slice(m * CH, (m + 1) * CH)
                term = env_ref[rows, :] * vec_ref[rows, :]
                total = term if total is None else total + term
        joined_ref[LAT + degree * CH : LAT + (degree + 1) * CH, :] = total.astype(BF16)

    z3_ref[...] = jnp.dot(w_lat_ref[...], joined_ref[...], preferred_element_type=F32)
    energy = jnp.zeros((8, PAIRS), F32)
    cut_grad = jnp.zeros((8, PAIRS), F32)
    for start in range(0, LAT, ROWS):
        rows = pl.ds(start, ROWS)
        value, gate = silu_parts(z3_ref[rows, :])
        readout = w_out_ref[rows, :].astype(F32)
        readout = jnp.concatenate([readout, readout], axis=1)
        updated = (joined_ref[rows, :].astype(F32) + value * cut).astype(BF16).astype(F32)
        energy = energy + folded(readout * updated)
        cut_grad = cut_grad + folded(readout * value)
        dz_ref[rows, :] = (readout * cut * gate).astype(BF16)

    grad_ref[...] = jnp.dot(w_lat_t_ref[...], dz_ref[...], preferred_element_type=F32)
    for m in range(9):
        rows = slice(m * CH, (m + 1) * CH)
        start = LAT + DEGREE[m] * CH
        dvec_ref[rows, :] = grad_ref[start : start + CH, :] * vec_ref[rows, :]
    dvec_ref[...] = split_dot(dvec_ref[...], same)
    weight_grad = None
    shape_grad = [None]
    for m in range(9):
        rows = slice(m * CH, (m + 1) * CH)
        start = LAT + DEGREE[m] * CH
        dvec = grad_ref[start : start + CH, :] * env_ref[rows, :] + dvec_ref[rows, :]
        if m == 0:
            weight_grad = dvec
        else:
            weight_grad = weight_grad + dvec * shapes[m]
            shape_grad.append(column_sum(dvec * weight))
    dlat_ref[...] = jnp.dot(
        w_env_t_ref[...], weight_grad.astype(BF16), preferred_element_type=F32
    )
    for start in range(0, LAT, ROWS):
        rows = pl.ds(start, ROWS)
        readout = w_out_ref[rows, :].astype(F32)
        readout = jnp.concatenate([readout, readout], axis=1)
        value, gate = silu_parts(z2_ref[rows, :])
        dlat = readout + grad_ref[rows, :] + dlat_ref[rows, :]
        cut_grad = cut_grad + folded(dlat * value)
        dz_ref[rows, :] = (dlat * cut * gate).astype(BF16)
    dlat_ref[...] = jnp.dot(w_hid_t_ref[...], dz_ref[...], preferred_element_type=F32)
    for start in range(0, LAT, ROWS):
        rows = pl.ds(start, ROWS)
        dz_ref[rows, :] = (dlat_ref[rows, :] * z1_ref[rows, :]).astype(BF16)
    feature_grad = jnp.dot(w_in_t_ref[...], dz_ref[...], preferred_element_type=F32)[0:8, :]

    cut_grad = column_sum(cut_grad + feature_grad * bessel)
    radius_grad = cut_grad * slope + cut * column_sum(feature_grad * bessel_slope)
    g1, g2, g3, g4, g5, g6, g7, g8 = shape_grad[1:]
    unit_grad = [
        ROOT3 * g1 + ROOT15 * (along_y * g4 + along_z * g7 + along_x * g8) - ROOT5 * along_x * g6,
        ROOT3 * g2 + ROOT15 * (along_x * g4 + along_z * g5 - along_y * g8) - ROOT5 * along_y * g6,
        ROOT3 * g3 + ROOT15 * (along_y * g5 + along_x * g7) + 2.0 * ROOT5 * along_z * g6,
    ]
    radial = sum(g * u for g, u in zip(unit_grad, unit))
    radius_grad = radius_grad - radial * inverse
    push = [g * inverse + radius_grad * u for g, u in zip(unit_grad, unit)]

    row = lax.broadcasted_iota(jnp.int32, (32, PAIRS), 0)
    cell = (row * 11) >> 5
    axis = row - 3 * cell
    cell_y = (cell * 11) >> 5
    wanted = 3 * cell_y + (cell - 3 * cell_y)
    moved = jnp.where(axis == 0, push[0], jnp.where(axis == 1, push[1], push[2]))
    moved = jnp.where(row < ENERGY_ROW, moved, 0.0)
    atom_row = lax.broadcasted_iota(jnp.int32, (ATOMS, PAIRS), 0)
    hit_near = jnp.where(atom_row == atom, 1.0, 0.0).astype(BF16)
    hit_own = jnp.where(atom_row == centre, 1.0, 0.0).astype(BF16)
    spread = jnp.concatenate(
        [jnp.where(slot == wanted + 9 * at_x, -moved, 0.0) for at_x in range(3)], axis=0
    )
    spread = split_dot_nt(spread, hit_near)
    home = split_dot_nt(jnp.where(cell == 4, moved, 0.0), hit_own)
    energy = column_sum(energy)
    energy = energy[:, 0:ATOMS] + energy[:, ATOMS:PAIRS]
    is_energy = lax.broadcasted_iota(jnp.int32, (32, ATOMS), 0) == ENERGY_ROW
    blank = jnp.where(is_energy, energy, 0.0)
    for peer in range(RING):
        out_ref[peer] = blank
    place = place_ref[0]
    for at_x in range(3):
        block = spread[32 * at_x : 32 * (at_x + 1), :]
        if at_x == 1:
            block = block + home
        out_ref[(place + (at_x + RING - 1)) & (RING - 1)] = jnp.where(is_energy, energy, block)


def both_sides(block, axis):
    up = [(i, (i + 1) % RING) for i in range(RING)]
    down = [((i + 1) % RING, i) for i in range(RING)]
    return lax.ppermute(block, axis, up), lax.ppermute(block, axis, down)


def addressed(total, axis, count):
    place = lax.axis_index(axis)
    peer = lax.broadcasted_iota(jnp.int32, (RING, 1, 1), 0)
    rows = jnp.zeros((RING, count, ATOMS), F32)
    for at in range(3):
        here = peer == (place + (at + RING - 1)) % RING
        rows = jnp.where(here, total[None, at * count : (at + 1) * count, :], rows)
    energies = jnp.broadcast_to(total[None, 3 * count : 3 * count + 1, :], (RING, 1, ATOMS))
    return jnp.concatenate([rows, energies], axis=1)


def body(coords, species, pair_ids, live_counts, w_two_in, w_two_hid, w_env, w_latent, w_out):
    ids = pair_ids[0, 0, 0]
    counts = live_counts[0, 0, 0]
    frame = jnp.concatenate([coords[0, 0, 0], species[0, 0, 0].astype(F32)[None]], axis=0)
    low, high = both_sides(frame, "gz")
    column = jnp.stack([low, frame, high], axis=0)
    low, high = both_sides(column, "gx")
    plane = jnp.concatenate([low, column, high], axis=0)
    below, above = both_sides(plane, "gy")

    same = jnp.where(ids[0][:, None] == ids[0][None, :], ENV_NORM, 0.0).astype(BF16)
    w_in = jnp.pad(w_two_in, ((0, 0), (0, 4)))
    readout = jnp.broadcast_to(w_out.reshape(LAT, 1), (LAT, ATOMS))
    place = lax.axis_index("gx").astype(jnp.int32).reshape(1)
    vmem = pl.BlockSpec(memory_space=pltpu.VMEM)
    smem = pl.BlockSpec(memory_space=pltpu.SMEM)
    sent = pl.pallas_call(
        force_kernel,
        out_shape=jax.ShapeDtypeStruct((RING, 32, ATOMS), F32),
        in_specs=[smem, smem] + [vmem] * 14,
        out_specs=vmem,
        scratch_shapes=[
            pltpu.VMEM((LAT, PAIRS), F32),
            pltpu.VMEM((LAT, PAIRS), F32),
            pltpu.VMEM((LAT, PAIRS), F32),
            pltpu.VMEM((LAT, PAIRS), BF16),
            pltpu.VMEM((LAT + 3 * CH, PAIRS), BF16),
            pltpu.VMEM((LAT + 3 * CH, PAIRS), F32),
            pltpu.VMEM((LAT, PAIRS), BF16),
            pltpu.VMEM((9 * CH, PAIRS), F32),
            pltpu.VMEM((9 * CH, PAIRS), F32),
            pltpu.VMEM((9 * CH, PAIRS), F32),
            pltpu.VMEM((LAT, PAIRS), F32),
        ],
        compiler_params=pltpu.CompilerParams(vmem_limit_bytes=24 * 1024 * 1024),
        name="forces_of_pairs",
    )(
        place,
        counts,
        ids,
        below,
        plane,
        above,
        same,
        w_in,
        w_in.T,
        w_two_hid,
        w_two_hid.T,
        w_env,
        w_env.T,
        w_latent,
        w_latent.T,
        readout,
    )
    total = jnp.sum(lax.all_to_all(sent, "gx", 0, 0), axis=0)
    total = jnp.sum(lax.all_to_all(addressed(total, "gy", 9), "gy", 0, 0), axis=0)
    total = jnp.sum(lax.all_to_all(addressed(total, "gz", 3), "gz", 0, 0), axis=0)
    forces = total[0:3].reshape(1, 1, 1, 3, ATOMS)
    return forces, jnp.sum(total[3]) * (1.0 / (ATOMS * RING**3))


def solution(mesh):
    in_specs = (
        P("gx", "gy", "gz", None, None),
        P("gx", "gy", "gz", None),
        P("gx", "gy", "gz", None, None),
        P("gx", "gy", "gz", None),
        P(),
        P(),
        P(),
        P(),
        P(),
    )
    out_specs = (P("gx", "gy", "gz", None, None), P())
    return jax.shard_map(body, mesh=mesh, in_specs=in_specs, out_specs=out_specs, check_vma=False)
```

```python
import math

import jax
import jax.numpy as jnp
from jax import lax
from jax.experimental import pallas as pl
from jax.experimental.pallas import tpu as pltpu
from jax.sharding import PartitionSpec as P

F32 = jnp.float32
BF16 = jnp.bfloat16
CUTOFF = 6.0
SOFTEN = 0.01
ENV_NORM = 0.25
EXTENT = (16.0, 16.0, 4.0)
ROOT3 = math.sqrt(3.0)
ROOT5 = math.sqrt(5.0)
ROOT15 = math.sqrt(15.0)
DEGREE = (0, 1, 1, 1, 2, 2, 2, 2, 2)
RING = 8
LAT = 512
CH = 64
PAIRS = 256
ATOMS = 128
ROWS = 64


def column_sum(block):
    return jnp.sum(block, axis=0, keepdims=True)


def folded(block):
    return jnp.sum(block.reshape(block.shape[0] // 8, 8, block.shape[1]), axis=0)


def silu_parts(z):
    gate = 0.5 * jnp.tanh(0.5 * z) + 0.5
    value = z * gate
    return value, gate + value * (1.0 - gate)


def split_dot(block, square):
    high = block.astype(BF16)
    low = (block - high.astype(F32)).astype(BF16)
    return jnp.dot(high, square, preferred_element_type=F32) + jnp.dot(
        low, square, preferred_element_type=F32
    )


def split_dot_nt(block, other):
    dims = (((1,), (1,)), ((), ()))
    high = block.astype(BF16)
    low = (block - high.astype(F32)).astype(BF16)
    return lax.dot_general(high, other, dims, preferred_element_type=F32) + lax.dot_general(
        low, other, dims, preferred_element_type=F32
    )


def pack_kernel(coords_ref, species_ref, out_ref):
    block = jnp.concatenate([coords_ref[...], species_ref[...].astype(F32)], axis=0)
    out_ref[...] = jnp.broadcast_to(block[None], out_ref.shape)


def around():
    at_y, at_z = lax.axis_index("gy"), lax.axis_index("gz")
    return [
        ((at_y + (RING + step_y)) & (RING - 1)) * RING + ((at_z + (RING + step_z)) & (RING - 1))
        for step_y in (-1, 0, 1)
        for step_z in (-1, 0, 1)
    ]


def pick_kernel(received_ref, out_ref):
    for cell, number in enumerate(around()):
        out_ref[cell] = received_ref[number]


def address_kernel(received_ref, out_ref):
    total = jnp.sum(received_ref[...], axis=0)
    is_energy = lax.broadcasted_iota(jnp.int32, (4, ATOMS), 0) == 3
    blank = jnp.where(is_energy, total[4], 0.0)
    out_ref[...] = jnp.broadcast_to(blank[None], out_ref.shape)
    for cell, number in enumerate(around()):
        out_ref[number] = total[cell]


def finish_kernel(received_ref, forces_ref, energy_ref):
    total = jnp.sum(received_ref[...], axis=0)
    forces_ref[...] = total[0:3]
    energy_ref[0] = jnp.sum(total[3:4]) * (1.0 / (ATOMS * RING**3))


def force_kernel(
    counts_ref,
    ids_ref,
    even_ref,
    level_ref,
    odd_ref,
    same_ref,
    w_in_ref,
    w_in_t_ref,
    w_hid_ref,
    w_hid_t_ref,
    w_env_ref,
    w_env_t_ref,
    w_lat_ref,
    w_lat_t_ref,
    w_out_ref,
    out_ref,
    z1_ref,
    z2_ref,
    z3_ref,
    hidden_ref,
    joined_ref,
    grad_ref,
    dz_ref,
    vec_ref,
    env_ref,
    dvec_ref,
    dlat_ref,
):
    centre = ids_ref[0:1, :]
    neighbour = ids_ref[1:2, :]
    slot = neighbour >> 7
    atom = neighbour & 127
    step_x = (slot * 57) >> 9
    rest = slot - 9 * step_x
    step_y = (rest * 11) >> 5
    step_z = rest - 3 * step_y

    place = lax.axis_index("gx")
    parity = place & 1
    near, own = [], []
    for half in range(2):
        lanes = slice(half * ATOMS, (half + 1) * ATOMS)
        pick = jnp.broadcast_to(atom[:, lanes], (4, ATOMS))
        slot_half = jnp.broadcast_to(slot[:, lanes], (4, ATOMS))
        total = jnp.zeros((4, ATOMS), F32)
        for slab, base in ((even_ref, 18 * (1 - parity)), (level_ref, 9), (odd_ref, 18 * parity)):
            for cell in range(9):
                rows = jnp.take_along_axis(slab[cell], pick, axis=1)
                total = jnp.where(slot_half == base + cell, rows, total)
        near.append(total)
        pick = jnp.broadcast_to(centre[:, lanes], (4, ATOMS))
        own.append(jnp.take_along_axis(level_ref[4], pick, axis=1))
    near = jnp.concatenate(near, axis=1)
    own = jnp.concatenate(own, axis=1)
    delta = [
        near[axis : axis + 1, :]
        + (step - 1).astype(F32) * EXTENT[axis]
        - own[axis : axis + 1, :]
        for axis, step in enumerate((step_x, step_y, step_z))
    ]

    lane = lax.broadcasted_iota(jnp.int32, (1, PAIRS), 1)
    half_live = jnp.where(lane < ATOMS, counts_ref[0], counts_ref[1] + ATOMS)
    live = jnp.where(lane < half_live, 1.0, 0.0)
    radius = jnp.sqrt(delta[0] * delta[0] + delta[1] * delta[1] + delta[2] * delta[2] + SOFTEN)
    inverse = 1.0 / radius
    ratio = radius * (1.0 / CUTOFF)
    inside = jnp.where(ratio < 1.0, live, 0.0)
    square = ratio * ratio
    fifth = square * square * ratio
    sixth = fifth * ratio
    cut = inside * (1.0 + sixth * (-28.0 + 48.0 * ratio - 21.0 * square))
    slope = inside * (-168.0 / CUTOFF) * fifth * (1.0 - ratio) * (1.0 - ratio)

    row8 = lax.broadcasted_iota(jnp.int32, (8, PAIRS), 0)
    order = (row8 + 1).astype(F32)
    turns = order * ratio
    whole = jnp.floor(turns + 0.5)
    sign = 1.0 - 2.0 * (whole.astype(jnp.int32) & 1).astype(F32)
    angle = (turns - whole) * math.pi
    angle2 = angle * angle
    sine = jnp.zeros_like(angle)
    for power in (11, 9, 7, 5, 3, 1):
        sine = sine * angle2 + (-1.0) ** (power // 2) / math.factorial(power)
    sine = sine * angle * sign
    cosine = jnp.zeros_like(angle)
    for power in (12, 10, 8, 6, 4, 2, 0):
        cosine = cosine * angle2 + (-1.0) ** (power // 2) / math.factorial(power)
    cosine = cosine * sign
    front = math.sqrt(2.0 / CUTOFF)
    bessel = front * sine * inverse
    bessel_slope = (front * math.pi / CUTOFF) * order * cosine * inverse - bessel * inverse

    kind_at = jnp.where(row8 < 2, own[3:4, :], near[3:4, :])
    kind = jnp.where((row8 < 4) & (kind_at == (row8 & 1).astype(F32)), 1.0, 0.0)
    features = jnp.concatenate([bessel * cut, kind], axis=0).astype(BF16)

    z1_ref[...] = jnp.dot(w_in_ref[...], features, preferred_element_type=F32)
    for start in range(0, LAT, ROWS):
        rows = pl.ds(start, ROWS)
        value, gate = silu_parts(z1_ref[rows, :])
        hidden_ref[rows, :] = value.astype(BF16)
        z1_ref[rows, :] = gate
    z2_ref[...] = jnp.dot(w_hid_ref[...], hidden_ref[...], preferred_element_type=F32)
    for start in range(0, LAT, ROWS):
        rows = pl.ds(start, ROWS)
        value, unused = silu_parts(z2_ref[rows, :])
        joined_ref[rows, :] = (value * cut).astype(BF16)

    unit = [part * inverse for part in delta]
    along_x, along_y, along_z = unit
    shapes = [
        None,
        ROOT3 * along_x,
        ROOT3 * along_y,
        ROOT3 * along_z,
        ROOT15 * along_x * along_y,
        ROOT15 * along_y * along_z,
        0.5 * ROOT5 * (2.0 * along_z * along_z - along_x * along_x - along_y * along_y),
        ROOT15 * along_x * along_z,
        0.5 * ROOT15 * (along_x * along_x - along_y * along_y),
    ]
    same = same_ref[...]
    weight = jnp.dot(w_env_ref[...], joined_ref[0:LAT, :], preferred_element_type=F32)
    for m in range(9):
        vec_ref[m * CH : (m + 1) * CH, :] = weight if m == 0 else weight * shapes[m]
    env_ref[...] = split_dot(vec_ref[...], same)
    for degree in range(3):
        total = None
        for m in range(9):
            if DEGREE[m] == degree:
                rows = slice(m * CH, (m + 1) * CH)
                term = env_ref[rows, :] * vec_ref[rows, :]
                total = term if total is None else total + term
        joined_ref[LAT + degree * CH : LAT + (degree + 1) * CH, :] = total.astype(BF16)

    z3_ref[...] = jnp.dot(w_lat_ref[...], joined_ref[...], preferred_element_type=F32)
    energy = jnp.zeros((8, PAIRS), F32)
    cut_grad = jnp.zeros((8, PAIRS), F32)
    for start in range(0, LAT, ROWS):
        rows = pl.ds(start, ROWS)
        value, gate = silu_parts(z3_ref[rows, :])
        readout = w_out_ref[rows, :].astype(F32)
        readout = jnp.concatenate([readout, readout], axis=1)
        updated = (joined_ref[rows, :].astype(F32) + value * cut).astype(BF16).astype(F32)
        energy = energy + folded(readout * updated)
        cut_grad = cut_grad + folded(readout * value)
        dz_ref[rows, :] = (readout * cut * gate).astype(BF16)

    grad_ref[...] = jnp.dot(w_lat_t_ref[...], dz_ref[...], preferred_element_type=F32)
    for m in range(9):
        rows = slice(m * CH, (m + 1) * CH)
        start = LAT + DEGREE[m] * CH
        dvec_ref[rows, :] = grad_ref[start : start + CH, :] * vec_ref[rows, :]
    dvec_ref[...] = split_dot(dvec_ref[...], same)
    weight_grad = None
    shape_grad = [None]
    for m in range(9):
        rows = slice(m * CH, (m + 1) * CH)
        start = LAT + DEGREE[m] * CH
        dvec = grad_ref[start : start + CH, :] * env_ref[rows, :] + dvec_ref[rows, :]
        if m == 0:
            weight_grad = dvec
        else:
            weight_grad = weight_grad + dvec * shapes[m]
            shape_grad.append(column_sum(dvec * weight))
    dlat_ref[...] = jnp.dot(
        w_env_t_ref[...], weight_grad.astype(BF16), preferred_element_type=F32
    )
    for start in range(0, LAT, ROWS):
        rows = pl.ds(start, ROWS)
        readout = w_out_ref[rows, :].astype(F32)
        readout = jnp.concatenate([readout, readout], axis=1)
        value, gate = silu_parts(z2_ref[rows, :])
        dlat = readout + grad_ref[rows, :] + dlat_ref[rows, :]
        cut_grad = cut_grad + folded(dlat * value)
        dz_ref[rows, :] = (dlat * cut * gate).astype(BF16)
    dlat_ref[...] = jnp.dot(w_hid_t_ref[...], dz_ref[...], preferred_element_type=F32)
    for start in range(0, LAT, ROWS):
        rows = pl.ds(start, ROWS)
        dz_ref[rows, :] = (dlat_ref[rows, :] * z1_ref[rows, :]).astype(BF16)
    feature_grad = jnp.dot(w_in_t_ref[...], dz_ref[...], preferred_element_type=F32)[0:8, :]

    cut_grad = column_sum(cut_grad + feature_grad * bessel)
    radius_grad = cut_grad * slope + cut * column_sum(feature_grad * bessel_slope)
    g1, g2, g3, g4, g5, g6, g7, g8 = shape_grad[1:]
    unit_grad = [
        ROOT3 * g1 + ROOT15 * (along_y * g4 + along_z * g7 + along_x * g8) - ROOT5 * along_x * g6,
        ROOT3 * g2 + ROOT15 * (along_x * g4 + along_z * g5 - along_y * g8) - ROOT5 * along_y * g6,
        ROOT3 * g3 + ROOT15 * (along_y * g5 + along_x * g7) + 2.0 * ROOT5 * along_z * g6,
    ]
    radial = sum(g * u for g, u in zip(unit_grad, unit))
    radius_grad = radius_grad - radial * inverse
    push = [g * inverse + radius_grad * u for g, u in zip(unit_grad, unit)]

    row = lax.broadcasted_iota(jnp.int32, (112, PAIRS), 0)
    axis = row & 3
    moved = jnp.where(axis == 0, push[0], jnp.where(axis == 1, push[1], push[2]))
    moved = jnp.where(axis == 3, 0.0, moved)
    atom_row = lax.broadcasted_iota(jnp.int32, (ATOMS, PAIRS), 0)
    hit_near = jnp.where(atom_row == atom, 1.0, 0.0).astype(BF16)
    hit_own = jnp.where(atom_row == centre, 1.0, 0.0).astype(BF16)
    spread = split_dot_nt(jnp.where((row >> 2) == slot, -moved, 0.0), hit_near)
    home = split_dot_nt(moved[0:8], hit_own)[0:4]
    spread = spread.reshape(28, 4, ATOMS)
    energy = column_sum(energy)
    energy = energy[:, 0:ATOMS] + energy[:, ATOMS:PAIRS]
    is_energy = lax.broadcasted_iota(jnp.int32, (4, ATOMS), 0) == 3
    blank = jnp.where(is_energy, energy, 0.0)
    out_ref[...] = jnp.broadcast_to(blank[None, None], out_ref.shape)
    for at_x in range(3):
        number = (place + (at_x + RING - 1)) & (RING - 1)
        for cell in range(9):
            block = spread[9 * at_x + cell]
            if 9 * at_x + cell == 13:
                block = block + home
            out_ref[number, cell] = block + blank


EVEN = [(i, i ^ 1) for i in range(RING)]
ODD = [(i, (((i + 1) ^ 1) - 1) % RING) for i in range(RING)]


def body(coords, species, pair_ids, live_counts, w_two_in, w_two_hid, w_env, w_latent, w_out):
    ids = pair_ids[0, 0, 0]
    counts = live_counts[0, 0, 0]
    vmem = pl.BlockSpec(memory_space=pltpu.VMEM)
    smem = pl.BlockSpec(memory_space=pltpu.SMEM)
    packed = pl.pallas_call(
        pack_kernel,
        out_shape=jax.ShapeDtypeStruct((RING * RING, 4, ATOMS), F32),
        in_specs=[vmem] * 2,
        out_specs=vmem,
        name="pack_frame",
    )(coords[0, 0, 0], species.reshape(1, ATOMS))
    plane = pl.pallas_call(
        pick_kernel,
        out_shape=jax.ShapeDtypeStruct((9, 4, ATOMS), F32),
        in_specs=[vmem],
        out_specs=vmem,
        name="pick_plane",
    )(lax.all_to_all(packed, ("gy", "gz"), 0, 0))
    even = lax.ppermute(plane, "gx", EVEN)
    odd = lax.ppermute(plane, "gx", ODD)

    same = jnp.where(ids[0][:, None] == ids[0][None, :], ENV_NORM, 0.0).astype(BF16)
    w_in = jnp.pad(w_two_in, ((0, 0), (0, 4)))
    readout = jnp.broadcast_to(w_out.reshape(LAT, 1), (LAT, ATOMS))
    sent = pl.pallas_call(
        force_kernel,
        out_shape=jax.ShapeDtypeStruct((RING, 9, 4, ATOMS), F32),
        in_specs=[smem] + [vmem] * 14,
        out_specs=vmem,
        scratch_shapes=[
            pltpu.VMEM((LAT, PAIRS), F32),
            pltpu.VMEM((LAT, PAIRS), F32),
            pltpu.VMEM((LAT, PAIRS), F32),
            pltpu.VMEM((LAT, PAIRS), BF16),
            pltpu.VMEM((LAT + 3 * CH, PAIRS), BF16),
            pltpu.VMEM((LAT + 3 * CH, PAIRS), F32),
            pltpu.VMEM((LAT, PAIRS), BF16),
            pltpu.VMEM((9 * CH, PAIRS), F32),
            pltpu.VMEM((9 * CH, PAIRS), F32),
            pltpu.VMEM((9 * CH, PAIRS), F32),
            pltpu.VMEM((LAT, PAIRS), F32),
        ],
        compiler_params=pltpu.CompilerParams(vmem_limit_bytes=24 * 1024 * 1024),
        name="forces_of_pairs",
    )(
        counts,
        ids,
        even,
        plane,
        odd,
        same,
        w_in,
        w_in.T,
        w_two_hid,
        w_two_hid.T,
        w_env,
        w_env.T,
        w_latent,
        w_latent.T,
        readout,
    )
    addressed = pl.pallas_call(
        address_kernel,
        out_shape=jax.ShapeDtypeStruct((RING * RING, 4, ATOMS), F32),
        in_specs=[vmem],
        out_specs=vmem,
        name="address_plane",
    )(lax.all_to_all(sent, "gx", 0, 0))
    forces, energy = pl.pallas_call(
        finish_kernel,
        out_shape=(jax.ShapeDtypeStruct((3, ATOMS), F32), jax.ShapeDtypeStruct((1,), F32)),
        in_specs=[vmem],
        out_specs=(vmem, smem),
        name="finish",
    )(lax.all_to_all(addressed, ("gy", "gz"), 0, 0))
    return forces.reshape(1, 1, 1, 3, ATOMS), energy.reshape(())


def solution(mesh):
    in_specs = (
        P("gx", "gy", "gz", None, None),
        P("gx", "gy", "gz", None),
        P("gx", "gy", "gz", None, None),
        P("gx", "gy", "gz", None),
        P(),
        P(),
        P(),
        P(),
        P(),
    )
    out_specs = (P("gx", "gy", "gz", None, None), P())
    return jax.shard_map(body, mesh=mesh, in_specs=in_specs, out_specs=out_specs, check_vma=False)
```

```python
import math

import jax
import jax.numpy as jnp
from jax import lax
from jax.experimental import pallas as pl
from jax.experimental.pallas import tpu as pltpu
from jax.sharding import PartitionSpec as P

F32 = jnp.float32
BF16 = jnp.bfloat16
CUTOFF = 6.0
SOFTEN = 0.01
ENV_NORM = 0.25
EXTENT = (16.0, 16.0, 4.0)
ROOT3 = math.sqrt(3.0)
ROOT5 = math.sqrt(5.0)
ROOT15 = math.sqrt(15.0)
DEGREE = (0, 1, 1, 1, 2, 2, 2, 2, 2)
RING = 8
LAT = 512
CH = 64
PAIRS = 256
ATOMS = 128
ROWS = 64


def column_sum(block):
    return jnp.sum(block, axis=0, keepdims=True)


def folded(block):
    return jnp.sum(block.reshape(block.shape[0] // 8, 8, block.shape[1]), axis=0)


def silu_parts(z):
    gate = 0.5 * jnp.tanh(0.5 * z) + 0.5
    value = z * gate
    return value, gate + value * (1.0 - gate)


def split_dot(block, square):
    high = block.astype(BF16)
    low = (block - high.astype(F32)).astype(BF16)
    return jnp.dot(high, square, preferred_element_type=F32) + jnp.dot(
        low, square, preferred_element_type=F32
    )


def split_dot_nt(block, other):
    dims = (((1,), (1,)), ((), ()))
    high = block.astype(BF16)
    low = (block - high.astype(F32)).astype(BF16)
    return lax.dot_general(high, other, dims, preferred_element_type=F32) + lax.dot_general(
        low, other, dims, preferred_element_type=F32
    )


def pack_kernel(coords_ref, species_ref, out_ref):
    rows = [coords_ref[axis] for axis in range(3)] + [species_ref[...].astype(F32)]
    block = jnp.concatenate(rows, axis=0)
    out_ref[...] = jnp.broadcast_to(block[None], out_ref.shape)


def around():
    at_y, at_z = lax.axis_index("gy"), lax.axis_index("gz")
    return [
        ((at_y + (RING + step_y)) & (RING - 1)) * RING + ((at_z + (RING + step_z)) & (RING - 1))
        for step_y in (-1, 0, 1)
        for step_z in (-1, 0, 1)
    ]


def pick_kernel(received_ref, out_ref):
    for cell, number in enumerate(around()):
        out_ref[cell] = received_ref[number]


def address_kernel(received_ref, out_ref):
    total = jnp.sum(received_ref[...], axis=0)
    is_energy = lax.broadcasted_iota(jnp.int32, (4, ATOMS), 0) == 3
    blank = jnp.where(is_energy, total[4], 0.0)
    out_ref[...] = jnp.broadcast_to(blank[None], out_ref.shape)
    for cell, number in enumerate(around()):
        out_ref[number] = total[cell]


def finish_kernel(received_ref, forces_ref, energy_ref):
    total = jnp.sum(received_ref[...], axis=0)
    for axis in range(3):
        forces_ref[axis] = total[axis : axis + 1]
    energy_ref[0] = jnp.sum(total[3:4]) * (1.0 / (ATOMS * RING**3))


def force_kernel(
    counts_ref,
    ids_ref,
    even_ref,
    level_ref,
    odd_ref,
    same_ref,
    w_in_ref,
    w_in_t_ref,
    w_hid_ref,
    w_hid_t_ref,
    w_env_ref,
    w_env_t_ref,
    w_lat_ref,
    w_lat_t_ref,
    w_out_ref,
    out_ref,
    z1_ref,
    z2_ref,
    z3_ref,
    hidden_ref,
    joined_ref,
    grad_ref,
    dz_ref,
    vec_ref,
    env_ref,
    dvec_ref,
    dlat_ref,
):
    centre = ids_ref[0:1, :]
    neighbour = ids_ref[1:2, :]
    slot = neighbour >> 7
    atom = neighbour & 127
    step_x = (slot * 57) >> 9
    rest = slot - 9 * step_x
    step_y = (rest * 11) >> 5
    step_z = rest - 3 * step_y

    place = lax.axis_index("gx")
    parity = place & 1
    near, own = [], []
    for half in range(2):
        lanes = slice(half * ATOMS, (half + 1) * ATOMS)
        pick = jnp.broadcast_to(atom[:, lanes], (4, ATOMS))
        slot_half = jnp.broadcast_to(slot[:, lanes], (4, ATOMS))
        total = jnp.zeros((4, ATOMS), F32)
        for slab, base in ((even_ref, 18 * (1 - parity)), (level_ref, 9), (odd_ref, 18 * parity)):
            for cell in range(9):
                rows = jnp.take_along_axis(slab[cell], pick, axis=1)
                total = jnp.where(slot_half == base + cell, rows, total)
        near.append(total)
        pick = jnp.broadcast_to(centre[:, lanes], (4, ATOMS))
        own.append(jnp.take_along_axis(level_ref[4], pick, axis=1))
    near = jnp.concatenate(near, axis=1)
    own = jnp.concatenate(own, axis=1)
    delta = [
        near[axis : axis + 1, :]
        + (step - 1).astype(F32) * EXTENT[axis]
        - own[axis : axis + 1, :]
        for axis, step in enumerate((step_x, step_y, step_z))
    ]

    lane = lax.broadcasted_iota(jnp.int32, (1, PAIRS), 1)
    half_live = jnp.where(lane < ATOMS, counts_ref[0], counts_ref[1] + ATOMS)
    live = jnp.where(lane < half_live, 1.0, 0.0)
    radius = jnp.sqrt(delta[0] * delta[0] + delta[1] * delta[1] + delta[2] * delta[2] + SOFTEN)
    inverse = 1.0 / radius
    ratio = radius * (1.0 / CUTOFF)
    inside = jnp.where(ratio < 1.0, live, 0.0)
    square = ratio * ratio
    fifth = square * square * ratio
    sixth = fifth * ratio
    cut = inside * (1.0 + sixth * (-28.0 + 48.0 * ratio - 21.0 * square))
    slope = inside * (-168.0 / CUTOFF) * fifth * (1.0 - ratio) * (1.0 - ratio)

    row8 = lax.broadcasted_iota(jnp.int32, (8, PAIRS), 0)
    order = (row8 + 1).astype(F32)
    turns = order * ratio
    whole = jnp.floor(turns + 0.5)
    sign = 1.0 - 2.0 * (whole.astype(jnp.int32) & 1).astype(F32)
    angle = (turns - whole) * math.pi
    angle2 = angle * angle
    sine = jnp.zeros_like(angle)
    for power in (11, 9, 7, 5, 3, 1):
        sine = sine * angle2 + (-1.0) ** (power // 2) / math.factorial(power)
    sine = sine * angle * sign
    cosine = jnp.zeros_like(angle)
    for power in (12, 10, 8, 6, 4, 2, 0):
        cosine = cosine * angle2 + (-1.0) ** (power // 2) / math.factorial(power)
    cosine = cosine * sign
    front = math.sqrt(2.0 / CUTOFF)
    bessel = front * sine * inverse
    bessel_slope = (front * math.pi / CUTOFF) * order * cosine * inverse - bessel * inverse

    kind_at = jnp.where(row8 < 2, own[3:4, :], near[3:4, :])
    kind = jnp.where((row8 < 4) & (kind_at == (row8 & 1).astype(F32)), 1.0, 0.0)
    features = jnp.concatenate([bessel * cut, kind], axis=0).astype(BF16)

    z1_ref[...] = jnp.dot(w_in_ref[...], features, preferred_element_type=F32)
    for start in range(0, LAT, ROWS):
        rows = pl.ds(start, ROWS)
        value, gate = silu_parts(z1_ref[rows, :])
        hidden_ref[rows, :] = value.astype(BF16)
        z1_ref[rows, :] = gate
    z2_ref[...] = jnp.dot(w_hid_ref[...], hidden_ref[...], preferred_element_type=F32)
    for start in range(0, LAT, ROWS):
        rows = pl.ds(start, ROWS)
        value, unused = silu_parts(z2_ref[rows, :])
        joined_ref[rows, :] = (value * cut).astype(BF16)

    unit = [part * inverse for part in delta]
    along_x, along_y, along_z = unit
    shapes = [
        None,
        ROOT3 * along_x,
        ROOT3 * along_y,
        ROOT3 * along_z,
        ROOT15 * along_x * along_y,
        ROOT15 * along_y * along_z,
        0.5 * ROOT5 * (2.0 * along_z * along_z - along_x * along_x - along_y * along_y),
        ROOT15 * along_x * along_z,
        0.5 * ROOT15 * (along_x * along_x - along_y * along_y),
    ]
    same = same_ref[...]
    weight = jnp.dot(w_env_ref[...], joined_ref[0:LAT, :], preferred_element_type=F32)
    for m in range(9):
        vec_ref[m * CH : (m + 1) * CH, :] = weight if m == 0 else weight * shapes[m]
    env_ref[...] = split_dot(vec_ref[...], same)
    for degree in range(3):
        total = None
        for m in range(9):
            if DEGREE[m] == degree:
                rows = slice(m * CH, (m + 1) * CH)
                term = env_ref[rows, :] * vec_ref[rows, :]
                total = term if total is None else total + term
        joined_ref[LAT + degree * CH : LAT + (degree + 1) * CH, :] = total.astype(BF16)

    z3_ref[...] = jnp.dot(w_lat_ref[...], joined_ref[...], preferred_element_type=F32)
    energy = jnp.zeros((8, PAIRS), F32)
    cut_grad = jnp.zeros((8, PAIRS), F32)
    for start in range(0, LAT, ROWS):
        rows = pl.ds(start, ROWS)
        value, gate = silu_parts(z3_ref[rows, :])
        readout = w_out_ref[rows, :].astype(F32)
        readout = jnp.concatenate([readout, readout], axis=1)
        updated = (joined_ref[rows, :].astype(F32) + value * cut).astype(BF16).astype(F32)
        energy = energy + folded(readout * updated)
        cut_grad = cut_grad + folded(readout * value)
        dz_ref[rows, :] = (readout * cut * gate).astype(BF16)

    grad_ref[...] = jnp.dot(w_lat_t_ref[...], dz_ref[...], preferred_element_type=F32)
    for m in range(9):
        rows = slice(m * CH, (m + 1) * CH)
        start = LAT + DEGREE[m] * CH
        dvec_ref[rows, :] = grad_ref[start : start + CH, :] * vec_ref[rows, :]
    dvec_ref[...] = split_dot(dvec_ref[...], same)
    weight_grad = None
    shape_grad = [None]
    for m in range(9):
        rows = slice(m * CH, (m + 1) * CH)
        start = LAT + DEGREE[m] * CH
        dvec = grad_ref[start : start + CH, :] * env_ref[rows, :] + dvec_ref[rows, :]
        if m == 0:
            weight_grad = dvec
        else:
            weight_grad = weight_grad + dvec * shapes[m]
            shape_grad.append(column_sum(dvec * weight))
    dlat_ref[...] = jnp.dot(
        w_env_t_ref[...], weight_grad.astype(BF16), preferred_element_type=F32
    )
    for start in range(0, LAT, ROWS):
        rows = pl.ds(start, ROWS)
        readout = w_out_ref[rows, :].astype(F32)
        readout = jnp.concatenate([readout, readout], axis=1)
        value, gate = silu_parts(z2_ref[rows, :])
        dlat = readout + grad_ref[rows, :] + dlat_ref[rows, :]
        cut_grad = cut_grad + folded(dlat * value)
        dz_ref[rows, :] = (dlat * cut * gate).astype(BF16)
    dlat_ref[...] = jnp.dot(w_hid_t_ref[...], dz_ref[...], preferred_element_type=F32)
    for start in range(0, LAT, ROWS):
        rows = pl.ds(start, ROWS)
        dz_ref[rows, :] = (dlat_ref[rows, :] * z1_ref[rows, :]).astype(BF16)
    feature_grad = jnp.dot(w_in_t_ref[...], dz_ref[...], preferred_element_type=F32)[0:8, :]

    cut_grad = column_sum(cut_grad + feature_grad * bessel)
    radius_grad = cut_grad * slope + cut * column_sum(feature_grad * bessel_slope)
    g1, g2, g3, g4, g5, g6, g7, g8 = shape_grad[1:]
    unit_grad = [
        ROOT3 * g1 + ROOT15 * (along_y * g4 + along_z * g7 + along_x * g8) - ROOT5 * along_x * g6,
        ROOT3 * g2 + ROOT15 * (along_x * g4 + along_z * g5 - along_y * g8) - ROOT5 * along_y * g6,
        ROOT3 * g3 + ROOT15 * (along_y * g5 + along_x * g7) + 2.0 * ROOT5 * along_z * g6,
    ]
    radial = sum(g * u for g, u in zip(unit_grad, unit))
    radius_grad = radius_grad - radial * inverse
    push = [g * inverse + radius_grad * u for g, u in zip(unit_grad, unit)]

    row = lax.broadcasted_iota(jnp.int32, (112, PAIRS), 0)
    axis = row & 3
    moved = jnp.where(axis == 0, push[0], jnp.where(axis == 1, push[1], push[2]))
    moved = jnp.where(axis == 3, 0.0, moved)
    atom_row = lax.broadcasted_iota(jnp.int32, (ATOMS, PAIRS), 0)
    hit_near = jnp.where(atom_row == atom, 1.0, 0.0).astype(BF16)
    hit_own = jnp.where(atom_row == centre, 1.0, 0.0).astype(BF16)
    spread = split_dot_nt(jnp.where((row >> 2) == slot, -moved, 0.0), hit_near)
    home = split_dot_nt(moved[0:8], hit_own)[0:4]
    spread = spread.reshape(28, 4, ATOMS)
    energy = column_sum(energy)
    energy = energy[:, 0:ATOMS] + energy[:, ATOMS:PAIRS]
    is_energy = lax.broadcasted_iota(jnp.int32, (4, ATOMS), 0) == 3
    blank = jnp.where(is_energy, energy, 0.0)
    out_ref[...] = jnp.broadcast_to(blank[None, None], out_ref.shape)
    for at_x in range(3):
        number = (place + (at_x + RING - 1)) & (RING - 1)
        for cell in range(9):
            block = spread[9 * at_x + cell]
            if 9 * at_x + cell == 13:
                block = block + home
            out_ref[number, cell] = block + blank


SMALL = pltpu.CompilerParams(vmem_limit_bytes=2 * 1024 * 1024)
EVEN = [(i, i ^ 1) for i in range(RING)]
ODD = [(i, (((i + 1) ^ 1) - 1) % RING) for i in range(RING)]


def body(coords, species, pair_ids, live_counts, w_two_in, w_two_hid, w_env, w_latent, w_out):
    ids = pair_ids[0, 0, 0]
    counts = live_counts[0, 0, 0]
    vmem = pl.BlockSpec(memory_space=pltpu.VMEM)
    smem = pl.BlockSpec(memory_space=pltpu.SMEM)
    packed = pl.pallas_call(
        pack_kernel,
        out_shape=jax.ShapeDtypeStruct((RING * RING, 4, ATOMS), F32),
        in_specs=[vmem] * 2,
        out_specs=vmem,
        compiler_params=SMALL,
        name="pack_frame",
    )(coords.reshape(3, 1, ATOMS), species.reshape(1, ATOMS))
    plane = pl.pallas_call(
        pick_kernel,
        out_shape=jax.ShapeDtypeStruct((9, 4, ATOMS), F32),
        in_specs=[vmem],
        out_specs=vmem,
        compiler_params=SMALL,
        name="pick_plane",
    )(lax.all_to_all(packed, ("gy", "gz"), 0, 0))
    even = lax.ppermute(plane, "gx", EVEN)
    odd = lax.ppermute(plane, "gx", ODD)

    same = jnp.where(ids[0][:, None] == ids[0][None, :], ENV_NORM, 0.0).astype(BF16)
    w_in = jnp.pad(w_two_in, ((0, 0), (0, 4)))
    readout = jnp.broadcast_to(w_out.reshape(LAT, 1), (LAT, ATOMS))
    sent = pl.pallas_call(
        force_kernel,
        out_shape=jax.ShapeDtypeStruct((RING, 9, 4, ATOMS), F32),
        in_specs=[smem] + [vmem] * 14,
        out_specs=vmem,
        scratch_shapes=[
            pltpu.VMEM((LAT, PAIRS), F32),
            pltpu.VMEM((LAT, PAIRS), F32),
            pltpu.VMEM((LAT, PAIRS), F32),
            pltpu.VMEM((LAT, PAIRS), BF16),
            pltpu.VMEM((LAT + 3 * CH, PAIRS), BF16),
            pltpu.VMEM((LAT + 3 * CH, PAIRS), F32),
            pltpu.VMEM((LAT, PAIRS), BF16),
            pltpu.VMEM((9 * CH, PAIRS), F32),
            pltpu.VMEM((9 * CH, PAIRS), F32),
            pltpu.VMEM((9 * CH, PAIRS), F32),
            pltpu.VMEM((LAT, PAIRS), F32),
        ],
        compiler_params=pltpu.CompilerParams(vmem_limit_bytes=24 * 1024 * 1024),
        name="forces_of_pairs",
    )(
        counts,
        ids,
        even,
        plane,
        odd,
        same,
        w_in,
        w_in.T,
        w_two_hid,
        w_two_hid.T,
        w_env,
        w_env.T,
        w_latent,
        w_latent.T,
        readout,
    )
    addressed = pl.pallas_call(
        address_kernel,
        out_shape=jax.ShapeDtypeStruct((RING * RING, 4, ATOMS), F32),
        in_specs=[vmem],
        out_specs=vmem,
        compiler_params=SMALL,
        name="address_plane",
    )(lax.all_to_all(sent, "gx", 0, 0))
    forces, energy = pl.pallas_call(
        finish_kernel,
        out_shape=(jax.ShapeDtypeStruct((3, 1, ATOMS), F32), jax.ShapeDtypeStruct((1,), F32)),
        in_specs=[vmem],
        out_specs=(vmem, smem),
        compiler_params=SMALL,
        name="finish",
    )(lax.all_to_all(addressed, ("gy", "gz"), 0, 0))
    return forces.reshape(1, 1, 1, 3, ATOMS), energy.reshape(())


def solution(mesh):
    in_specs = (
        P("gx", "gy", "gz", None, None),
        P("gx", "gy", "gz", None),
        P("gx", "gy", "gz", None, None),
        P("gx", "gy", "gz", None),
        P(),
        P(),
        P(),
        P(),
        P(),
    )
    out_specs = (P("gx", "gy", "gz", None, None), P())
    return jax.shard_map(body, mesh=mesh, in_specs=in_specs, out_specs=out_specs, check_vma=False)
```

```python
import math

import jax
import jax.numpy as jnp
from jax import lax
from jax.experimental import pallas as pl
from jax.experimental.pallas import tpu as pltpu
from jax.sharding import PartitionSpec as P

F32 = jnp.float32
BF16 = jnp.bfloat16
CUTOFF = 6.0
SOFTEN = 0.01
ENV_NORM = 0.25
EXTENT = (16.0, 16.0, 4.0)
ROOT3 = math.sqrt(3.0)
ROOT5 = math.sqrt(5.0)
ROOT15 = math.sqrt(15.0)
DEGREE = (0, 1, 1, 1, 2, 2, 2, 2, 2)
RING = 8
LAT = 512
CH = 64
PAIRS = 256
ATOMS = 128
ROWS = 64


def column_sum(block):
    return jnp.sum(block, axis=0, keepdims=True)


def folded(block):
    return jnp.sum(block.reshape(block.shape[0] // 8, 8, block.shape[1]), axis=0)


def silu_parts(z):
    gate = 0.5 * jnp.tanh(0.5 * z) + 0.5
    value = z * gate
    return value, gate + value * (1.0 - gate)


def dot_tn(left, right):
    return lax.dot_general(left, right, (((0,), (0,)), ((), ())), preferred_element_type=F32)


def split_dot_nt(block, other):
    dims = (((1,), (1,)), ((), ()))
    high = block.astype(BF16)
    low = (block - high.astype(F32)).astype(BF16)
    return lax.dot_general(high, other, dims, preferred_element_type=F32) + lax.dot_general(
        low, other, dims, preferred_element_type=F32
    )


def pack_kernel(coords_ref, species_ref, out_ref):
    rows = [coords_ref[axis] for axis in range(3)] + [species_ref[...].astype(F32)]
    block = jnp.concatenate(rows, axis=0)
    out_ref[...] = jnp.broadcast_to(block[None], out_ref.shape)


def around():
    at_y, at_z = lax.axis_index("gy"), lax.axis_index("gz")
    return [
        ((at_y + (RING + step_y)) & (RING - 1)) * RING + ((at_z + (RING + step_z)) & (RING - 1))
        for step_y in (-1, 0, 1)
        for step_z in (-1, 0, 1)
    ]


def pick_kernel(received_ref, out_ref):
    for cell, number in enumerate(around()):
        out_ref[cell] = received_ref[number]


def address_kernel(received_ref, out_ref):
    total = jnp.sum(received_ref[...], axis=0)
    is_energy = lax.broadcasted_iota(jnp.int32, (4, ATOMS), 0) == 3
    blank = jnp.where(is_energy, total[4], 0.0)
    out_ref[...] = jnp.broadcast_to(blank[None], out_ref.shape)
    for cell, number in enumerate(around()):
        out_ref[number] = total[cell]


def finish_kernel(received_ref, forces_ref, energy_ref):
    total = jnp.sum(received_ref[...], axis=0)
    for axis in range(3):
        forces_ref[axis] = total[axis : axis + 1]
    energy_ref[0] = jnp.sum(total[3:4]) * (1.0 / (ATOMS * RING**3))


def prepare_kernel(counts_ref, ids_ref, w_out_ref, pairs_ref, hits_ref, same_ref, readout_ref):
    centre = ids_ref[0:1, :]
    neighbour = ids_ref[1:2, :]
    lane = lax.broadcasted_iota(jnp.int32, (1, PAIRS), 1)
    live = lane < jnp.where(lane < ATOMS, counts_ref[0], counts_ref[1] + ATOMS)
    rows = [centre, neighbour >> 7, neighbour & 127, live.astype(jnp.int32)]
    pairs_ref[...] = jnp.concatenate(rows + rows, axis=0)
    atom_row = lax.broadcasted_iota(jnp.int32, (ATOMS, PAIRS), 0)
    hits_ref[0] = jnp.where(atom_row == rows[2], 1.0, 0.0).astype(BF16)
    hits_ref[1] = jnp.where(atom_row == centre, 1.0, 0.0).astype(BF16)
    across = jnp.broadcast_to(centre.astype(F32), (PAIRS, PAIRS))
    same_ref[...] = jnp.where(across == across.T, ENV_NORM, 0.0).astype(BF16)
    readout_ref[...] = jnp.broadcast_to(w_out_ref[...].astype(F32), (ATOMS, LAT)).T.astype(BF16)


def force_kernel(
    pairs_ref,
    hits_ref,
    even_ref,
    level_ref,
    odd_ref,
    same_ref,
    w_in_ref,
    w_in_t_ref,
    w_hid_ref,
    w_hid_t_ref,
    w_env_ref,
    w_env_t_ref,
    w_lat_ref,
    w_lat_t_ref,
    w_out_ref,
    out_ref,
    z1_ref,
    z2_ref,
    z3_ref,
    hidden_ref,
    joined_ref,
    grad_ref,
    dz_ref,
    dlat_ref,
):
    centre = pairs_ref[0:1, :]
    slot = pairs_ref[1:2, :]
    atom = pairs_ref[2:3, :]
    live = pairs_ref[3:4, :].astype(F32)
    step_x = (slot * 57) >> 9
    rest = slot - 9 * step_x
    step_y = (rest * 11) >> 5
    step_z = rest - 3 * step_y

    place = lax.axis_index("gx")
    parity = place & 1
    near, own = [], []
    for half in range(2):
        lanes = slice(half * ATOMS, (half + 1) * ATOMS)
        pick = jnp.broadcast_to(atom[:, lanes], (4, ATOMS))
        slot_half = jnp.broadcast_to(slot[:, lanes], (4, ATOMS))
        total = jnp.zeros((4, ATOMS), F32)
        for slab, base in ((even_ref, 18 * (1 - parity)), (level_ref, 9), (odd_ref, 18 * parity)):
            for cell in range(9):
                rows = jnp.take_along_axis(slab[cell], pick, axis=1, mode="promise_in_bounds")
                total = jnp.where(slot_half == base + cell, rows, total)
        near.append(total)
        pick = jnp.broadcast_to(centre[:, lanes], (4, ATOMS))
        own.append(jnp.take_along_axis(level_ref[4], pick, axis=1, mode="promise_in_bounds"))
    near = jnp.concatenate(near, axis=1)
    own = jnp.concatenate(own, axis=1)
    delta = [
        near[axis : axis + 1, :]
        + (step - 1).astype(F32) * EXTENT[axis]
        - own[axis : axis + 1, :]
        for axis, step in enumerate((step_x, step_y, step_z))
    ]

    radius = jnp.sqrt(delta[0] * delta[0] + delta[1] * delta[1] + delta[2] * delta[2] + SOFTEN)
    inverse = 1.0 / radius
    ratio = radius * (1.0 / CUTOFF)
    inside = jnp.where(ratio < 1.0, live, 0.0)
    square = ratio * ratio
    fifth = square * square * ratio
    sixth = fifth * ratio
    cut = inside * (1.0 + sixth * (-28.0 + 48.0 * ratio - 21.0 * square))
    slope = inside * (-168.0 / CUTOFF) * fifth * (1.0 - ratio) * (1.0 - ratio)

    row8 = lax.broadcasted_iota(jnp.int32, (8, PAIRS), 0)
    order = (row8 + 1).astype(F32)
    turns = order * ratio
    whole = jnp.floor(turns + 0.5)
    sign = 1.0 - 2.0 * (whole.astype(jnp.int32) & 1).astype(F32)
    angle = (turns - whole) * math.pi
    angle2 = angle * angle
    sine = jnp.zeros_like(angle)
    for power in (11, 9, 7, 5, 3, 1):
        sine = sine * angle2 + (-1.0) ** (power // 2) / math.factorial(power)
    sine = sine * angle * sign
    cosine = jnp.zeros_like(angle)
    for power in (12, 10, 8, 6, 4, 2, 0):
        cosine = cosine * angle2 + (-1.0) ** (power // 2) / math.factorial(power)
    cosine = cosine * sign
    front = math.sqrt(2.0 / CUTOFF)
    bessel = front * sine * inverse
    bessel_slope = (front * math.pi / CUTOFF) * order * cosine * inverse - bessel * inverse

    kind_at = jnp.where(row8 < 2, own[3:4, :], near[3:4, :])
    kind = jnp.where((row8 < 4) & (kind_at == (row8 & 1).astype(F32)), 1.0, 0.0)
    features = jnp.concatenate([bessel * cut, kind], axis=0).astype(BF16)

    z1_ref[...] = jnp.dot(w_in_ref[...], features, preferred_element_type=F32)
    for start in range(0, LAT, ROWS):
        rows = pl.ds(start, ROWS)
        value, gate = silu_parts(z1_ref[rows, :])
        hidden_ref[rows, :] = value.astype(BF16)
        z1_ref[rows, :] = gate
    z2_ref[...] = jnp.dot(w_hid_ref[...], hidden_ref[...], preferred_element_type=F32)
    for start in range(0, LAT, ROWS):
        rows = pl.ds(start, ROWS)
        value, unused = silu_parts(z2_ref[rows, :])
        joined_ref[rows, :] = (value * cut).astype(BF16)

    unit = [part * inverse for part in delta]
    along_x, along_y, along_z = unit
    zero = jnp.zeros_like(along_x)
    first = [ROOT3 * along_x, ROOT3 * along_y, ROOT3 * along_z]
    second = [
        ROOT15 * along_x * along_y,
        ROOT15 * along_y * along_z,
        0.5 * ROOT5 * (2.0 * along_z * along_z - along_x * along_x - along_y * along_y),
        ROOT15 * along_x * along_z,
        0.5 * ROOT15 * (along_x * along_x - along_y * along_y),
    ]
    shapes = [
        jnp.concatenate(rows + [zero] * (16 - len(rows)), axis=0).astype(BF16)
        for rows in (first, second)
    ]
    same = same_ref[...]
    links = [same] + [dot_tn(rows, rows).astype(BF16) * same for rows in shapes]
    weight = jnp.dot(w_env_ref[...], joined_ref[0:LAT, :], preferred_element_type=F32)
    z3_ref[...] = jnp.dot(
        w_lat_ref[:, 0:LAT], joined_ref[0:LAT, :], preferred_element_type=F32
    )
    weight_b = weight.astype(BF16)
    sums = [jnp.dot(weight_b, link, preferred_element_type=F32) for link in links]
    for degree in range(3):
        rows = slice(LAT + degree * CH, LAT + (degree + 1) * CH)
        joined_ref[rows, :] = (weight * sums[degree]).astype(BF16)

    z3_ref[...] += jnp.dot(
        w_lat_ref[:, LAT:], joined_ref[LAT:, :], preferred_element_type=F32
    )
    energy = jnp.zeros((8, PAIRS), F32)
    cut_grad = jnp.zeros((8, PAIRS), F32)
    for start in range(0, LAT, ROWS):
        rows = pl.ds(start, ROWS)
        value, gate = silu_parts(z3_ref[rows, :])
        readout = w_out_ref[rows, :].astype(F32)
        readout = jnp.concatenate([readout, readout], axis=1)
        updated = (joined_ref[rows, :].astype(F32) + value * cut).astype(BF16).astype(F32)
        energy = energy + folded(readout * updated)
        cut_grad = cut_grad + folded(readout * value)
        dz_ref[rows, :] = (readout * cut * gate).astype(BF16)

    grad_ref[LAT:, :] = jnp.dot(w_lat_t_ref[LAT:, :], dz_ref[...], preferred_element_type=F32)
    grad_ref[0:LAT, :] = jnp.dot(w_lat_t_ref[0:LAT, :], dz_ref[...], preferred_element_type=F32)
    weight_grad = jnp.zeros_like(weight)
    passes = []
    for degree in range(3):
        inv_grad = grad_ref[LAT + degree * CH : LAT + (degree + 1) * CH, :]
        passed = (inv_grad * weight).astype(BF16)
        weight_grad = weight_grad + inv_grad * sums[degree]
        weight_grad = weight_grad + jnp.dot(passed, links[degree], preferred_element_type=F32)
        passes.append(passed)
    dlat_ref[...] = jnp.dot(
        w_env_t_ref[...], weight_grad.astype(BF16), preferred_element_type=F32
    )
    for start in range(0, LAT, ROWS):
        rows = pl.ds(start, ROWS)
        readout = w_out_ref[rows, :].astype(F32)
        readout = jnp.concatenate([readout, readout], axis=1)
        value, gate = silu_parts(z2_ref[rows, :])
        dlat = readout + grad_ref[rows, :] + dlat_ref[rows, :]
        cut_grad = cut_grad + folded(dlat * value)
        dz_ref[rows, :] = (dlat * cut * gate).astype(BF16)
    shape_grad = []
    for degree in (1, 2):
        passed = passes[degree]
        both = dot_tn(
            jnp.concatenate([weight_b, passed], axis=0),
            jnp.concatenate([passed, weight_b], axis=0),
        )
        both = both.astype(BF16) * same
        shape_grad.append(jnp.dot(shapes[degree - 1], both, preferred_element_type=F32))
    dlat_ref[...] = jnp.dot(w_hid_t_ref[...], dz_ref[...], preferred_element_type=F32)
    for start in range(0, LAT, ROWS):
        rows = pl.ds(start, ROWS)
        dz_ref[rows, :] = (dlat_ref[rows, :] * z1_ref[rows, :]).astype(BF16)
    feature_grad = jnp.dot(w_in_t_ref[...], dz_ref[...], preferred_element_type=F32)[0:8, :]

    cut_grad = column_sum(cut_grad + feature_grad * bessel)
    radius_grad = cut_grad * slope + cut * column_sum(feature_grad * bessel_slope)
    g1, g2, g3 = [shape_grad[0][i : i + 1] for i in range(3)]
    g4, g5, g6, g7, g8 = [shape_grad[1][i : i + 1] for i in range(5)]
    unit_grad = [
        ROOT3 * g1 + ROOT15 * (along_y * g4 + along_z * g7 + along_x * g8) - ROOT5 * along_x * g6,
        ROOT3 * g2 + ROOT15 * (along_x * g4 + along_z * g5 - along_y * g8) - ROOT5 * along_y * g6,
        ROOT3 * g3 + ROOT15 * (along_y * g5 + along_x * g7) + 2.0 * ROOT5 * along_z * g6,
    ]
    radial = sum(g * u for g, u in zip(unit_grad, unit))
    radius_grad = radius_grad - radial * inverse
    push = [g * inverse + radius_grad * u for g, u in zip(unit_grad, unit)]

    row = lax.broadcasted_iota(jnp.int32, (112, PAIRS), 0)
    axis = row & 3
    moved = jnp.where(axis == 0, push[0], jnp.where(axis == 1, push[1], push[2]))
    moved = jnp.where(axis == 3, 0.0, moved)
    spread = split_dot_nt(jnp.where((row >> 2) == slot, -moved, 0.0), hits_ref[0])
    home = split_dot_nt(moved[0:8], hits_ref[1])[0:4]
    spread = spread.reshape(28, 4, ATOMS)
    energy = column_sum(energy)
    energy = energy[:, 0:ATOMS] + energy[:, ATOMS:PAIRS]
    is_energy = lax.broadcasted_iota(jnp.int32, (4, ATOMS), 0) == 3
    blank = jnp.where(is_energy, energy, 0.0)
    out_ref[...] = jnp.broadcast_to(blank[None, None], out_ref.shape)
    for at_x in range(3):
        number = (place + (at_x + RING - 1)) & (RING - 1)
        for cell in range(9):
            block = spread[9 * at_x + cell]
            if 9 * at_x + cell == 13:
                block = block + home
            out_ref[number, cell] = block + blank


def pair_forces(*operands):
    vmem = pl.BlockSpec(memory_space=pltpu.VMEM)
    return pl.pallas_call(
        force_kernel,
        out_shape=jax.ShapeDtypeStruct((RING, 9, 4, ATOMS), F32),
        in_specs=[vmem] * 15,
        out_specs=vmem,
        scratch_shapes=[
            pltpu.VMEM((LAT, PAIRS), F32),
            pltpu.VMEM((LAT, PAIRS), F32),
            pltpu.VMEM((LAT, PAIRS), F32),
            pltpu.VMEM((LAT, PAIRS), BF16),
            pltpu.VMEM((LAT + 3 * CH, PAIRS), BF16),
            pltpu.VMEM((LAT + 3 * CH, PAIRS), F32),
            pltpu.VMEM((LAT, PAIRS), BF16),
            pltpu.VMEM((LAT, PAIRS), F32),
        ],
        compiler_params=pltpu.CompilerParams(vmem_limit_bytes=24 * 1024 * 1024),
        name="forces_of_pairs",
    )(*operands)


SMALL = pltpu.CompilerParams(vmem_limit_bytes=2 * 1024 * 1024)
EVEN = [(i, i ^ 1) for i in range(RING)]
ODD = [(i, (((i + 1) ^ 1) - 1) % RING) for i in range(RING)]


def body(coords, species, pair_ids, live_counts, w_two_in, w_two_hid, w_env, w_latent, w_out):
    ids = pair_ids[0, 0, 0]
    counts = live_counts[0, 0, 0]
    vmem = pl.BlockSpec(memory_space=pltpu.VMEM)
    smem = pl.BlockSpec(memory_space=pltpu.SMEM)
    packed = pl.pallas_call(
        pack_kernel,
        out_shape=jax.ShapeDtypeStruct((RING * RING, 4, ATOMS), F32),
        in_specs=[vmem] * 2,
        out_specs=vmem,
        compiler_params=SMALL,
        name="pack_frame",
    )(coords.reshape(3, 1, ATOMS), species.reshape(1, ATOMS))
    plane = pl.pallas_call(
        pick_kernel,
        out_shape=jax.ShapeDtypeStruct((9, 4, ATOMS), F32),
        in_specs=[vmem],
        out_specs=vmem,
        compiler_params=SMALL,
        name="pick_plane",
    )(lax.all_to_all(packed, ("gy", "gz"), 0, 0))
    even = lax.ppermute(plane, "gx", EVEN)
    odd = lax.ppermute(plane, "gx", ODD)

    pairs, hits, same, readout = pl.pallas_call(
        prepare_kernel,
        out_shape=(
            jax.ShapeDtypeStruct((8, PAIRS), jnp.int32),
            jax.ShapeDtypeStruct((2, ATOMS, PAIRS), BF16),
            jax.ShapeDtypeStruct((PAIRS, PAIRS), BF16),
            jax.ShapeDtypeStruct((LAT, ATOMS), BF16),
        ),
        in_specs=[smem, vmem, vmem],
        out_specs=(vmem,) * 4,
        compiler_params=SMALL,
        name="prepare_pairs",
    )(counts, ids, w_out)
    w_in = jnp.pad(w_two_in, ((0, 0), (0, 4)))
    sent = pair_forces(
        pairs,
        hits,
        even,
        plane,
        odd,
        same,
        w_in,
        w_in.T,
        w_two_hid,
        w_two_hid.T,
        w_env,
        w_env.T,
        w_latent,
        w_latent.T,
        readout,
    )
    addressed = pl.pallas_call(
        address_kernel,
        out_shape=jax.ShapeDtypeStruct((RING * RING, 4, ATOMS), F32),
        in_specs=[vmem],
        out_specs=vmem,
        compiler_params=SMALL,
        name="address_plane",
    )(lax.all_to_all(sent, "gx", 0, 0))
    forces, energy = pl.pallas_call(
        finish_kernel,
        out_shape=(jax.ShapeDtypeStruct((3, 1, ATOMS), F32), jax.ShapeDtypeStruct((1,), F32)),
        in_specs=[vmem],
        out_specs=(vmem, smem),
        compiler_params=SMALL,
        name="finish",
    )(lax.all_to_all(addressed, ("gy", "gz"), 0, 0))
    return forces.reshape(1, 1, 1, 3, ATOMS), energy.reshape(())


def solution(mesh):
    in_specs = (
        P("gx", "gy", "gz", None, None),
        P("gx", "gy", "gz", None),
        P("gx", "gy", "gz", None, None),
        P("gx", "gy", "gz", None),
        P(),
        P(),
        P(),
        P(),
        P(),
    )
    out_specs = (P("gx", "gy", "gz", None, None), P())
    return jax.shard_map(body, mesh=mesh, in_specs=in_specs, out_specs=out_specs, check_vma=False)
```

```python
import math

import jax
import jax.numpy as jnp
from jax import lax
from jax.experimental import pallas as pl
from jax.experimental.pallas import tpu as pltpu
from jax.sharding import PartitionSpec as P

F32 = jnp.float32
BF16 = jnp.bfloat16
CUTOFF = 6.0
SOFTEN = 0.01
ENV_NORM = 0.25
EXTENT = (16.0, 16.0, 4.0)
ROOT3 = math.sqrt(3.0)
ROOT5 = math.sqrt(5.0)
ROOT15 = math.sqrt(15.0)
DEGREE = (0, 1, 1, 1, 2, 2, 2, 2, 2)
RING = 8
LAT = 512
CH = 64
PAIRS = 256
ATOMS = 128
ROWS = 64


def column_sum(block):
    return jnp.sum(block, axis=0, keepdims=True)


def folded(block):
    return jnp.sum(block.reshape(block.shape[0] // 8, 8, block.shape[1]), axis=0)


def silu_parts(z):
    gate = 0.5 * jnp.tanh(0.5 * z) + 0.5
    value = z * gate
    return value, gate + value * (1.0 - gate)


def dot_tn(left, right):
    return lax.dot_general(left, right, (((0,), (0,)), ((), ())), preferred_element_type=F32)


def split_dot_nt(block, other):
    dims = (((1,), (1,)), ((), ()))
    high = block.astype(BF16)
    low = (block - high.astype(F32)).astype(BF16)
    return lax.dot_general(high, other, dims, preferred_element_type=F32) + lax.dot_general(
        low, other, dims, preferred_element_type=F32
    )


def pack_kernel(frame_ref, out_ref):
    out_ref[...] = jnp.broadcast_to(frame_ref[...][None], out_ref.shape)


def around():
    at_y, at_z = lax.axis_index("gy"), lax.axis_index("gz")
    return [
        ((at_y + (RING + step_y)) & (RING - 1)) * RING + ((at_z + (RING + step_z)) & (RING - 1))
        for step_y in (-1, 0, 1)
        for step_z in (-1, 0, 1)
    ]


def pick_kernel(received_ref, out_ref):
    for cell, number in enumerate(around()):
        out_ref[cell] = received_ref[number]


def address_kernel(received_ref, out_ref):
    total = jnp.sum(received_ref[...], axis=0)
    is_energy = lax.broadcasted_iota(jnp.int32, (4, ATOMS), 0) == 3
    blank = jnp.where(is_energy, total[4], 0.0)
    out_ref[...] = jnp.broadcast_to(blank[None], out_ref.shape)
    for cell, number in enumerate(around()):
        out_ref[number] = total[cell]


def finish_kernel(received_ref, forces_ref, energy_ref):
    total = jnp.sum(received_ref[...], axis=0)
    for axis in range(3):
        forces_ref[axis] = total[axis : axis + 1]
    energy_ref[0] = jnp.sum(total[3:4]) * (1.0 / (ATOMS * RING**3))


def prepare_kernel(counts_ref, ids_ref, w_out_ref, pairs_ref, hits_ref, same_ref, readout_ref):
    centre = ids_ref[0:1, :]
    neighbour = ids_ref[1:2, :]
    lane = lax.broadcasted_iota(jnp.int32, (1, PAIRS), 1)
    live = lane < jnp.where(lane < ATOMS, counts_ref[0], counts_ref[1] + ATOMS)
    rows = [centre, neighbour >> 7, neighbour & 127, live.astype(jnp.int32)]
    pairs_ref[...] = jnp.concatenate(rows + rows, axis=0)
    atom_row = lax.broadcasted_iota(jnp.int32, (ATOMS, PAIRS), 0)
    hits_ref[0] = jnp.where(atom_row == rows[2], 1.0, 0.0).astype(BF16)
    hits_ref[1] = jnp.where(atom_row == centre, 1.0, 0.0).astype(BF16)
    across = jnp.broadcast_to(centre.astype(F32), (PAIRS, PAIRS))
    same_ref[...] = jnp.where(across == across.T, ENV_NORM, 0.0).astype(BF16)
    readout_ref[...] = jnp.broadcast_to(w_out_ref[...].astype(F32), (ATOMS, LAT)).T.astype(BF16)


def force_kernel(
    pairs_ref,
    hits_ref,
    even_ref,
    level_ref,
    odd_ref,
    same_ref,
    w_in_ref,
    w_in_t_ref,
    w_hid_ref,
    w_hid_t_ref,
    w_env_ref,
    w_env_t_ref,
    w_lat_ref,
    w_lat_t_ref,
    w_out_ref,
    out_ref,
    z1_ref,
    z2_ref,
    z3_ref,
    hidden_ref,
    joined_ref,
    grad_ref,
    dz_ref,
    dlat_ref,
):
    centre = pairs_ref[0:1, :]
    slot = pairs_ref[1:2, :]
    atom = pairs_ref[2:3, :]
    live = pairs_ref[3:4, :].astype(F32)
    step_x = (slot * 57) >> 9
    rest = slot - 9 * step_x
    step_y = (rest * 11) >> 5
    step_z = rest - 3 * step_y

    place = lax.axis_index("gx")
    parity = place & 1
    near, own = [], []
    for half in range(2):
        lanes = slice(half * ATOMS, (half + 1) * ATOMS)
        pick = jnp.broadcast_to(atom[:, lanes], (4, ATOMS))
        slot_half = jnp.broadcast_to(slot[:, lanes], (4, ATOMS))
        total = jnp.zeros((4, ATOMS), F32)
        for slab, base in ((even_ref, 18 * (1 - parity)), (level_ref, 9), (odd_ref, 18 * parity)):
            for cell in range(9):
                rows = jnp.take_along_axis(slab[cell], pick, axis=1, mode="promise_in_bounds")
                total = jnp.where(slot_half == base + cell, rows, total)
        near.append(total)
        pick = jnp.broadcast_to(centre[:, lanes], (4, ATOMS))
        own.append(jnp.take_along_axis(level_ref[4], pick, axis=1, mode="promise_in_bounds"))
    near = jnp.concatenate(near, axis=1)
    own = jnp.concatenate(own, axis=1)
    delta = [
        near[axis : axis + 1, :]
        + (step - 1).astype(F32) * EXTENT[axis]
        - own[axis : axis + 1, :]
        for axis, step in enumerate((step_x, step_y, step_z))
    ]

    radius = jnp.sqrt(delta[0] * delta[0] + delta[1] * delta[1] + delta[2] * delta[2] + SOFTEN)
    inverse = 1.0 / radius
    ratio = radius * (1.0 / CUTOFF)
    inside = jnp.where(ratio < 1.0, live, 0.0)
    square = ratio * ratio
    fifth = square * square * ratio
    sixth = fifth * ratio
    cut = inside * (1.0 + sixth * (-28.0 + 48.0 * ratio - 21.0 * square))
    slope = inside * (-168.0 / CUTOFF) * fifth * (1.0 - ratio) * (1.0 - ratio)

    row8 = lax.broadcasted_iota(jnp.int32, (8, PAIRS), 0)
    order = (row8 + 1).astype(F32)
    turns = order * ratio
    whole = jnp.floor(turns + 0.5)
    sign = 1.0 - 2.0 * (whole.astype(jnp.int32) & 1).astype(F32)
    angle = (turns - whole) * math.pi
    angle2 = angle * angle
    sine = jnp.zeros_like(angle)
    for power in (11, 9, 7, 5, 3, 1):
        sine = sine * angle2 + (-1.0) ** (power // 2) / math.factorial(power)
    sine = sine * angle * sign
    cosine = jnp.zeros_like(angle)
    for power in (12, 10, 8, 6, 4, 2, 0):
        cosine = cosine * angle2 + (-1.0) ** (power // 2) / math.factorial(power)
    cosine = cosine * sign
    front = math.sqrt(2.0 / CUTOFF)
    bessel = front * sine * inverse
    bessel_slope = (front * math.pi / CUTOFF) * order * cosine * inverse - bessel * inverse

    kind_at = jnp.where(row8 < 2, own[3:4, :], near[3:4, :])
    kind = jnp.where((row8 < 4) & (kind_at == (row8 & 1).astype(F32)), 1.0, 0.0)
    features = jnp.concatenate([bessel * cut, kind], axis=0).astype(BF16)

    z1_ref[...] = jnp.dot(w_in_ref[...], features, preferred_element_type=F32)
    for start in range(0, LAT, ROWS):
        rows = pl.ds(start, ROWS)
        value, gate = silu_parts(z1_ref[rows, :])
        hidden_ref[rows, :] = value.astype(BF16)
        z1_ref[rows, :] = gate
    z2_ref[...] = jnp.dot(w_hid_ref[...], hidden_ref[...], preferred_element_type=F32)
    for start in range(0, LAT, ROWS):
        rows = pl.ds(start, ROWS)
        value, unused = silu_parts(z2_ref[rows, :])
        joined_ref[rows, :] = (value * cut).astype(BF16)

    unit = [part * inverse for part in delta]
    along_x, along_y, along_z = unit
    zero = jnp.zeros_like(along_x)
    first = [ROOT3 * along_x, ROOT3 * along_y, ROOT3 * along_z]
    second = [
        ROOT15 * along_x * along_y,
        ROOT15 * along_y * along_z,
        0.5 * ROOT5 * (2.0 * along_z * along_z - along_x * along_x - along_y * along_y),
        ROOT15 * along_x * along_z,
        0.5 * ROOT15 * (along_x * along_x - along_y * along_y),
    ]
    shapes = [
        jnp.concatenate(rows + [zero] * (16 - len(rows)), axis=0).astype(BF16)
        for rows in (first, second)
    ]
    same = same_ref[...]
    links = [same] + [dot_tn(rows, rows).astype(BF16) * same for rows in shapes]
    weight = jnp.dot(w_env_ref[...], joined_ref[0:LAT, :], preferred_element_type=F32)
    z3_ref[...] = jnp.dot(
        w_lat_ref[:, 0:LAT], joined_ref[0:LAT, :], preferred_element_type=F32
    )
    weight_b = weight.astype(BF16)
    sums = [jnp.dot(weight_b, link, preferred_element_type=F32) for link in links]
    for degree in range(3):
        rows = slice(LAT + degree * CH, LAT + (degree + 1) * CH)
        joined_ref[rows, :] = (weight * sums[degree]).astype(BF16)

    z3_ref[...] += jnp.dot(
        w_lat_ref[:, LAT:], joined_ref[LAT:, :], preferred_element_type=F32
    )
    energy = jnp.zeros((8, PAIRS), F32)
    cut_grad = jnp.zeros((8, PAIRS), F32)
    for start in range(0, LAT, ROWS):
        rows = pl.ds(start, ROWS)
        value, gate = silu_parts(z3_ref[rows, :])
        readout = w_out_ref[rows, :].astype(F32)
        readout = jnp.concatenate([readout, readout], axis=1)
        updated = (joined_ref[rows, :].astype(F32) + value * cut).astype(BF16).astype(F32)
        energy = energy + folded(readout * updated)
        cut_grad = cut_grad + folded(readout * value)
        dz_ref[rows, :] = (readout * cut * gate).astype(BF16)

    grad_ref[LAT:, :] = jnp.dot(w_lat_t_ref[LAT:, :], dz_ref[...], preferred_element_type=F32)
    grad_ref[0:LAT, :] = jnp.dot(w_lat_t_ref[0:LAT, :], dz_ref[...], preferred_element_type=F32)
    weight_grad = jnp.zeros_like(weight)
    passes = []
    for degree in range(3):
        inv_grad = grad_ref[LAT + degree * CH : LAT + (degree + 1) * CH, :]
        passed = (inv_grad * weight).astype(BF16)
        weight_grad = weight_grad + inv_grad * sums[degree]
        weight_grad = weight_grad + jnp.dot(passed, links[degree], preferred_element_type=F32)
        passes.append(passed)
    dlat_ref[...] = jnp.dot(
        w_env_t_ref[...], weight_grad.astype(BF16), preferred_element_type=F32
    )
    for start in range(0, LAT, ROWS):
        rows = pl.ds(start, ROWS)
        readout = w_out_ref[rows, :].astype(F32)
        readout = jnp.concatenate([readout, readout], axis=1)
        value, gate = silu_parts(z2_ref[rows, :])
        dlat = readout + grad_ref[rows, :] + dlat_ref[rows, :]
        cut_grad = cut_grad + folded(dlat * value)
        dz_ref[rows, :] = (dlat * cut * gate).astype(BF16)
    shape_grad = []
    for degree in (1, 2):
        passed = passes[degree]
        both = dot_tn(
            jnp.concatenate([weight_b, passed], axis=0),
            jnp.concatenate([passed, weight_b], axis=0),
        )
        both = both.astype(BF16) * same
        shape_grad.append(jnp.dot(shapes[degree - 1], both, preferred_element_type=F32))
    dlat_ref[...] = jnp.dot(w_hid_t_ref[...], dz_ref[...], preferred_element_type=F32)
    for start in range(0, LAT, ROWS):
        rows = pl.ds(start, ROWS)
        dz_ref[rows, :] = (dlat_ref[rows, :] * z1_ref[rows, :]).astype(BF16)
    feature_grad = jnp.dot(w_in_t_ref[...], dz_ref[...], preferred_element_type=F32)[0:8, :]

    cut_grad = column_sum(cut_grad + feature_grad * bessel)
    radius_grad = cut_grad * slope + cut * column_sum(feature_grad * bessel_slope)
    g1, g2, g3 = [shape_grad[0][i : i + 1] for i in range(3)]
    g4, g5, g6, g7, g8 = [shape_grad[1][i : i + 1] for i in range(5)]
    unit_grad = [
        ROOT3 * g1 + ROOT15 * (along_y * g4 + along_z * g7 + along_x * g8) - ROOT5 * along_x * g6,
        ROOT3 * g2 + ROOT15 * (along_x * g4 + along_z * g5 - along_y * g8) - ROOT5 * along_y * g6,
        ROOT3 * g3 + ROOT15 * (along_y * g5 + along_x * g7) + 2.0 * ROOT5 * along_z * g6,
    ]
    radial = sum(g * u for g, u in zip(unit_grad, unit))
    radius_grad = radius_grad - radial * inverse
    push = [g * inverse + radius_grad * u for g, u in zip(unit_grad, unit)]

    row = lax.broadcasted_iota(jnp.int32, (112, PAIRS), 0)
    axis = row & 3
    moved = jnp.where(axis == 0, push[0], jnp.where(axis == 1, push[1], push[2]))
    moved = jnp.where(axis == 3, 0.0, moved)
    spread = split_dot_nt(jnp.where((row >> 2) == slot, -moved, 0.0), hits_ref[0])
    home = split_dot_nt(moved[0:8], hits_ref[1])[0:4]
    spread = spread.reshape(28, 4, ATOMS)
    energy = column_sum(energy)
    energy = energy[:, 0:ATOMS] + energy[:, ATOMS:PAIRS]
    is_energy = lax.broadcasted_iota(jnp.int32, (4, ATOMS), 0) == 3
    blank = jnp.where(is_energy, energy, 0.0)
    out_ref[...] = jnp.broadcast_to(blank[None, None], out_ref.shape)
    for at_x in range(3):
        number = (place + (at_x + RING - 1)) & (RING - 1)
        for cell in range(9):
            block = spread[9 * at_x + cell]
            if 9 * at_x + cell == 13:
                block = block + home
            out_ref[number, cell] = block + blank


def pair_forces(*operands):
    vmem = pl.BlockSpec(memory_space=pltpu.VMEM)
    return pl.pallas_call(
        force_kernel,
        out_shape=jax.ShapeDtypeStruct((RING, 9, 4, ATOMS), F32),
        in_specs=[vmem] * 15,
        out_specs=vmem,
        scratch_shapes=[
            pltpu.VMEM((LAT, PAIRS), F32),
            pltpu.VMEM((LAT, PAIRS), F32),
            pltpu.VMEM((LAT, PAIRS), F32),
            pltpu.VMEM((LAT, PAIRS), BF16),
            pltpu.VMEM((LAT + 3 * CH, PAIRS), BF16),
            pltpu.VMEM((LAT + 3 * CH, PAIRS), F32),
            pltpu.VMEM((LAT, PAIRS), BF16),
            pltpu.VMEM((LAT, PAIRS), F32),
        ],
        compiler_params=pltpu.CompilerParams(vmem_limit_bytes=24 * 1024 * 1024),
        name="forces_of_pairs",
    )(*operands)


SMALL = pltpu.CompilerParams(vmem_limit_bytes=2 * 1024 * 1024)
EVEN = [(i, i ^ 1) for i in range(RING)]
ODD = [(i, (((i + 1) ^ 1) - 1) % RING) for i in range(RING)]


def body(coords, species, pair_ids, live_counts, w_two_in, w_two_hid, w_env, w_latent, w_out):
    ids = pair_ids[0, 0, 0]
    counts = live_counts[0, 0, 0]
    vmem = pl.BlockSpec(memory_space=pltpu.VMEM)
    smem = pl.BlockSpec(memory_space=pltpu.SMEM)
    packed = pl.pallas_call(
        pack_kernel,
        out_shape=jax.ShapeDtypeStruct((RING * RING, 4, ATOMS), F32),
        in_specs=[vmem],
        out_specs=vmem,
        compiler_params=SMALL,
        name="pack_frame",
    )(jnp.concatenate([coords[0, 0, 0], species[0, 0, 0].astype(F32)[None]], axis=0))
    plane = pl.pallas_call(
        pick_kernel,
        out_shape=jax.ShapeDtypeStruct((9, 4, ATOMS), F32),
        in_specs=[vmem],
        out_specs=vmem,
        compiler_params=SMALL,
        name="pick_plane",
    )(lax.all_to_all(packed, ("gy", "gz"), 0, 0))
    even = lax.ppermute(plane, "gx", EVEN)
    odd = lax.ppermute(plane, "gx", ODD)

    pairs, hits, same, readout = pl.pallas_call(
        prepare_kernel,
        out_shape=(
            jax.ShapeDtypeStruct((8, PAIRS), jnp.int32),
            jax.ShapeDtypeStruct((2, ATOMS, PAIRS), BF16),
            jax.ShapeDtypeStruct((PAIRS, PAIRS), BF16),
            jax.ShapeDtypeStruct((LAT, ATOMS), BF16),
        ),
        in_specs=[smem, vmem, vmem],
        out_specs=(vmem,) * 4,
        compiler_params=SMALL,
        name="prepare_pairs",
    )(counts, ids, w_out)
    w_in = jnp.pad(w_two_in, ((0, 0), (0, 4)))
    sent = pair_forces(
        pairs,
        hits,
        even,
        plane,
        odd,
        same,
        w_in,
        w_in.T,
        w_two_hid,
        w_two_hid.T,
        w_env,
        w_env.T,
        w_latent,
        w_latent.T,
        readout,
    )
    addressed = pl.pallas_call(
        address_kernel,
        out_shape=jax.ShapeDtypeStruct((RING * RING, 4, ATOMS), F32),
        in_specs=[vmem],
        out_specs=vmem,
        compiler_params=SMALL,
        name="address_plane",
    )(lax.all_to_all(sent, "gx", 0, 0))
    forces, energy = pl.pallas_call(
        finish_kernel,
        out_shape=(jax.ShapeDtypeStruct((3, 1, ATOMS), F32), jax.ShapeDtypeStruct((1,), F32)),
        in_specs=[vmem],
        out_specs=(vmem, smem),
        compiler_params=SMALL,
        name="finish",
    )(lax.all_to_all(addressed, ("gy", "gz"), 0, 0))
    return forces.reshape(1, 1, 1, 3, ATOMS), energy.reshape(())


def solution(mesh):
    in_specs = (
        P("gx", "gy", "gz", None, None),
        P("gx", "gy", "gz", None),
        P("gx", "gy", "gz", None, None),
        P("gx", "gy", "gz", None),
        P(),
        P(),
        P(),
        P(),
        P(),
    )
    out_specs = (P("gx", "gy", "gz", None, None), P())
    return jax.shard_map(body, mesh=mesh, in_specs=in_specs, out_specs=out_specs, check_vma=False)
```

```python
import math

import jax
import jax.numpy as jnp
from jax import lax
from jax.experimental import pallas as pl
from jax.experimental.pallas import tpu as pltpu
from jax.sharding import PartitionSpec as P

F32 = jnp.float32
BF16 = jnp.bfloat16
CUTOFF = 6.0
SOFTEN = 0.01
ENV_NORM = 0.25
EXTENT = (16.0, 16.0, 4.0)
ROOT3 = math.sqrt(3.0)
ROOT5 = math.sqrt(5.0)
ROOT15 = math.sqrt(15.0)
RING = 8
LAT = 512
CH = 64
PAIRS = 256
ATOMS = 128
ROWS = 64


def column_sum(block):
    return jnp.sum(block, axis=0, keepdims=True)


def folded(block):
    return jnp.sum(block.reshape(block.shape[0] // 8, 8, block.shape[1]), axis=0)


def silu_parts(z):
    gate = 0.5 * jnp.tanh(0.5 * z) + 0.5
    value = z * gate
    return value, gate + value * (1.0 - gate)


def dot_tn(left, right):
    return lax.dot_general(left, right, (((0,), (0,)), ((), ())), preferred_element_type=F32)


def split_dot_nt(block, other):
    dims = (((1,), (1,)), ((), ()))
    high = block.astype(BF16)
    low = (block - high.astype(F32)).astype(BF16)
    return lax.dot_general(high, other, dims, preferred_element_type=F32) + lax.dot_general(
        low, other, dims, preferred_element_type=F32
    )


def pack_kernel(frame_ref, out_ref):
    out_ref[...] = jnp.broadcast_to(frame_ref[...][None], out_ref.shape)


def place_of():
    at_z = lax.axis_index("gz")
    return lax.axis_index("gx"), lax.axis_index("gy"), at_z >> 1, at_z & 1


def around():
    at_y, at_z = lax.axis_index("gy"), lax.axis_index("gz")
    return [
        ((at_y + (RING + step_y)) & (RING - 1)) * RING + ((at_z + (RING + step_z)) & (RING - 1))
        for step_y in (-1, 0, 1)
        for step_z in (-1, 0, 1)
    ]


def relay_kernel(near_ref, out_ref):
    at_x, at_y, chip, high = place_of()
    own, other = (at_x & 1) * 16, (1 - (at_x & 1)) * 16
    side = 1 - (at_x & 1)
    out_ref[...] = jnp.zeros(out_ref.shape, F32)
    chip_third = (chip + 5 - 2 * high) & 3
    for row in range(3):
        number = ((at_y + (RING - 1 + row)) & (RING - 1)) * 2
        for level in range(2):
            out_ref[(1 - side) * 4 + chip, 2 * row + level] = near_ref[own + number + level]
        for to in (side, 1 - side):
            out_ref[to * 4 + chip_third, row] = near_ref[own + number + 1 - high]
            out_ref[to * 4 + chip_third, 3 + row] = near_ref[other + number + 1 - high]


def pick_kernel(near_ref, far_ref, even_ref, level_ref, odd_ref):
    at_x, at_y, chip, high = place_of()
    own, other = (at_x & 1) * 16, (1 - (at_x & 1)) * 16
    side = 1 - (at_x & 1)
    chip_third = (chip + 3 + 2 * high) & 3
    for row in range(3):
        number = ((at_y + (RING - 1 + row)) & (RING - 1)) * 2
        for level in range(2):
            cell = 3 * row + 1 + level - high
            level_ref[cell] = near_ref[own + number + level]
            even_ref[cell] = near_ref[other + number + level]
            odd_ref[cell] = far_ref[(1 - side) * 4 + chip, 2 * row + level]
        cell = 3 * row + 2 * high
        level_ref[cell] = far_ref[side * 4 + chip_third, row]
        even_ref[cell] = far_ref[side * 4 + chip_third, 3 + row]
        odd_ref[cell] = far_ref[(1 - side) * 4 + chip_third, row]


def address_kernel(received_ref, out_ref):
    total = jnp.sum(received_ref[...], axis=0)
    is_energy = lax.broadcasted_iota(jnp.int32, (4, ATOMS), 0) == 3
    blank = jnp.where(is_energy, total[4], 0.0)
    out_ref[...] = jnp.broadcast_to(blank[None], out_ref.shape)
    for cell, number in enumerate(around()):
        out_ref[number] = total[cell]


def finish_kernel(received_ref, forces_ref, energy_ref):
    total = jnp.sum(received_ref[...], axis=0)
    for axis in range(3):
        forces_ref[axis] = total[axis : axis + 1]
    energy_ref[0] = jnp.sum(total[3:4]) * (1.0 / (ATOMS * RING**3))


def prepare_kernel(counts_ref, ids_ref, w_out_ref, pairs_ref, hits_ref, same_ref, readout_ref):
    centre = ids_ref[0:1, :]
    neighbour = ids_ref[1:2, :]
    lane = lax.broadcasted_iota(jnp.int32, (1, PAIRS), 1)
    live = lane < jnp.where(lane < ATOMS, counts_ref[0], counts_ref[1] + ATOMS)
    rows = [centre, neighbour >> 7, neighbour & 127, live.astype(jnp.int32)]
    pairs_ref[...] = jnp.concatenate(rows + rows, axis=0)
    atom_row = lax.broadcasted_iota(jnp.int32, (ATOMS, PAIRS), 0)
    hits_ref[0] = jnp.where(atom_row == rows[2], 1.0, 0.0).astype(BF16)
    hits_ref[1] = jnp.where(atom_row == centre, 1.0, 0.0).astype(BF16)
    across = jnp.broadcast_to(centre.astype(F32), (PAIRS, PAIRS))
    same_ref[...] = jnp.where(across == across.T, ENV_NORM, 0.0).astype(BF16)
    readout_ref[...] = jnp.broadcast_to(w_out_ref[...].astype(F32), (ATOMS, LAT)).T.astype(BF16)


def force_kernel(
    pairs_ref,
    hits_ref,
    even_ref,
    level_ref,
    odd_ref,
    same_ref,
    w_in_ref,
    w_in_t_ref,
    w_hid_ref,
    w_hid_t_ref,
    w_env_ref,
    w_env_t_ref,
    w_lat_ref,
    w_lat_t_ref,
    w_out_ref,
    out_ref,
    z1_ref,
    z2_ref,
    z3_ref,
    hidden_ref,
    joined_ref,
    grad_ref,
    dz_ref,
    dlat_ref,
):
    centre = pairs_ref[0:1, :]
    slot = pairs_ref[1:2, :]
    atom = pairs_ref[2:3, :]
    live = pairs_ref[3:4, :].astype(F32)
    step_x = (slot * 57) >> 9
    rest = slot - 9 * step_x
    step_y = (rest * 11) >> 5
    step_z = rest - 3 * step_y

    place = lax.axis_index("gx")
    parity = place & 1
    near, own = [], []
    for half in range(2):
        lanes = slice(half * ATOMS, (half + 1) * ATOMS)
        pick = jnp.broadcast_to(atom[:, lanes], (4, ATOMS))
        slot_half = jnp.broadcast_to(slot[:, lanes], (4, ATOMS))
        total = jnp.zeros((4, ATOMS), F32)
        for slab, base in ((even_ref, 18 * (1 - parity)), (level_ref, 9), (odd_ref, 18 * parity)):
            for cell in range(9):
                rows = jnp.take_along_axis(slab[cell], pick, axis=1, mode="promise_in_bounds")
                total = jnp.where(slot_half == base + cell, rows, total)
        near.append(total)
        pick = jnp.broadcast_to(centre[:, lanes], (4, ATOMS))
        own.append(jnp.take_along_axis(level_ref[4], pick, axis=1, mode="promise_in_bounds"))
    near = jnp.concatenate(near, axis=1)
    own = jnp.concatenate(own, axis=1)
    delta = [
        near[axis : axis + 1, :]
        + (step - 1).astype(F32) * EXTENT[axis]
        - own[axis : axis + 1, :]
        for axis, step in enumerate((step_x, step_y, step_z))
    ]

    radius = jnp.sqrt(delta[0] * delta[0] + delta[1] * delta[1] + delta[2] * delta[2] + SOFTEN)
    inverse = 1.0 / radius
    ratio = radius * (1.0 / CUTOFF)
    inside = jnp.where(ratio < 1.0, live, 0.0)
    square = ratio * ratio
    fifth = square * square * ratio
    sixth = fifth * ratio
    cut = inside * (1.0 + sixth * (-28.0 + 48.0 * ratio - 21.0 * square))
    slope = inside * (-168.0 / CUTOFF) * fifth * (1.0 - ratio) * (1.0 - ratio)

    row8 = lax.broadcasted_iota(jnp.int32, (8, PAIRS), 0)
    order = (row8 + 1).astype(F32)
    turns = order * ratio
    whole = jnp.floor(turns + 0.5)
    sign = 1.0 - 2.0 * (whole.astype(jnp.int32) & 1).astype(F32)
    angle = (turns - whole) * math.pi
    angle2 = angle * angle
    sine = jnp.zeros_like(angle)
    for power in (11, 9, 7, 5, 3, 1):
        sine = sine * angle2 + (-1.0) ** (power // 2) / math.factorial(power)
    sine = sine * angle * sign
    cosine = jnp.zeros_like(angle)
    for power in (12, 10, 8, 6, 4, 2, 0):
        cosine = cosine * angle2 + (-1.0) ** (power // 2) / math.factorial(power)
    cosine = cosine * sign
    front = math.sqrt(2.0 / CUTOFF)
    bessel = front * sine * inverse
    bessel_slope = (front * math.pi / CUTOFF) * order * cosine * inverse - bessel * inverse

    kind_at = jnp.where(row8 < 2, own[3:4, :], near[3:4, :])
    kind = jnp.where((row8 < 4) & (kind_at == (row8 & 1).astype(F32)), 1.0, 0.0)
    features = jnp.concatenate([bessel * cut, kind], axis=0).astype(BF16)

    z1_ref[...] = jnp.dot(w_in_ref[...], features, preferred_element_type=F32)
    for start in range(0, LAT, ROWS):
        rows = pl.ds(start, ROWS)
        value, gate = silu_parts(z1_ref[rows, :])
        hidden_ref[rows, :] = value.astype(BF16)
        z1_ref[rows, :] = gate
    z2_ref[...] = jnp.dot(w_hid_ref[...], hidden_ref[...], preferred_element_type=F32)
    for start in range(0, LAT, ROWS):
        rows = pl.ds(start, ROWS)
        value, unused = silu_parts(z2_ref[rows, :])
        joined_ref[rows, :] = (value * cut).astype(BF16)

    unit = [part * inverse for part in delta]
    along_x, along_y, along_z = unit
    zero = jnp.zeros_like(along_x)
    first = [ROOT3 * along_x, ROOT3 * along_y, ROOT3 * along_z]
    second = [
        ROOT15 * along_x * along_y,
        ROOT15 * along_y * along_z,
        0.5 * ROOT5 * (2.0 * along_z * along_z - along_x * along_x - along_y * along_y),
        ROOT15 * along_x * along_z,
        0.5 * ROOT15 * (along_x * along_x - along_y * along_y),
    ]
    shapes = [
        jnp.concatenate(rows + [zero] * (16 - len(rows)), axis=0).astype(BF16)
        for rows in (first, second)
    ]
    same = same_ref[...]
    links = [same] + [dot_tn(rows, rows).astype(BF16) * same for rows in shapes]
    weight = jnp.dot(w_env_ref[...], joined_ref[0:LAT, :], preferred_element_type=F32)
    z3_ref[...] = jnp.dot(
        w_lat_ref[:, 0:LAT], joined_ref[0:LAT, :], preferred_element_type=F32
    )
    weight_b = weight.astype(BF16)
    sums = [jnp.dot(weight_b, link, preferred_element_type=F32) for link in links]
    for degree in range(3):
        rows = slice(LAT + degree * CH, LAT + (degree + 1) * CH)
        joined_ref[rows, :] = (weight * sums[degree]).astype(BF16)

    z3_ref[...] += jnp.dot(
        w_lat_ref[:, LAT:], joined_ref[LAT:, :], preferred_element_type=F32
    )
    energy = jnp.zeros((8, PAIRS), F32)
    cut_grad = jnp.zeros((8, PAIRS), F32)
    for start in range(0, LAT, ROWS):
        rows = pl.ds(start, ROWS)
        value, gate = silu_parts(z3_ref[rows, :])
        readout = w_out_ref[rows, :].astype(F32)
        readout = jnp.concatenate([readout, readout], axis=1)
        updated = (joined_ref[rows, :].astype(F32) + value * cut).astype(BF16).astype(F32)
        energy = energy + folded(readout * updated)
        cut_grad = cut_grad + folded(readout * value)
        dz_ref[rows, :] = (readout * cut * gate).astype(BF16)

    grad_ref[LAT:, :] = jnp.dot(w_lat_t_ref[LAT:, :], dz_ref[...], preferred_element_type=F32)
    grad_ref[0:LAT, :] = jnp.dot(w_lat_t_ref[0:LAT, :], dz_ref[...], preferred_element_type=F32)
    weight_grad = jnp.zeros_like(weight)
    passes = []
    for degree in range(3):
        inv_grad = grad_ref[LAT + degree * CH : LAT + (degree + 1) * CH, :]
        passed = (inv_grad * weight).astype(BF16)
        weight_grad = weight_grad + inv_grad * sums[degree]
        weight_grad = weight_grad + jnp.dot(passed, links[degree], preferred_element_type=F32)
        passes.append(passed)
    dlat_ref[...] = jnp.dot(
        w_env_t_ref[...], weight_grad.astype(BF16), preferred_element_type=F32
    )
    for start in range(0, LAT, ROWS):
        rows = pl.ds(start, ROWS)
        readout = w_out_ref[rows, :].astype(F32)
        readout = jnp.concatenate([readout, readout], axis=1)
        value, gate = silu_parts(z2_ref[rows, :])
        dlat = readout + grad_ref[rows, :] + dlat_ref[rows, :]
        cut_grad = cut_grad + folded(dlat * value)
        dz_ref[rows, :] = (dlat * cut * gate).astype(BF16)
    shape_grad = []
    for degree in (1, 2):
        passed = passes[degree]
        both = dot_tn(
            jnp.concatenate([weight_b, passed], axis=0),
            jnp.concatenate([passed, weight_b], axis=0),
        )
        both = both.astype(BF16) * same
        shape_grad.append(jnp.dot(shapes[degree - 1], both, preferred_element_type=F32))
    dlat_ref[...] = jnp.dot(w_hid_t_ref[...], dz_ref[...], preferred_element_type=F32)
    for start in range(0, LAT, ROWS):
        rows = pl.ds(start, ROWS)
        dz_ref[rows, :] = (dlat_ref[rows, :] * z1_ref[rows, :]).astype(BF16)
    feature_grad = jnp.dot(w_in_t_ref[...], dz_ref[...], preferred_element_type=F32)[0:8, :]

    cut_grad = column_sum(cut_grad + feature_grad * bessel)
    radius_grad = cut_grad * slope + cut * column_sum(feature_grad * bessel_slope)
    g1, g2, g3 = [shape_grad[0][i : i + 1] for i in range(3)]
    g4, g5, g6, g7, g8 = [shape_grad[1][i : i + 1] for i in range(5)]
    unit_grad = [
        ROOT3 * g1 + ROOT15 * (along_y * g4 + along_z * g7 + along_x * g8) - ROOT5 * along_x * g6,
        ROOT3 * g2 + ROOT15 * (along_x * g4 + along_z * g5 - along_y * g8) - ROOT5 * along_y * g6,
        ROOT3 * g3 + ROOT15 * (along_y * g5 + along_x * g7) + 2.0 * ROOT5 * along_z * g6,
    ]
    radial = sum(g * u for g, u in zip(unit_grad, unit))
    radius_grad = radius_grad - radial * inverse
    push = [g * inverse + radius_grad * u for g, u in zip(unit_grad, unit)]

    row = lax.broadcasted_iota(jnp.int32, (112, PAIRS), 0)
    axis = row & 3
    moved = jnp.where(axis == 0, push[0], jnp.where(axis == 1, push[1], push[2]))
    moved = jnp.where(axis == 3, 0.0, moved)
    spread = split_dot_nt(jnp.where((row >> 2) == slot, -moved, 0.0), hits_ref[0])
    home = split_dot_nt(moved[0:8], hits_ref[1])[0:4]
    spread = spread.reshape(28, 4, ATOMS)
    energy = column_sum(energy)
    energy = energy[:, 0:ATOMS] + energy[:, ATOMS:PAIRS]
    is_energy = lax.broadcasted_iota(jnp.int32, (4, ATOMS), 0) == 3
    blank = jnp.where(is_energy, energy, 0.0)
    out_ref[...] = jnp.broadcast_to(blank[None, None], out_ref.shape)
    for at_x in range(3):
        number = (place + (at_x + RING - 1)) & (RING - 1)
        for cell in range(9):
            block = spread[9 * at_x + cell]
            if 9 * at_x + cell == 13:
                block = block + home
            out_ref[number, cell] = block + blank


def pair_forces(*operands):
    vmem = pl.BlockSpec(memory_space=pltpu.VMEM)
    return pl.pallas_call(
        force_kernel,
        out_shape=jax.ShapeDtypeStruct((RING, 9, 4, ATOMS), F32),
        in_specs=[vmem] * 15,
        out_specs=vmem,
        scratch_shapes=[
            pltpu.VMEM((LAT, PAIRS), F32),
            pltpu.VMEM((LAT, PAIRS), F32),
            pltpu.VMEM((LAT, PAIRS), F32),
            pltpu.VMEM((LAT, PAIRS), BF16),
            pltpu.VMEM((LAT + 3 * CH, PAIRS), BF16),
            pltpu.VMEM((LAT + 3 * CH, PAIRS), F32),
            pltpu.VMEM((LAT, PAIRS), BF16),
            pltpu.VMEM((LAT, PAIRS), F32),
        ],
        compiler_params=pltpu.CompilerParams(vmem_limit_bytes=24 * 1024 * 1024),
        name="forces_of_pairs",
    )(*operands)


SMALL = pltpu.CompilerParams(vmem_limit_bytes=2 * 1024 * 1024)
AXES = ("gx", "gy", "gz")


def flat(at_x, at_y, chip, high):
    return ((at_x % RING) * RING + at_y) * RING + 2 * chip + high


NEAR = [
    [flat(2 * pair + i, at_y, chip, high) for i in range(2) for at_y in range(8) for high in range(2)]
    for pair in range(4)
    for chip in range(4)
]
FAR = [
    [flat(2 * pair + 1 + i, at_y, chip, high) for i in range(2) for chip in range(4)]
    for pair in range(4)
    for at_y in range(8)
    for high in range(2)
]


def body(coords, species, pair_ids, live_counts, w_two_in, w_two_hid, w_env, w_latent, w_out):
    ids = pair_ids[0, 0, 0]
    counts = live_counts[0, 0, 0]
    vmem = pl.BlockSpec(memory_space=pltpu.VMEM)
    smem = pl.BlockSpec(memory_space=pltpu.SMEM)
    packed = pl.pallas_call(
        pack_kernel,
        out_shape=jax.ShapeDtypeStruct((32, 4, ATOMS), F32),
        in_specs=[vmem],
        out_specs=vmem,
        compiler_params=SMALL,
        name="pack_frame",
    )(jnp.concatenate([coords[0, 0, 0], species[0, 0, 0].astype(F32)[None]], axis=0))
    near = lax.all_to_all(packed, AXES, 0, 0, axis_index_groups=NEAR)
    relayed = pl.pallas_call(
        relay_kernel,
        out_shape=jax.ShapeDtypeStruct((8, 6, 4, ATOMS), F32),
        in_specs=[vmem],
        out_specs=vmem,
        compiler_params=SMALL,
        name="relay_frames",
    )(near)
    far = lax.all_to_all(relayed, AXES, 0, 0, axis_index_groups=FAR)
    even, plane, odd = pl.pallas_call(
        pick_kernel,
        out_shape=(jax.ShapeDtypeStruct((9, 4, ATOMS), F32),) * 3,
        in_specs=[vmem] * 2,
        out_specs=(vmem,) * 3,
        compiler_params=SMALL,
        name="pick_planes",
    )(near, far)

    pairs, hits, same, readout = pl.pallas_call(
        prepare_kernel,
        out_shape=(
            jax.ShapeDtypeStruct((8, PAIRS), jnp.int32),
            jax.ShapeDtypeStruct((2, ATOMS, PAIRS), BF16),
            jax.ShapeDtypeStruct((PAIRS, PAIRS), BF16),
            jax.ShapeDtypeStruct((LAT, ATOMS), BF16),
        ),
        in_specs=[smem, vmem, vmem],
        out_specs=(vmem,) * 4,
        compiler_params=SMALL,
        name="prepare_pairs",
    )(counts, ids, w_out)
    w_in = jnp.pad(w_two_in, ((0, 0), (0, 4)))
    sent = pair_forces(
        pairs,
        hits,
        even,
        plane,
        odd,
        same,
        w_in,
        w_in.T,
        w_two_hid,
        w_two_hid.T,
        w_env,
        w_env.T,
        w_latent,
        w_latent.T,
        readout,
    )
    addressed = pl.pallas_call(
        address_kernel,
        out_shape=jax.ShapeDtypeStruct((RING * RING, 4, ATOMS), F32),
        in_specs=[vmem],
        out_specs=vmem,
        compiler_params=SMALL,
        name="address_plane",
    )(lax.all_to_all(sent, "gx", 0, 0))
    forces, energy = pl.pallas_call(
        finish_kernel,
        out_shape=(jax.ShapeDtypeStruct((3, 1, ATOMS), F32), jax.ShapeDtypeStruct((1,), F32)),
        in_specs=[vmem],
        out_specs=(vmem, smem),
        compiler_params=SMALL,
        name="finish",
    )(lax.all_to_all(addressed, ("gy", "gz"), 0, 0))
    return forces.reshape(1, 1, 1, 3, ATOMS), energy.reshape(())


def solution(mesh):
    in_specs = (
        P("gx", "gy", "gz", None, None),
        P("gx", "gy", "gz", None),
        P("gx", "gy", "gz", None, None),
        P("gx", "gy", "gz", None),
        P(),
        P(),
        P(),
        P(),
        P(),
    )
    out_specs = (P("gx", "gy", "gz", None, None), P())
    return jax.shard_map(body, mesh=mesh, in_specs=in_specs, out_specs=out_specs, check_vma=False)
```

```python
import math

import jax
import jax.numpy as jnp
from jax import lax
from jax.experimental import pallas as pl
from jax.experimental.pallas import tpu as pltpu
from jax.sharding import PartitionSpec as P

F32 = jnp.float32
BF16 = jnp.bfloat16
CUTOFF = 6.0
SOFTEN = 0.01
ENV_NORM = 0.25
EXTENT = (16.0, 16.0, 4.0)
ROOT3 = math.sqrt(3.0)
ROOT5 = math.sqrt(5.0)
ROOT15 = math.sqrt(15.0)
RING = 8
LAT = 512
CH = 64
PAIRS = 256
ATOMS = 128
ROWS = 64


def column_sum(block):
    return jnp.sum(block, axis=0, keepdims=True)


def folded(block):
    return jnp.sum(block.reshape(block.shape[0] // 8, 8, block.shape[1]), axis=0)


def silu_parts(z):
    gate = 0.5 * jnp.tanh(0.5 * z) + 0.5
    value = z * gate
    return value, gate + value * (1.0 - gate)


def dot_tn(left, right):
    return lax.dot_general(left, right, (((0,), (0,)), ((), ())), preferred_element_type=F32)


def split_dot_nt(block, other):
    dims = (((1,), (1,)), ((), ()))
    high = block.astype(BF16)
    low = (block - high.astype(F32)).astype(BF16)
    return lax.dot_general(high, other, dims, preferred_element_type=F32) + lax.dot_general(
        low, other, dims, preferred_element_type=F32
    )


def pack_kernel(frame_ref, out_ref):
    out_ref[...] = jnp.broadcast_to(frame_ref[...][None], out_ref.shape)


def place_of():
    at_z = lax.axis_index("gz")
    return lax.axis_index("gx"), lax.axis_index("gy"), at_z >> 1, at_z & 1


def back_place(at_x):
    turned = (at_x + (RING - 1)) & (RING - 1)
    return (turned & 1) + 2 * (turned >> 2)


def relay_kernel(near_ref, out_ref):
    at_x, at_y, chip, high = place_of()
    own, other = (at_x & 1) * 16, (1 - (at_x & 1)) * 16
    side = 1 - (at_x & 1)
    out_ref[...] = jnp.zeros(out_ref.shape, F32)
    chip_third = (chip + 5 - 2 * high) & 3
    for row in range(3):
        number = ((at_y + (RING - 1 + row)) & (RING - 1)) * 2
        for level in range(2):
            out_ref[(1 - side) * 4 + chip, 2 * row + level] = near_ref[own + number + level]
        for to in (side, 1 - side):
            out_ref[to * 4 + chip_third, row] = near_ref[own + number + 1 - high]
            out_ref[to * 4 + chip_third, 3 + row] = near_ref[other + number + 1 - high]


def pick_kernel(near_ref, far_ref, even_ref, level_ref, odd_ref):
    at_x, at_y, chip, high = place_of()
    own, other = (at_x & 1) * 16, (1 - (at_x & 1)) * 16
    side = 1 - (at_x & 1)
    chip_third = (chip + 3 + 2 * high) & 3
    for row in range(3):
        number = ((at_y + (RING - 1 + row)) & (RING - 1)) * 2
        for level in range(2):
            cell = 3 * row + 1 + level - high
            level_ref[cell] = near_ref[own + number + level]
            even_ref[cell] = near_ref[other + number + level]
            odd_ref[cell] = far_ref[(1 - side) * 4 + chip, 2 * row + level]
        cell = 3 * row + 2 * high
        level_ref[cell] = far_ref[side * 4 + chip_third, row]
        even_ref[cell] = far_ref[side * 4 + chip_third, 3 + row]
        odd_ref[cell] = far_ref[(1 - side) * 4 + chip_third, row]


def combine_kernel(received_ref, home_ref, out_ref):
    at_x, at_y, chip, high = place_of()
    own, other = (at_x & 1) * 16, (1 - (at_x & 1)) * 16
    back = back_place(at_x)
    beside = back ^ 1
    chip_third = (chip + 5 - 2 * high) & 3
    is_energy = lax.broadcasted_iota(jnp.int32, (4, ATOMS), 0) == 3

    def moved(member, cell):
        return jnp.where(is_energy, 0.0, received_ref[member, cell])

    total = received_ref[0, 0]
    for member in range(1, 16):
        total = total + received_ref[member, 0]
    blank = jnp.where(is_energy, total, 0.0)
    out_ref[...] = jnp.broadcast_to(blank[None], out_ref.shape)
    for row in range(3):
        number = ((at_y + (RING - 1 + row)) & (RING - 1)) * 2
        for level in range(2):
            cell = 2 * row + level
            mine = home_ref[cell] + moved(beside * 4 + chip, cell)
            out_ref[own + number + level] = blank + mine
            out_ref[other + number + level] = blank + home_ref[6 + cell]
        across = number + 1 - high
        third = moved(back * 4 + chip_third, row) + moved(beside * 4 + chip_third, row)
        out_ref[own + across] = out_ref[own + across] + third
        out_ref[other + across] = out_ref[other + across] + moved(back * 4 + chip_third, 3 + row)


def finish_kernel(received_ref, forces_ref, energy_ref):
    halves = []
    for start in (0, 16):
        total = received_ref[start]
        for member in range(start + 1, start + 16):
            total = total + received_ref[member]
        halves.append(total)
    total = halves[0] + halves[1]
    for axis in range(3):
        forces_ref[axis] = total[axis : axis + 1]
    energy_ref[0] = jnp.sum(total[3:4]) * (1.0 / (ATOMS * RING**3))


def prepare_kernel(counts_ref, ids_ref, w_out_ref, pairs_ref, hits_ref, same_ref, readout_ref):
    centre = ids_ref[0:1, :]
    neighbour = ids_ref[1:2, :]
    lane = lax.broadcasted_iota(jnp.int32, (1, PAIRS), 1)
    live = lane < jnp.where(lane < ATOMS, counts_ref[0], counts_ref[1] + ATOMS)
    rows = [centre, neighbour >> 7, neighbour & 127, live.astype(jnp.int32)]
    pairs_ref[...] = jnp.concatenate(rows + rows, axis=0)
    atom_row = lax.broadcasted_iota(jnp.int32, (ATOMS, PAIRS), 0)
    hits_ref[0] = jnp.where(atom_row == rows[2], 1.0, 0.0).astype(BF16)
    hits_ref[1] = jnp.where(atom_row == centre, 1.0, 0.0).astype(BF16)
    across = jnp.broadcast_to(centre.astype(F32), (PAIRS, PAIRS))
    same_ref[...] = jnp.where(across == across.T, ENV_NORM, 0.0).astype(BF16)
    readout_ref[...] = jnp.broadcast_to(w_out_ref[...].astype(F32), (ATOMS, LAT)).T.astype(BF16)


def force_kernel(
    pairs_ref,
    hits_ref,
    even_ref,
    level_ref,
    odd_ref,
    same_ref,
    w_in_ref,
    w_in_t_ref,
    w_hid_ref,
    w_hid_t_ref,
    w_env_ref,
    w_env_t_ref,
    w_lat_ref,
    w_lat_t_ref,
    w_out_ref,
    out_ref,
    home_ref,
    z1_ref,
    z2_ref,
    z3_ref,
    hidden_ref,
    joined_ref,
    grad_ref,
    dz_ref,
    dlat_ref,
    spread_ref,
):
    centre = pairs_ref[0:1, :]
    slot = pairs_ref[1:2, :]
    atom = pairs_ref[2:3, :]
    live = pairs_ref[3:4, :].astype(F32)
    step_x = (slot * 57) >> 9
    rest = slot - 9 * step_x
    step_y = (rest * 11) >> 5
    step_z = rest - 3 * step_y

    parity = lax.axis_index("gx") & 1
    near, own = [], []
    for half in range(2):
        lanes = slice(half * ATOMS, (half + 1) * ATOMS)
        pick = jnp.broadcast_to(atom[:, lanes], (4, ATOMS))
        slot_half = jnp.broadcast_to(slot[:, lanes], (4, ATOMS))
        total = jnp.zeros((4, ATOMS), F32)
        for slab, base in ((even_ref, 18 * (1 - parity)), (level_ref, 9), (odd_ref, 18 * parity)):
            for cell in range(9):
                rows = jnp.take_along_axis(slab[cell], pick, axis=1, mode="promise_in_bounds")
                total = jnp.where(slot_half == base + cell, rows, total)
        near.append(total)
        pick = jnp.broadcast_to(centre[:, lanes], (4, ATOMS))
        own.append(jnp.take_along_axis(level_ref[4], pick, axis=1, mode="promise_in_bounds"))
    near = jnp.concatenate(near, axis=1)
    own = jnp.concatenate(own, axis=1)
    delta = [
        near[axis : axis + 1, :]
        + (step - 1).astype(F32) * EXTENT[axis]
        - own[axis : axis + 1, :]
        for axis, step in enumerate((step_x, step_y, step_z))
    ]

    radius = jnp.sqrt(delta[0] * delta[0] + delta[1] * delta[1] + delta[2] * delta[2] + SOFTEN)
    inverse = 1.0 / radius
    ratio = radius * (1.0 / CUTOFF)
    inside = jnp.where(ratio < 1.0, live, 0.0)
    square = ratio * ratio
    fifth = square * square * ratio
    sixth = fifth * ratio
    cut = inside * (1.0 + sixth * (-28.0 + 48.0 * ratio - 21.0 * square))
    slope = inside * (-168.0 / CUTOFF) * fifth * (1.0 - ratio) * (1.0 - ratio)

    row8 = lax.broadcasted_iota(jnp.int32, (8, PAIRS), 0)
    order = (row8 + 1).astype(F32)
    turns = order * ratio
    whole = jnp.floor(turns + 0.5)
    sign = 1.0 - 2.0 * (whole.astype(jnp.int32) & 1).astype(F32)
    angle = (turns - whole) * math.pi
    angle2 = angle * angle
    sine = jnp.zeros_like(angle)
    for power in (11, 9, 7, 5, 3, 1):
        sine = sine * angle2 + (-1.0) ** (power // 2) / math.factorial(power)
    sine = sine * angle * sign
    cosine = jnp.zeros_like(angle)
    for power in (12, 10, 8, 6, 4, 2, 0):
        cosine = cosine * angle2 + (-1.0) ** (power // 2) / math.factorial(power)
    cosine = cosine * sign
    front = math.sqrt(2.0 / CUTOFF)
    bessel = front * sine * inverse
    bessel_slope = (front * math.pi / CUTOFF) * order * cosine * inverse - bessel * inverse

    kind_at = jnp.where(row8 < 2, own[3:4, :], near[3:4, :])
    kind = jnp.where((row8 < 4) & (kind_at == (row8 & 1).astype(F32)), 1.0, 0.0)
    features = jnp.concatenate([bessel * cut, kind], axis=0).astype(BF16)

    z1_ref[...] = jnp.dot(w_in_ref[...], features, preferred_element_type=F32)
    for start in range(0, LAT, ROWS):
        rows = pl.ds(start, ROWS)
        value, gate = silu_parts(z1_ref[rows, :])
        hidden_ref[rows, :] = value.astype(BF16)
        z1_ref[rows, :] = gate
    z2_ref[...] = jnp.dot(w_hid_ref[...], hidden_ref[...], preferred_element_type=F32)
    for start in range(0, LAT, ROWS):
        rows = pl.ds(start, ROWS)
        value, unused = silu_parts(z2_ref[rows, :])
        joined_ref[rows, :] = (value * cut).astype(BF16)

    unit = [part * inverse for part in delta]
    along_x, along_y, along_z = unit
    zero = jnp.zeros_like(along_x)
    first = [ROOT3 * along_x, ROOT3 * along_y, ROOT3 * along_z]
    second = [
        ROOT15 * along_x * along_y,
        ROOT15 * along_y * along_z,
        0.5 * ROOT5 * (2.0 * along_z * along_z - along_x * along_x - along_y * along_y),
        ROOT15 * along_x * along_z,
        0.5 * ROOT15 * (along_x * along_x - along_y * along_y),
    ]
    shapes = [
        jnp.concatenate(rows + [zero] * (16 - len(rows)), axis=0).astype(BF16)
        for rows in (first, second)
    ]
    same = same_ref[...]
    links = [same] + [dot_tn(rows, rows).astype(BF16) * same for rows in shapes]
    weight = jnp.dot(w_env_ref[...], joined_ref[0:LAT, :], preferred_element_type=F32)
    z3_ref[...] = jnp.dot(
        w_lat_ref[:, 0:LAT], joined_ref[0:LAT, :], preferred_element_type=F32
    )
    weight_b = weight.astype(BF16)
    sums = [jnp.dot(weight_b, link, preferred_element_type=F32) for link in links]
    for degree in range(3):
        rows = slice(LAT + degree * CH, LAT + (degree + 1) * CH)
        joined_ref[rows, :] = (weight * sums[degree]).astype(BF16)

    z3_ref[...] += jnp.dot(
        w_lat_ref[:, LAT:], joined_ref[LAT:, :], preferred_element_type=F32
    )
    energy = jnp.zeros((8, PAIRS), F32)
    cut_grad = jnp.zeros((8, PAIRS), F32)
    for start in range(0, LAT, ROWS):
        rows = pl.ds(start, ROWS)
        value, gate = silu_parts(z3_ref[rows, :])
        readout = w_out_ref[rows, :].astype(F32)
        readout = jnp.concatenate([readout, readout], axis=1)
        updated = (joined_ref[rows, :].astype(F32) + value * cut).astype(BF16).astype(F32)
        energy = energy + folded(readout * updated)
        cut_grad = cut_grad + folded(readout * value)
        dz_ref[rows, :] = (readout * cut * gate).astype(BF16)

    grad_ref[LAT:, :] = jnp.dot(w_lat_t_ref[LAT:, :], dz_ref[...], preferred_element_type=F32)
    grad_ref[0:LAT, :] = jnp.dot(w_lat_t_ref[0:LAT, :], dz_ref[...], preferred_element_type=F32)
    weight_grad = jnp.zeros_like(weight)
    passes = []
    for degree in range(3):
        inv_grad = grad_ref[LAT + degree * CH : LAT + (degree + 1) * CH, :]
        passed = (inv_grad * weight).astype(BF16)
        weight_grad = weight_grad + inv_grad * sums[degree]
        weight_grad = weight_grad + jnp.dot(passed, links[degree], preferred_element_type=F32)
        passes.append(passed)
    dlat_ref[...] = jnp.dot(
        w_env_t_ref[...], weight_grad.astype(BF16), preferred_element_type=F32
    )
    for start in range(0, LAT, ROWS):
        rows = pl.ds(start, ROWS)
        readout = w_out_ref[rows, :].astype(F32)
        readout = jnp.concatenate([readout, readout], axis=1)
        value, gate = silu_parts(z2_ref[rows, :])
        dlat = readout + grad_ref[rows, :] + dlat_ref[rows, :]
        cut_grad = cut_grad + folded(dlat * value)
        dz_ref[rows, :] = (dlat * cut * gate).astype(BF16)
    shape_grad = []
    for degree in (1, 2):
        passed = passes[degree]
        both = dot_tn(
            jnp.concatenate([weight_b, passed], axis=0),
            jnp.concatenate([passed, weight_b], axis=0),
        )
        both = both.astype(BF16) * same
        shape_grad.append(jnp.dot(shapes[degree - 1], both, preferred_element_type=F32))
    dlat_ref[...] = jnp.dot(w_hid_t_ref[...], dz_ref[...], preferred_element_type=F32)
    for start in range(0, LAT, ROWS):
        rows = pl.ds(start, ROWS)
        dz_ref[rows, :] = (dlat_ref[rows, :] * z1_ref[rows, :]).astype(BF16)
    feature_grad = jnp.dot(w_in_t_ref[...], dz_ref[...], preferred_element_type=F32)[0:8, :]

    cut_grad = column_sum(cut_grad + feature_grad * bessel)
    radius_grad = cut_grad * slope + cut * column_sum(feature_grad * bessel_slope)
    g1, g2, g3 = [shape_grad[0][i : i + 1] for i in range(3)]
    g4, g5, g6, g7, g8 = [shape_grad[1][i : i + 1] for i in range(5)]
    unit_grad = [
        ROOT3 * g1 + ROOT15 * (along_y * g4 + along_z * g7 + along_x * g8) - ROOT5 * along_x * g6,
        ROOT3 * g2 + ROOT15 * (along_x * g4 + along_z * g5 - along_y * g8) - ROOT5 * along_y * g6,
        ROOT3 * g3 + ROOT15 * (along_y * g5 + along_x * g7) + 2.0 * ROOT5 * along_z * g6,
    ]
    radial = sum(g * u for g, u in zip(unit_grad, unit))
    radius_grad = radius_grad - radial * inverse
    push = [g * inverse + radius_grad * u for g, u in zip(unit_grad, unit)]

    row = lax.broadcasted_iota(jnp.int32, (112, PAIRS), 0)
    axis = row & 3
    moved = jnp.where(axis == 0, push[0], jnp.where(axis == 1, push[1], push[2]))
    moved = jnp.where(axis == 3, 0.0, moved)
    spread = split_dot_nt(jnp.where((row >> 2) == slot, -moved, 0.0), hits_ref[0])
    home = split_dot_nt(moved[0:8], hits_ref[1])[0:4]
    spread_ref[...] = spread.reshape(28, 4, ATOMS)
    spread_ref[13] = spread_ref[13] + home
    energy = column_sum(energy)
    energy = energy[:, 0:ATOMS] + energy[:, ATOMS:PAIRS]
    is_energy = lax.broadcasted_iota(jnp.int32, (4, ATOMS), 0) == 3
    blank = jnp.where(is_energy, energy, 0.0)
    out_ref[...] = jnp.broadcast_to(blank[None, None], out_ref.shape)
    at_x, unused, chip, high = place_of()
    aligned, shifted = 18 * (1 - parity), 18 * parity
    back = back_place(at_x)
    beside = back ^ 1
    chip_third = (chip + 3 + 2 * high) & 3
    for row in range(3):
        for level in range(2):
            cell, slot_at = 2 * row + level, 3 * row + 1 + level - high
            home_ref[cell] = spread_ref[9 + slot_at]
            home_ref[6 + cell] = spread_ref[aligned + slot_at]
            out_ref[beside * 4 + chip, cell] = blank + spread_ref[shifted + slot_at]
        slot_at = 3 * row + 2 * high
        out_ref[back * 4 + chip_third, row] = blank + spread_ref[9 + slot_at]
        out_ref[back * 4 + chip_third, 3 + row] = blank + spread_ref[aligned + slot_at]
        out_ref[beside * 4 + chip_third, row] = blank + spread_ref[shifted + slot_at]


def pair_forces(*operands):
    vmem = pl.BlockSpec(memory_space=pltpu.VMEM)
    return pl.pallas_call(
        force_kernel,
        out_shape=(
            jax.ShapeDtypeStruct((16, 6, 4, ATOMS), F32),
            jax.ShapeDtypeStruct((12, 4, ATOMS), F32),
        ),
        in_specs=[vmem] * 15,
        out_specs=(vmem, vmem),
        scratch_shapes=[
            pltpu.VMEM((LAT, PAIRS), F32),
            pltpu.VMEM((LAT, PAIRS), F32),
            pltpu.VMEM((LAT, PAIRS), F32),
            pltpu.VMEM((LAT, PAIRS), BF16),
            pltpu.VMEM((LAT + 3 * CH, PAIRS), BF16),
            pltpu.VMEM((LAT + 3 * CH, PAIRS), F32),
            pltpu.VMEM((LAT, PAIRS), BF16),
            pltpu.VMEM((LAT, PAIRS), F32),
            pltpu.VMEM((28, 4, ATOMS), F32),
        ],
        compiler_params=pltpu.CompilerParams(vmem_limit_bytes=24 * 1024 * 1024),
        name="forces_of_pairs",
    )(*operands)


SMALL = pltpu.CompilerParams(vmem_limit_bytes=2 * 1024 * 1024)
AXES = ("gx", "gy", "gz")


def flat(at_x, at_y, chip, high):
    return ((at_x % RING) * RING + at_y) * RING + 2 * chip + high


NEAR = [
    [flat(2 * pair + i, at_y, chip, high) for i in range(2) for at_y in range(8) for high in range(2)]
    for pair in range(4)
    for chip in range(4)
]
FAR = [
    [flat(2 * pair + 1 + i, at_y, chip, high) for i in range(2) for chip in range(4)]
    for pair in range(4)
    for at_y in range(8)
    for high in range(2)
]
BACK = [
    [flat(base + i, at_y, chip, high) for i in (0, 1, 4, 5) for chip in range(4)]
    for base in (1, 3)
    for at_y in range(8)
    for high in range(2)
]


def body(coords, species, pair_ids, live_counts, w_two_in, w_two_hid, w_env, w_latent, w_out):
    ids = pair_ids[0, 0, 0]
    counts = live_counts[0, 0, 0]
    vmem = pl.BlockSpec(memory_space=pltpu.VMEM)
    smem = pl.BlockSpec(memory_space=pltpu.SMEM)
    packed = pl.pallas_call(
        pack_kernel,
        out_shape=jax.ShapeDtypeStruct((32, 4, ATOMS), F32),
        in_specs=[vmem],
        out_specs=vmem,
        compiler_params=SMALL,
        name="pack_frame",
    )(jnp.concatenate([coords[0, 0, 0], species[0, 0, 0].astype(F32)[None]], axis=0))
    near = lax.all_to_all(packed, AXES, 0, 0, axis_index_groups=NEAR)
    relayed = pl.pallas_call(
        relay_kernel,
        out_shape=jax.ShapeDtypeStruct((8, 6, 4, ATOMS), F32),
        in_specs=[vmem],
        out_specs=vmem,
        compiler_params=SMALL,
        name="relay_frames",
    )(near)
    far = lax.all_to_all(relayed, AXES, 0, 0, axis_index_groups=FAR)
    even, plane, odd = pl.pallas_call(
        pick_kernel,
        out_shape=(jax.ShapeDtypeStruct((9, 4, ATOMS), F32),) * 3,
        in_specs=[vmem] * 2,
        out_specs=(vmem,) * 3,
        compiler_params=SMALL,
        name="pick_planes",
    )(near, far)

    pairs, hits, same, readout = pl.pallas_call(
        prepare_kernel,
        out_shape=(
            jax.ShapeDtypeStruct((8, PAIRS), jnp.int32),
            jax.ShapeDtypeStruct((2, ATOMS, PAIRS), BF16),
            jax.ShapeDtypeStruct((PAIRS, PAIRS), BF16),
            jax.ShapeDtypeStruct((LAT, ATOMS), BF16),
        ),
        in_specs=[smem, vmem, vmem],
        out_specs=(vmem,) * 4,
        compiler_params=SMALL,
        name="prepare_pairs",
    )(counts, ids, w_out)
    w_in = jnp.pad(w_two_in, ((0, 0), (0, 4)))
    sent, home = pair_forces(
        pairs,
        hits,
        even,
        plane,
        odd,
        same,
        w_in,
        w_in.T,
        w_two_hid,
        w_two_hid.T,
        w_env,
        w_env.T,
        w_latent,
        w_latent.T,
        readout,
    )
    combined = pl.pallas_call(
        combine_kernel,
        out_shape=jax.ShapeDtypeStruct((32, 4, ATOMS), F32),
        in_specs=[vmem] * 2,
        out_specs=vmem,
        compiler_params=SMALL,
        name="combine_forces",
    )(lax.all_to_all(sent, AXES, 0, 0, axis_index_groups=BACK), home)
    forces, energy = pl.pallas_call(
        finish_kernel,
        out_shape=(jax.ShapeDtypeStruct((3, 1, ATOMS), F32), jax.ShapeDtypeStruct((1,), F32)),
        in_specs=[vmem],
        out_specs=(vmem, smem),
        compiler_params=SMALL,
        name="finish",
    )(lax.all_to_all(combined, AXES, 0, 0, axis_index_groups=NEAR))
    return forces.reshape(1, 1, 1, 3, ATOMS), energy.reshape(())


def solution(mesh):
    in_specs = (
        P("gx", "gy", "gz", None, None),
        P("gx", "gy", "gz", None),
        P("gx", "gy", "gz", None, None),
        P("gx", "gy", "gz", None),
        P(),
        P(),
        P(),
        P(),
        P(),
    )
    out_specs = (P("gx", "gy", "gz", None, None), P())
    return jax.shard_map(body, mesh=mesh, in_specs=in_specs, out_specs=out_specs, check_vma=False)
```

```python
import math

import jax
import jax.numpy as jnp
from jax import lax
from jax.experimental import pallas as pl
from jax.experimental.pallas import tpu as pltpu
from jax.sharding import PartitionSpec as P

F32 = jnp.float32
BF16 = jnp.bfloat16
CUTOFF = 6.0
SOFTEN = 0.01
ENV_NORM = 0.25
EXTENT = (16.0, 16.0, 4.0)
ROOT3 = math.sqrt(3.0)
ROOT5 = math.sqrt(5.0)
ROOT15 = math.sqrt(15.0)
RING = 8
LAT = 512
CH = 64
PAIRS = 256
ATOMS = 128
ROWS = 128


def column_sum(block):
    return jnp.sum(block, axis=0, keepdims=True)


def folded(block):
    return jnp.sum(block.reshape(block.shape[0] // 8, 8, block.shape[1]), axis=0)


def silu_parts(z):
    gate = 0.5 * jnp.tanh(0.5 * z) + 0.5
    value = z * gate
    return value, gate + value * (1.0 - gate)


def dot_tn(left, right):
    return lax.dot_general(left, right, (((0,), (0,)), ((), ())), preferred_element_type=F32)


def split_dot_nt(block, other):
    dims = (((1,), (1,)), ((), ()))
    high = block.astype(BF16)
    low = (block - high.astype(F32)).astype(BF16)
    return lax.dot_general(high, other, dims, preferred_element_type=F32) + lax.dot_general(
        low, other, dims, preferred_element_type=F32
    )


def pack_kernel(frame_ref, out_ref):
    out_ref[...] = jnp.broadcast_to(frame_ref[...][None], out_ref.shape)


def place_of():
    at_z = lax.axis_index("gz")
    return lax.axis_index("gx"), lax.axis_index("gy"), at_z >> 1, at_z & 1


def back_place(at_x):
    turned = (at_x + (RING - 1)) & (RING - 1)
    return (turned & 1) + 2 * (turned >> 2)


def relay_kernel(near_ref, out_ref):
    at_x, at_y, chip, high = place_of()
    own, other = (at_x & 1) * 16, (1 - (at_x & 1)) * 16
    side = 1 - (at_x & 1)
    out_ref[...] = jnp.zeros(out_ref.shape, F32)
    chip_third = (chip + 5 - 2 * high) & 3
    for row in range(3):
        number = ((at_y + (RING - 1 + row)) & (RING - 1)) * 2
        for level in range(2):
            out_ref[(1 - side) * 4 + chip, 2 * row + level] = near_ref[own + number + level]
        for to in (side, 1 - side):
            out_ref[to * 4 + chip_third, row] = near_ref[own + number + 1 - high]
            out_ref[to * 4 + chip_third, 3 + row] = near_ref[other + number + 1 - high]


def pick_kernel(near_ref, far_ref, even_ref, level_ref, odd_ref):
    at_x, at_y, chip, high = place_of()
    own, other = (at_x & 1) * 16, (1 - (at_x & 1)) * 16
    side = 1 - (at_x & 1)
    chip_third = (chip + 3 + 2 * high) & 3
    for row in range(3):
        number = ((at_y + (RING - 1 + row)) & (RING - 1)) * 2
        for level in range(2):
            cell = 3 * row + 1 + level - high
            level_ref[cell] = near_ref[own + number + level]
            even_ref[cell] = near_ref[other + number + level]
            odd_ref[cell] = far_ref[(1 - side) * 4 + chip, 2 * row + level]
        cell = 3 * row + 2 * high
        level_ref[cell] = far_ref[side * 4 + chip_third, row]
        even_ref[cell] = far_ref[side * 4 + chip_third, 3 + row]
        odd_ref[cell] = far_ref[(1 - side) * 4 + chip_third, row]


def combine_kernel(received_ref, home_ref, out_ref):
    at_x, at_y, chip, high = place_of()
    own, other = (at_x & 1) * 16, (1 - (at_x & 1)) * 16
    back = back_place(at_x)
    beside = back ^ 1
    chip_third = (chip + 5 - 2 * high) & 3
    is_energy = lax.broadcasted_iota(jnp.int32, (4, ATOMS), 0) == 3

    def moved(member, cell):
        return jnp.where(is_energy, 0.0, received_ref[member, cell])

    total = received_ref[0, 0]
    for member in range(1, 16):
        total = total + received_ref[member, 0]
    blank = jnp.where(is_energy, total, 0.0)
    out_ref[...] = jnp.broadcast_to(blank[None], out_ref.shape)
    for row in range(3):
        number = ((at_y + (RING - 1 + row)) & (RING - 1)) * 2
        for level in range(2):
            cell = 2 * row + level
            mine = home_ref[cell] + moved(beside * 4 + chip, cell)
            out_ref[own + number + level] = blank + mine
            out_ref[other + number + level] = blank + home_ref[6 + cell]
        across = number + 1 - high
        third = moved(back * 4 + chip_third, row) + moved(beside * 4 + chip_third, row)
        out_ref[own + across] = out_ref[own + across] + third
        out_ref[other + across] = out_ref[other + across] + moved(back * 4 + chip_third, 3 + row)


def finish_kernel(received_ref, forces_ref, energy_ref):
    halves = []
    for start in (0, 16):
        total = received_ref[start]
        for member in range(start + 1, start + 16):
            total = total + received_ref[member]
        halves.append(total)
    total = halves[0] + halves[1]
    for axis in range(3):
        forces_ref[axis] = total[axis : axis + 1]
    energy_ref[0] = jnp.sum(total[3:4]) * (1.0 / (ATOMS * RING**3))


def prepare_kernel(counts_ref, ids_ref, w_out_ref, pairs_ref, hits_ref, same_ref, readout_ref):
    centre = ids_ref[0:1, :]
    neighbour = ids_ref[1:2, :]
    lane = lax.broadcasted_iota(jnp.int32, (1, PAIRS), 1)
    live = lane < jnp.where(lane < ATOMS, counts_ref[0], counts_ref[1] + ATOMS)
    rows = [centre, neighbour >> 7, neighbour & 127, live.astype(jnp.int32)]
    pairs_ref[...] = jnp.concatenate(rows + rows, axis=0)
    atom_row = lax.broadcasted_iota(jnp.int32, (ATOMS, PAIRS), 0)
    hits_ref[0] = jnp.where(atom_row == rows[2], 1.0, 0.0).astype(BF16)
    hits_ref[1] = jnp.where(atom_row == centre, 1.0, 0.0).astype(BF16)
    across = jnp.broadcast_to(centre.astype(F32), (PAIRS, PAIRS))
    same_ref[...] = jnp.where(across == across.T, ENV_NORM, 0.0).astype(BF16)
    readout_ref[...] = jnp.broadcast_to(w_out_ref[...].astype(F32), (ATOMS, LAT)).T.astype(BF16)


def force_kernel(
    pairs_ref,
    hits_ref,
    even_ref,
    level_ref,
    odd_ref,
    same_ref,
    w_in_ref,
    w_in_t_ref,
    w_hid_ref,
    w_hid_t_ref,
    w_env_ref,
    w_env_t_ref,
    w_lat_ref,
    w_lat_t_ref,
    w_out_ref,
    out_ref,
    home_ref,
    z1_ref,
    z2_ref,
    z3_ref,
    hidden_ref,
    joined_ref,
    grad_ref,
    dz_ref,
    dlat_ref,
    spread_ref,
):
    centre = pairs_ref[0:1, :]
    slot = pairs_ref[1:2, :]
    atom = pairs_ref[2:3, :]
    live = pairs_ref[3:4, :].astype(F32)
    step_x = (slot * 57) >> 9
    rest = slot - 9 * step_x
    step_y = (rest * 11) >> 5
    step_z = rest - 3 * step_y

    parity = lax.axis_index("gx") & 1
    near, own = [], []
    for half in range(2):
        lanes = slice(half * ATOMS, (half + 1) * ATOMS)
        pick = jnp.broadcast_to(atom[:, lanes], (4, ATOMS))
        slot_half = jnp.broadcast_to(slot[:, lanes], (4, ATOMS))
        total = jnp.zeros((4, ATOMS), F32)
        for slab, base in ((even_ref, 18 * (1 - parity)), (level_ref, 9), (odd_ref, 18 * parity)):
            for cell in range(9):
                rows = jnp.take_along_axis(slab[cell], pick, axis=1, mode="promise_in_bounds")
                total = jnp.where(slot_half == base + cell, rows, total)
        near.append(total)
        pick = jnp.broadcast_to(centre[:, lanes], (4, ATOMS))
        own.append(jnp.take_along_axis(level_ref[4], pick, axis=1, mode="promise_in_bounds"))
    near = jnp.concatenate(near, axis=1)
    own = jnp.concatenate(own, axis=1)
    delta = [
        near[axis : axis + 1, :]
        + (step - 1).astype(F32) * EXTENT[axis]
        - own[axis : axis + 1, :]
        for axis, step in enumerate((step_x, step_y, step_z))
    ]

    radius = jnp.sqrt(delta[0] * delta[0] + delta[1] * delta[1] + delta[2] * delta[2] + SOFTEN)
    inverse = 1.0 / radius
    ratio = radius * (1.0 / CUTOFF)
    inside = jnp.where(ratio < 1.0, live, 0.0)
    square = ratio * ratio
    fifth = square * square * ratio
    sixth = fifth * ratio
    cut = inside * (1.0 + sixth * (-28.0 + 48.0 * ratio - 21.0 * square))
    slope = inside * (-168.0 / CUTOFF) * fifth * (1.0 - ratio) * (1.0 - ratio)

    row8 = lax.broadcasted_iota(jnp.int32, (8, PAIRS), 0)
    order = (row8 + 1).astype(F32)
    turns = order * ratio
    whole = jnp.floor(turns + 0.5)
    sign = 1.0 - 2.0 * (whole.astype(jnp.int32) & 1).astype(F32)
    angle = (turns - whole) * math.pi
    angle2 = angle * angle
    sine = jnp.zeros_like(angle)
    for power in (11, 9, 7, 5, 3, 1):
        sine = sine * angle2 + (-1.0) ** (power // 2) / math.factorial(power)
    sine = sine * angle * sign
    cosine = jnp.zeros_like(angle)
    for power in (12, 10, 8, 6, 4, 2, 0):
        cosine = cosine * angle2 + (-1.0) ** (power // 2) / math.factorial(power)
    cosine = cosine * sign
    front = math.sqrt(2.0 / CUTOFF)
    bessel = front * sine * inverse
    bessel_slope = (front * math.pi / CUTOFF) * order * cosine * inverse - bessel * inverse

    kind_at = jnp.where(row8 < 2, own[3:4, :], near[3:4, :])
    kind = jnp.where((row8 < 4) & (kind_at == (row8 & 1).astype(F32)), 1.0, 0.0)
    features = jnp.concatenate([bessel * cut, kind], axis=0).astype(BF16)

    for start in range(0, LAT, ROWS):
        rows = pl.ds(start, ROWS)
        value, gate = silu_parts(
            jnp.dot(w_in_ref[rows, :], features, preferred_element_type=F32)
        )
        hidden_ref[rows, :] = value.astype(BF16)
        z1_ref[rows, :] = gate
    for start in range(0, LAT, ROWS):
        rows = pl.ds(start, ROWS)
        z2 = jnp.dot(w_hid_ref[rows, :], hidden_ref[...], preferred_element_type=F32)
        z2_ref[rows, :] = z2
        value, unused = silu_parts(z2)
        joined_ref[rows, :] = (value * cut).astype(BF16)

    unit = [part * inverse for part in delta]
    along_x, along_y, along_z = unit
    zero = jnp.zeros_like(along_x)
    first = [ROOT3 * along_x, ROOT3 * along_y, ROOT3 * along_z]
    second = [
        ROOT15 * along_x * along_y,
        ROOT15 * along_y * along_z,
        0.5 * ROOT5 * (2.0 * along_z * along_z - along_x * along_x - along_y * along_y),
        ROOT15 * along_x * along_z,
        0.5 * ROOT15 * (along_x * along_x - along_y * along_y),
    ]
    shapes = [
        jnp.concatenate(rows + [zero] * (16 - len(rows)), axis=0).astype(BF16)
        for rows in (first, second)
    ]
    same = same_ref[...]
    links = [same] + [dot_tn(rows, rows).astype(BF16) * same for rows in shapes]
    weight = jnp.dot(w_env_ref[...], joined_ref[0:LAT, :], preferred_element_type=F32)
    z3_ref[...] = jnp.dot(
        w_lat_ref[:, 0:LAT], joined_ref[0:LAT, :], preferred_element_type=F32
    )
    weight_b = weight.astype(BF16)
    sums = [jnp.dot(weight_b, link, preferred_element_type=F32) for link in links]
    for degree in range(3):
        rows = slice(LAT + degree * CH, LAT + (degree + 1) * CH)
        joined_ref[rows, :] = (weight * sums[degree]).astype(BF16)

    z3_ref[...] += jnp.dot(
        w_lat_ref[:, LAT:], joined_ref[LAT:, :], preferred_element_type=F32
    )
    energy = jnp.zeros((8, PAIRS), F32)
    cut_grad = jnp.zeros((8, PAIRS), F32)
    for start in range(0, LAT, ROWS):
        rows = pl.ds(start, ROWS)
        value, gate = silu_parts(z3_ref[rows, :])
        readout = w_out_ref[rows, :].astype(F32)
        readout = jnp.concatenate([readout, readout], axis=1)
        updated = (joined_ref[rows, :].astype(F32) + value * cut).astype(BF16).astype(F32)
        energy = energy + folded(readout * updated)
        cut_grad = cut_grad + folded(readout * value)
        dz_ref[rows, :] = (readout * cut * gate).astype(BF16)

    grad_ref[LAT:, :] = jnp.dot(w_lat_t_ref[LAT:, :], dz_ref[...], preferred_element_type=F32)
    grad_ref[0:LAT, :] = jnp.dot(w_lat_t_ref[0:LAT, :], dz_ref[...], preferred_element_type=F32)
    weight_grad = jnp.zeros_like(weight)
    passes = []
    for degree in range(3):
        inv_grad = grad_ref[LAT + degree * CH : LAT + (degree + 1) * CH, :]
        passed = (inv_grad * weight).astype(BF16)
        weight_grad = weight_grad + inv_grad * sums[degree]
        weight_grad = weight_grad + jnp.dot(passed, links[degree], preferred_element_type=F32)
        passes.append(passed)
    dlat_ref[...] = jnp.dot(
        w_env_t_ref[...], weight_grad.astype(BF16), preferred_element_type=F32
    )
    for start in range(0, LAT, ROWS):
        rows = pl.ds(start, ROWS)
        readout = w_out_ref[rows, :].astype(F32)
        readout = jnp.concatenate([readout, readout], axis=1)
        value, gate = silu_parts(z2_ref[rows, :])
        dlat = readout + grad_ref[rows, :] + dlat_ref[rows, :]
        cut_grad = cut_grad + folded(dlat * value)
        dz_ref[rows, :] = (dlat * cut * gate).astype(BF16)
    shape_grad = []
    for degree in (1, 2):
        passed = passes[degree]
        both = dot_tn(
            jnp.concatenate([weight_b, passed], axis=0),
            jnp.concatenate([passed, weight_b], axis=0),
        )
        both = both.astype(BF16) * same
        shape_grad.append(jnp.dot(shapes[degree - 1], both, preferred_element_type=F32))
    for start in range(0, LAT, ROWS):
        rows = pl.ds(start, ROWS)
        hidden_grad = jnp.dot(w_hid_t_ref[rows, :], dz_ref[...], preferred_element_type=F32)
        hidden_ref[rows, :] = (hidden_grad * z1_ref[rows, :]).astype(BF16)
    feature_grad = jnp.dot(w_in_t_ref[...], hidden_ref[...], preferred_element_type=F32)[0:8, :]

    cut_grad = column_sum(cut_grad + feature_grad * bessel)
    radius_grad = cut_grad * slope + cut * column_sum(feature_grad * bessel_slope)
    g1, g2, g3 = [shape_grad[0][i : i + 1] for i in range(3)]
    g4, g5, g6, g7, g8 = [shape_grad[1][i : i + 1] for i in range(5)]
    unit_grad = [
        ROOT3 * g1 + ROOT15 * (along_y * g4 + along_z * g7 + along_x * g8) - ROOT5 * along_x * g6,
        ROOT3 * g2 + ROOT15 * (along_x * g4 + along_z * g5 - along_y * g8) - ROOT5 * along_y * g6,
        ROOT3 * g3 + ROOT15 * (along_y * g5 + along_x * g7) + 2.0 * ROOT5 * along_z * g6,
    ]
    radial = sum(g * u for g, u in zip(unit_grad, unit))
    radius_grad = radius_grad - radial * inverse
    push = [g * inverse + radius_grad * u for g, u in zip(unit_grad, unit)]

    row = lax.broadcasted_iota(jnp.int32, (112, PAIRS), 0)
    axis = row & 3
    moved = jnp.where(axis == 0, push[0], jnp.where(axis == 1, push[1], push[2]))
    moved = jnp.where(axis == 3, 0.0, moved)
    spread = split_dot_nt(jnp.where((row >> 2) == slot, -moved, 0.0), hits_ref[0])
    home = split_dot_nt(moved[0:8], hits_ref[1])[0:4]
    spread_ref[...] = spread.reshape(28, 4, ATOMS)
    spread_ref[13] = spread_ref[13] + home
    energy = column_sum(energy)
    energy = energy[:, 0:ATOMS] + energy[:, ATOMS:PAIRS]
    is_energy = lax.broadcasted_iota(jnp.int32, (4, ATOMS), 0) == 3
    blank = jnp.where(is_energy, energy, 0.0)
    out_ref[...] = jnp.broadcast_to(blank[None, None], out_ref.shape)
    at_x, unused, chip, high = place_of()
    aligned, shifted = 18 * (1 - parity), 18 * parity
    back = back_place(at_x)
    beside = back ^ 1
    chip_third = (chip + 3 + 2 * high) & 3
    for row in range(3):
        for level in range(2):
            cell, slot_at = 2 * row + level, 3 * row + 1 + level - high
            home_ref[cell] = spread_ref[9 + slot_at]
            home_ref[6 + cell] = spread_ref[aligned + slot_at]
            out_ref[beside * 4 + chip, cell] = blank + spread_ref[shifted + slot_at]
        slot_at = 3 * row + 2 * high
        out_ref[back * 4 + chip_third, row] = blank + spread_ref[9 + slot_at]
        out_ref[back * 4 + chip_third, 3 + row] = blank + spread_ref[aligned + slot_at]
        out_ref[beside * 4 + chip_third, row] = blank + spread_ref[shifted + slot_at]


def pair_forces(*operands):
    vmem = pl.BlockSpec(memory_space=pltpu.VMEM)
    return pl.pallas_call(
        force_kernel,
        out_shape=(
            jax.ShapeDtypeStruct((16, 6, 4, ATOMS), F32),
            jax.ShapeDtypeStruct((12, 4, ATOMS), F32),
        ),
        in_specs=[vmem] * 15,
        out_specs=(vmem, vmem),
        scratch_shapes=[
            pltpu.VMEM((LAT, PAIRS), F32),
            pltpu.VMEM((LAT, PAIRS), F32),
            pltpu.VMEM((LAT, PAIRS), F32),
            pltpu.VMEM((LAT, PAIRS), BF16),
            pltpu.VMEM((LAT + 3 * CH, PAIRS), BF16),
            pltpu.VMEM((LAT + 3 * CH, PAIRS), F32),
            pltpu.VMEM((LAT, PAIRS), BF16),
            pltpu.VMEM((LAT, PAIRS), F32),
            pltpu.VMEM((28, 4, ATOMS), F32),
        ],
        compiler_params=pltpu.CompilerParams(vmem_limit_bytes=24 * 1024 * 1024),
        name="forces_of_pairs",
    )(*operands)


SMALL = pltpu.CompilerParams(vmem_limit_bytes=2 * 1024 * 1024)
AXES = ("gx", "gy", "gz")


def flat(at_x, at_y, chip, high):
    return ((at_x % RING) * RING + at_y) * RING + 2 * chip + high


NEAR = [
    [flat(2 * pair + i, at_y, chip, high) for i in range(2) for at_y in range(8) for high in range(2)]
    for pair in range(4)
    for chip in range(4)
]
FAR = [
    [flat(2 * pair + 1 + i, at_y, chip, high) for i in range(2) for chip in range(4)]
    for pair in range(4)
    for at_y in range(8)
    for high in range(2)
]
BACK = [
    [flat(base + i, at_y, chip, high) for i in (0, 1, 4, 5) for chip in range(4)]
    for base in (1, 3)
    for at_y in range(8)
    for high in range(2)
]


def body(coords, species, pair_ids, live_counts, w_two_in, w_two_hid, w_env, w_latent, w_out):
    ids = pair_ids[0, 0, 0]
    counts = live_counts[0, 0, 0]
    vmem = pl.BlockSpec(memory_space=pltpu.VMEM)
    smem = pl.BlockSpec(memory_space=pltpu.SMEM)
    packed = pl.pallas_call(
        pack_kernel,
        out_shape=jax.ShapeDtypeStruct((32, 4, ATOMS), F32),
        in_specs=[vmem],
        out_specs=vmem,
        compiler_params=SMALL,
        name="pack_frame",
    )(jnp.concatenate([coords[0, 0, 0], species[0, 0, 0].astype(F32)[None]], axis=0))
    near = lax.all_to_all(packed, AXES, 0, 0, axis_index_groups=NEAR)
    relayed = pl.pallas_call(
        relay_kernel,
        out_shape=jax.ShapeDtypeStruct((8, 6, 4, ATOMS), F32),
        in_specs=[vmem],
        out_specs=vmem,
        compiler_params=SMALL,
        name="relay_frames",
    )(near)
    far = lax.all_to_all(relayed, AXES, 0, 0, axis_index_groups=FAR)
    even, plane, odd = pl.pallas_call(
        pick_kernel,
        out_shape=(jax.ShapeDtypeStruct((9, 4, ATOMS), F32),) * 3,
        in_specs=[vmem] * 2,
        out_specs=(vmem,) * 3,
        compiler_params=SMALL,
        name="pick_planes",
    )(near, far)

    pairs, hits, same, readout = pl.pallas_call(
        prepare_kernel,
        out_shape=(
            jax.ShapeDtypeStruct((8, PAIRS), jnp.int32),
            jax.ShapeDtypeStruct((2, ATOMS, PAIRS), BF16),
            jax.ShapeDtypeStruct((PAIRS, PAIRS), BF16),
            jax.ShapeDtypeStruct((LAT, ATOMS), BF16),
        ),
        in_specs=[smem, vmem, vmem],
        out_specs=(vmem,) * 4,
        compiler_params=SMALL,
        name="prepare_pairs",
    )(counts, ids, w_out)
    w_in = jnp.pad(w_two_in, ((0, 0), (0, 4)))
    sent, home = pair_forces(
        pairs,
        hits,
        even,
        plane,
        odd,
        same,
        w_in,
        w_in.T,
        w_two_hid,
        w_two_hid.T,
        w_env,
        w_env.T,
        w_latent,
        w_latent.T,
        readout,
    )
    combined = pl.pallas_call(
        combine_kernel,
        out_shape=jax.ShapeDtypeStruct((32, 4, ATOMS), F32),
        in_specs=[vmem] * 2,
        out_specs=vmem,
        compiler_params=SMALL,
        name="combine_forces",
    )(lax.all_to_all(sent, AXES, 0, 0, axis_index_groups=BACK), home)
    forces, energy = pl.pallas_call(
        finish_kernel,
        out_shape=(jax.ShapeDtypeStruct((3, 1, ATOMS), F32), jax.ShapeDtypeStruct((1,), F32)),
        in_specs=[vmem],
        out_specs=(vmem, smem),
        compiler_params=SMALL,
        name="finish",
    )(lax.all_to_all(combined, AXES, 0, 0, axis_index_groups=NEAR))
    return forces.reshape(1, 1, 1, 3, ATOMS), energy.reshape(())


def solution(mesh):
    in_specs = (
        P("gx", "gy", "gz", None, None),
        P("gx", "gy", "gz", None),
        P("gx", "gy", "gz", None, None),
        P("gx", "gy", "gz", None),
        P(),
        P(),
        P(),
        P(),
        P(),
    )
    out_specs = (P("gx", "gy", "gz", None, None), P())
    return jax.shard_map(body, mesh=mesh, in_specs=in_specs, out_specs=out_specs, check_vma=False)
```

```python
import math

import jax
import jax.numpy as jnp
from jax import lax
from jax.experimental import pallas as pl
from jax.experimental.pallas import tpu as pltpu
from jax.sharding import PartitionSpec as P

F32 = jnp.float32
BF16 = jnp.bfloat16
CUTOFF = 6.0
SOFTEN = 0.01
ENV_NORM = 0.25
EXTENT = (16.0, 16.0, 4.0)
ROOT3 = math.sqrt(3.0)
ROOT5 = math.sqrt(5.0)
ROOT15 = math.sqrt(15.0)
RING = 8
LAT = 512
CH = 64
PAIRS = 256
ATOMS = 128
ROWS = 128


def column_sum(block):
    return jnp.sum(block, axis=0, keepdims=True)


def folded(block):
    return jnp.sum(block.reshape(block.shape[0] // 8, 8, block.shape[1]), axis=0)


def silu_parts(z):
    gate = 0.5 * jnp.tanh(0.5 * z) + 0.5
    value = z * gate
    return value, gate + value * (1.0 - gate)


def dot_tn(left, right):
    return lax.dot_general(left, right, (((0,), (0,)), ((), ())), preferred_element_type=F32)


def split_dot_nt(block, other):
    dims = (((1,), (1,)), ((), ()))
    high = block.astype(BF16)
    low = (block - high.astype(F32)).astype(BF16)
    return lax.dot_general(high, other, dims, preferred_element_type=F32) + lax.dot_general(
        low, other, dims, preferred_element_type=F32
    )


def pack_kernel(frame_ref, out_ref):
    out_ref[...] = jnp.broadcast_to(frame_ref[...][None], out_ref.shape)


def place_of():
    at_z = lax.axis_index("gz")
    return lax.axis_index("gx"), lax.axis_index("gy"), at_z >> 1, at_z & 1


def back_place(at_x):
    turned = (at_x + (RING - 1)) & (RING - 1)
    low, high = turned & 1, turned >> 2
    return 2 * high + low * (3 - 4 * high)


def relay_kernel(near_ref, out_ref):
    at_x, at_y, chip, high = place_of()
    own, other = (at_x & 1) * 16, (1 - (at_x & 1)) * 16
    side = 1 - (at_x & 1)
    out_ref[...] = jnp.zeros(out_ref.shape, F32)
    chip_third = (chip + 5 - 2 * high) & 3
    for row in range(3):
        number = ((at_y + (RING - 1 + row)) & (RING - 1)) * 2
        for level in range(2):
            out_ref[(1 - side) * 4 + chip, 2 * row + level] = near_ref[own + number + level]
        for to in (side, 1 - side):
            out_ref[to * 4 + chip_third, row] = near_ref[own + number + 1 - high]
            out_ref[to * 4 + chip_third, 3 + row] = near_ref[other + number + 1 - high]


def pick_kernel(near_ref, far_ref, even_ref, level_ref, odd_ref):
    at_x, at_y, chip, high = place_of()
    own, other = (at_x & 1) * 16, (1 - (at_x & 1)) * 16
    side = 1 - (at_x & 1)
    chip_third = (chip + 3 + 2 * high) & 3
    for row in range(3):
        number = ((at_y + (RING - 1 + row)) & (RING - 1)) * 2
        for level in range(2):
            cell = 3 * row + 1 + level - high
            level_ref[cell] = near_ref[own + number + level]
            even_ref[cell] = near_ref[other + number + level]
            odd_ref[cell] = far_ref[(1 - side) * 4 + chip, 2 * row + level]
        cell = 3 * row + 2 * high
        level_ref[cell] = far_ref[side * 4 + chip_third, row]
        even_ref[cell] = far_ref[side * 4 + chip_third, 3 + row]
        odd_ref[cell] = far_ref[(1 - side) * 4 + chip_third, row]


def combine_kernel(received_ref, home_ref, out_ref):
    at_x, at_y, chip, high = place_of()
    own, other = (at_x & 1) * 16, (1 - (at_x & 1)) * 16
    back = back_place(at_x)
    beside = 3 - back
    chip_third = (chip + 5 - 2 * high) & 3
    is_energy = lax.broadcasted_iota(jnp.int32, (4, ATOMS), 0) == 3

    def moved(member, cell):
        return jnp.where(is_energy, 0.0, received_ref[member, cell])

    total = received_ref[0, 0]
    for member in range(1, 16):
        total = total + received_ref[member, 0]
    blank = jnp.where(is_energy, total, 0.0)
    out_ref[...] = jnp.broadcast_to(blank[None], out_ref.shape)
    for row in range(3):
        number = ((at_y + (RING - 1 + row)) & (RING - 1)) * 2
        for level in range(2):
            cell = 2 * row + level
            mine = home_ref[cell] + moved(beside * 4 + chip, cell)
            out_ref[own + number + level] = blank + mine
            out_ref[other + number + level] = blank + home_ref[6 + cell]
        across = number + 1 - high
        third = moved(back * 4 + chip_third, row) + moved(beside * 4 + chip_third, row)
        out_ref[own + across] = out_ref[own + across] + third
        out_ref[other + across] = out_ref[other + across] + moved(back * 4 + chip_third, 3 + row)


def finish_kernel(received_ref, forces_ref, energy_ref):
    halves = []
    for start in (0, 16):
        total = received_ref[start]
        for member in range(start + 1, start + 16):
            total = total + received_ref[member]
        halves.append(total)
    total = halves[0] + halves[1]
    for axis in range(3):
        forces_ref[axis] = total[axis : axis + 1]
    energy_ref[0] = jnp.sum(total[3:4]) * (1.0 / (ATOMS * RING**3))


def prepare_kernel(counts_ref, ids_ref, w_out_ref, pairs_ref, hits_ref, same_ref, readout_ref):
    centre = ids_ref[0:1, :]
    neighbour = ids_ref[1:2, :]
    lane = lax.broadcasted_iota(jnp.int32, (1, PAIRS), 1)
    live = lane < jnp.where(lane < ATOMS, counts_ref[0], counts_ref[1] + ATOMS)
    rows = [centre, neighbour >> 7, neighbour & 127, live.astype(jnp.int32)]
    pairs_ref[...] = jnp.concatenate(rows + rows, axis=0)
    atom_row = lax.broadcasted_iota(jnp.int32, (ATOMS, PAIRS), 0)
    hits_ref[0] = jnp.where(atom_row == rows[2], 1.0, 0.0).astype(BF16)
    hits_ref[1] = jnp.where(atom_row == centre, 1.0, 0.0).astype(BF16)
    across = jnp.broadcast_to(centre.astype(F32), (PAIRS, PAIRS))
    same_ref[...] = jnp.where(across == across.T, ENV_NORM, 0.0).astype(BF16)
    readout_ref[...] = jnp.broadcast_to(w_out_ref[...].astype(F32), (ATOMS, LAT)).T.astype(BF16)


def force_kernel(
    pairs_ref,
    hits_ref,
    even_ref,
    level_ref,
    odd_ref,
    same_ref,
    w_in_ref,
    w_in_t_ref,
    w_hid_ref,
    w_hid_t_ref,
    w_env_ref,
    w_env_t_ref,
    w_lat_ref,
    w_lat_t_ref,
    w_out_ref,
    out_ref,
    home_ref,
    z1_ref,
    z2_ref,
    z3_ref,
    hidden_ref,
    joined_ref,
    grad_ref,
    dz_ref,
    dlat_ref,
    spread_ref,
):
    centre = pairs_ref[0:1, :]
    slot = pairs_ref[1:2, :]
    atom = pairs_ref[2:3, :]
    live = pairs_ref[3:4, :].astype(F32)
    step_x = (slot * 57) >> 9
    rest = slot - 9 * step_x
    step_y = (rest * 11) >> 5
    step_z = rest - 3 * step_y

    parity = lax.axis_index("gx") & 1
    near, own = [], []
    for half in range(2):
        lanes = slice(half * ATOMS, (half + 1) * ATOMS)
        pick = jnp.broadcast_to(atom[:, lanes], (4, ATOMS))
        slot_half = jnp.broadcast_to(slot[:, lanes], (4, ATOMS))
        total = jnp.zeros((4, ATOMS), F32)
        for slab, base in ((even_ref, 18 * (1 - parity)), (level_ref, 9), (odd_ref, 18 * parity)):
            for cell in range(9):
                rows = jnp.take_along_axis(slab[cell], pick, axis=1, mode="promise_in_bounds")
                total = jnp.where(slot_half == base + cell, rows, total)
        near.append(total)
        pick = jnp.broadcast_to(centre[:, lanes], (4, ATOMS))
        own.append(jnp.take_along_axis(level_ref[4], pick, axis=1, mode="promise_in_bounds"))
    near = jnp.concatenate(near, axis=1)
    own = jnp.concatenate(own, axis=1)
    delta = [
        near[axis : axis + 1, :]
        + (step - 1).astype(F32) * EXTENT[axis]
        - own[axis : axis + 1, :]
        for axis, step in enumerate((step_x, step_y, step_z))
    ]

    radius = jnp.sqrt(delta[0] * delta[0] + delta[1] * delta[1] + delta[2] * delta[2] + SOFTEN)
    inverse = 1.0 / radius
    ratio = radius * (1.0 / CUTOFF)
    inside = jnp.where(ratio < 1.0, live, 0.0)
    square = ratio * ratio
    fifth = square * square * ratio
    sixth = fifth * ratio
    cut = inside * (1.0 + sixth * (-28.0 + 48.0 * ratio - 21.0 * square))
    slope = inside * (-168.0 / CUTOFF) * fifth * (1.0 - ratio) * (1.0 - ratio)

    row8 = lax.broadcasted_iota(jnp.int32, (8, PAIRS), 0)
    order = (row8 + 1).astype(F32)
    turns = order * ratio
    whole = jnp.floor(turns + 0.5)
    sign = 1.0 - 2.0 * (whole.astype(jnp.int32) & 1).astype(F32)
    angle = (turns - whole) * math.pi
    angle2 = angle * angle
    sine = jnp.zeros_like(angle)
    for power in (11, 9, 7, 5, 3, 1):
        sine = sine * angle2 + (-1.0) ** (power // 2) / math.factorial(power)
    sine = sine * angle * sign
    cosine = jnp.zeros_like(angle)
    for power in (12, 10, 8, 6, 4, 2, 0):
        cosine = cosine * angle2 + (-1.0) ** (power // 2) / math.factorial(power)
    cosine = cosine * sign
    front = math.sqrt(2.0 / CUTOFF)
    bessel = front * sine * inverse
    bessel_slope = (front * math.pi / CUTOFF) * order * cosine * inverse - bessel * inverse

    kind_at = jnp.where(row8 < 2, own[3:4, :], near[3:4, :])
    kind = jnp.where((row8 < 4) & (kind_at == (row8 & 1).astype(F32)), 1.0, 0.0)
    features = jnp.concatenate([bessel * cut, kind], axis=0).astype(BF16)

    for start in range(0, LAT, ROWS):
        rows = pl.ds(start, ROWS)
        value, gate = silu_parts(
            jnp.dot(w_in_ref[rows, :], features, preferred_element_type=F32)
        )
        hidden_ref[rows, :] = value.astype(BF16)
        z1_ref[rows, :] = gate
    for start in range(0, LAT, ROWS):
        rows = pl.ds(start, ROWS)
        z2 = jnp.dot(w_hid_ref[rows, :], hidden_ref[...], preferred_element_type=F32)
        z2_ref[rows, :] = z2
        value, unused = silu_parts(z2)
        joined_ref[rows, :] = (value * cut).astype(BF16)

    unit = [part * inverse for part in delta]
    along_x, along_y, along_z = unit
    zero = jnp.zeros_like(along_x)
    first = [ROOT3 * along_x, ROOT3 * along_y, ROOT3 * along_z]
    second = [
        ROOT15 * along_x * along_y,
        ROOT15 * along_y * along_z,
        0.5 * ROOT5 * (2.0 * along_z * along_z - along_x * along_x - along_y * along_y),
        ROOT15 * along_x * along_z,
        0.5 * ROOT15 * (along_x * along_x - along_y * along_y),
    ]
    shapes = [
        jnp.concatenate(rows + [zero] * (16 - len(rows)), axis=0).astype(BF16)
        for rows in (first, second)
    ]
    same = same_ref[...]
    links = [same] + [dot_tn(rows, rows).astype(BF16) * same for rows in shapes]
    weight = jnp.dot(w_env_ref[...], joined_ref[0:LAT, :], preferred_element_type=F32)
    z3_ref[...] = jnp.dot(
        w_lat_ref[:, 0:LAT], joined_ref[0:LAT, :], preferred_element_type=F32
    )
    weight_b = weight.astype(BF16)
    sums = [jnp.dot(weight_b, link, preferred_element_type=F32) for link in links]
    for degree in range(3):
        rows = slice(LAT + degree * CH, LAT + (degree + 1) * CH)
        joined_ref[rows, :] = (weight * sums[degree]).astype(BF16)

    z3_ref[...] += jnp.dot(
        w_lat_ref[:, LAT:], joined_ref[LAT:, :], preferred_element_type=F32
    )
    energy = jnp.zeros((8, PAIRS), F32)
    cut_grad = jnp.zeros((8, PAIRS), F32)
    for start in range(0, LAT, ROWS):
        rows = pl.ds(start, ROWS)
        value, gate = silu_parts(z3_ref[rows, :])
        readout = w_out_ref[rows, :].astype(F32)
        readout = jnp.concatenate([readout, readout], axis=1)
        updated = (joined_ref[rows, :].astype(F32) + value * cut).astype(BF16).astype(F32)
        energy = energy + folded(readout * updated)
        cut_grad = cut_grad + folded(readout * value)
        dz_ref[rows, :] = (readout * cut * gate).astype(BF16)

    grad_ref[LAT:, :] = jnp.dot(w_lat_t_ref[LAT:, :], dz_ref[...], preferred_element_type=F32)
    grad_ref[0:LAT, :] = jnp.dot(w_lat_t_ref[0:LAT, :], dz_ref[...], preferred_element_type=F32)
    weight_grad = jnp.zeros_like(weight)
    passes = []
    for degree in range(3):
        inv_grad = grad_ref[LAT + degree * CH : LAT + (degree + 1) * CH, :]
        passed = (inv_grad * weight).astype(BF16)
        weight_grad = weight_grad + inv_grad * sums[degree]
        weight_grad = weight_grad + jnp.dot(passed, links[degree], preferred_element_type=F32)
        passes.append(passed)
    dlat_ref[...] = jnp.dot(
        w_env_t_ref[...], weight_grad.astype(BF16), preferred_element_type=F32
    )
    for start in range(0, LAT, ROWS):
        rows = pl.ds(start, ROWS)
        readout = w_out_ref[rows, :].astype(F32)
        readout = jnp.concatenate([readout, readout], axis=1)
        value, gate = silu_parts(z2_ref[rows, :])
        dlat = readout + grad_ref[rows, :] + dlat_ref[rows, :]
        cut_grad = cut_grad + folded(dlat * value)
        dz_ref[rows, :] = (dlat * cut * gate).astype(BF16)
    shape_grad = []
    for degree in (1, 2):
        passed = passes[degree]
        both = dot_tn(
            jnp.concatenate([weight_b, passed], axis=0),
            jnp.concatenate([passed, weight_b], axis=0),
        )
        both = both.astype(BF16) * same
        shape_grad.append(jnp.dot(shapes[degree - 1], both, preferred_element_type=F32))
    for start in range(0, LAT, ROWS):
        rows = pl.ds(start, ROWS)
        hidden_grad = jnp.dot(w_hid_t_ref[rows, :], dz_ref[...], preferred_element_type=F32)
        hidden_ref[rows, :] = (hidden_grad * z1_ref[rows, :]).astype(BF16)
    feature_grad = jnp.dot(w_in_t_ref[...], hidden_ref[...], preferred_element_type=F32)[0:8, :]

    cut_grad = column_sum(cut_grad + feature_grad * bessel)
    radius_grad = cut_grad * slope + cut * column_sum(feature_grad * bessel_slope)
    g1, g2, g3 = [shape_grad[0][i : i + 1] for i in range(3)]
    g4, g5, g6, g7, g8 = [shape_grad[1][i : i + 1] for i in range(5)]
    unit_grad = [
        ROOT3 * g1 + ROOT15 * (along_y * g4 + along_z * g7 + along_x * g8) - ROOT5 * along_x * g6,
        ROOT3 * g2 + ROOT15 * (along_x * g4 + along_z * g5 - along_y * g8) - ROOT5 * along_y * g6,
        ROOT3 * g3 + ROOT15 * (along_y * g5 + along_x * g7) + 2.0 * ROOT5 * along_z * g6,
    ]
    radial = sum(g * u for g, u in zip(unit_grad, unit))
    radius_grad = radius_grad - radial * inverse
    push = [g * inverse + radius_grad * u for g, u in zip(unit_grad, unit)]

    row = lax.broadcasted_iota(jnp.int32, (112, PAIRS), 0)
    axis = row & 3
    moved = jnp.where(axis == 0, push[0], jnp.where(axis == 1, push[1], push[2]))
    moved = jnp.where(axis == 3, 0.0, moved)
    spread = split_dot_nt(jnp.where((row >> 2) == slot, -moved, 0.0), hits_ref[0])
    home = split_dot_nt(moved[0:8], hits_ref[1])[0:4]
    spread_ref[...] = spread.reshape(28, 4, ATOMS)
    spread_ref[13] = spread_ref[13] + home
    energy = column_sum(energy)
    energy = energy[:, 0:ATOMS] + energy[:, ATOMS:PAIRS]
    is_energy = lax.broadcasted_iota(jnp.int32, (4, ATOMS), 0) == 3
    blank = jnp.where(is_energy, energy, 0.0)
    out_ref[...] = jnp.broadcast_to(blank[None, None], out_ref.shape)
    at_x, unused, chip, high = place_of()
    aligned, shifted = 18 * (1 - parity), 18 * parity
    back = back_place(at_x)
    beside = 3 - back
    chip_third = (chip + 3 + 2 * high) & 3
    for row in range(3):
        for level in range(2):
            cell, slot_at = 2 * row + level, 3 * row + 1 + level - high
            home_ref[cell] = spread_ref[9 + slot_at]
            home_ref[6 + cell] = spread_ref[aligned + slot_at]
            out_ref[beside * 4 + chip, cell] = blank + spread_ref[shifted + slot_at]
        slot_at = 3 * row + 2 * high
        out_ref[back * 4 + chip_third, row] = blank + spread_ref[9 + slot_at]
        out_ref[back * 4 + chip_third, 3 + row] = blank + spread_ref[aligned + slot_at]
        out_ref[beside * 4 + chip_third, row] = blank + spread_ref[shifted + slot_at]


def pair_forces(*operands):
    vmem = pl.BlockSpec(memory_space=pltpu.VMEM)
    return pl.pallas_call(
        force_kernel,
        out_shape=(
            jax.ShapeDtypeStruct((16, 6, 4, ATOMS), F32),
            jax.ShapeDtypeStruct((12, 4, ATOMS), F32),
        ),
        in_specs=[vmem] * 15,
        out_specs=(vmem, vmem),
        scratch_shapes=[
            pltpu.VMEM((LAT, PAIRS), F32),
            pltpu.VMEM((LAT, PAIRS), F32),
            pltpu.VMEM((LAT, PAIRS), F32),
            pltpu.VMEM((LAT, PAIRS), BF16),
            pltpu.VMEM((LAT + 3 * CH, PAIRS), BF16),
            pltpu.VMEM((LAT + 3 * CH, PAIRS), F32),
            pltpu.VMEM((LAT, PAIRS), BF16),
            pltpu.VMEM((LAT, PAIRS), F32),
            pltpu.VMEM((28, 4, ATOMS), F32),
        ],
        compiler_params=pltpu.CompilerParams(vmem_limit_bytes=24 * 1024 * 1024),
        name="forces_of_pairs",
    )(*operands)


SMALL = pltpu.CompilerParams(vmem_limit_bytes=2 * 1024 * 1024)
AXES = ("gx", "gy", "gz")


def flat(at_x, at_y, chip, high):
    return ((at_x % RING) * RING + at_y) * RING + 2 * chip + high


NEAR = [
    [flat(2 * pair + i, at_y, chip, high) for i in range(2) for at_y in range(8) for high in range(2)]
    for pair in range(4)
    for chip in range(4)
]
FAR = [
    [flat(2 * pair + 1 + i, at_y, chip, high) for i in range(2) for chip in range(4)]
    for pair in range(4)
    for at_y in range(8)
    for high in range(2)
]
BACK = [
    [flat(base + i, at_y, chip, high) for i in (0, 5, 4, 1) for chip in range(4)]
    for base in (1, 3)
    for at_y in range(8)
    for high in range(2)
]


def body(coords, species, pair_ids, live_counts, w_two_in, w_two_hid, w_env, w_latent, w_out):
    ids = pair_ids[0, 0, 0]
    counts = live_counts[0, 0, 0]
    vmem = pl.BlockSpec(memory_space=pltpu.VMEM)
    smem = pl.BlockSpec(memory_space=pltpu.SMEM)
    packed = pl.pallas_call(
        pack_kernel,
        out_shape=jax.ShapeDtypeStruct((32, 4, ATOMS), F32),
        in_specs=[vmem],
        out_specs=vmem,
        compiler_params=SMALL,
        name="pack_frame",
    )(jnp.concatenate([coords[0, 0, 0], species[0, 0, 0].astype(F32)[None]], axis=0))
    near = lax.all_to_all(packed, AXES, 0, 0, axis_index_groups=NEAR)
    relayed = pl.pallas_call(
        relay_kernel,
        out_shape=jax.ShapeDtypeStruct((8, 6, 4, ATOMS), F32),
        in_specs=[vmem],
        out_specs=vmem,
        compiler_params=SMALL,
        name="relay_frames",
    )(near)
    far = lax.all_to_all(relayed, AXES, 0, 0, axis_index_groups=FAR)
    even, plane, odd = pl.pallas_call(
        pick_kernel,
        out_shape=(jax.ShapeDtypeStruct((9, 4, ATOMS), F32),) * 3,
        in_specs=[vmem] * 2,
        out_specs=(vmem,) * 3,
        compiler_params=SMALL,
        name="pick_planes",
    )(near, far)

    pairs, hits, same, readout = pl.pallas_call(
        prepare_kernel,
        out_shape=(
            jax.ShapeDtypeStruct((8, PAIRS), jnp.int32),
            jax.ShapeDtypeStruct((2, ATOMS, PAIRS), BF16),
            jax.ShapeDtypeStruct((PAIRS, PAIRS), BF16),
            jax.ShapeDtypeStruct((LAT, ATOMS), BF16),
        ),
        in_specs=[smem, vmem, vmem],
        out_specs=(vmem,) * 4,
        compiler_params=SMALL,
        name="prepare_pairs",
    )(counts, ids, w_out)
    w_in = jnp.pad(w_two_in, ((0, 0), (0, 4)))
    sent, home = pair_forces(
        pairs,
        hits,
        even,
        plane,
        odd,
        same,
        w_in,
        w_in.T,
        w_two_hid,
        w_two_hid.T,
        w_env,
        w_env.T,
        w_latent,
        w_latent.T,
        readout,
    )
    combined = pl.pallas_call(
        combine_kernel,
        out_shape=jax.ShapeDtypeStruct((32, 4, ATOMS), F32),
        in_specs=[vmem] * 2,
        out_specs=vmem,
        compiler_params=SMALL,
        name="combine_forces",
    )(lax.all_to_all(sent, AXES, 0, 0, axis_index_groups=BACK), home)
    forces, energy = pl.pallas_call(
        finish_kernel,
        out_shape=(jax.ShapeDtypeStruct((3, 1, ATOMS), F32), jax.ShapeDtypeStruct((1,), F32)),
        in_specs=[vmem],
        out_specs=(vmem, smem),
        compiler_params=SMALL,
        name="finish",
    )(lax.all_to_all(combined, AXES, 0, 0, axis_index_groups=NEAR))
    return forces.reshape(1, 1, 1, 3, ATOMS), energy.reshape(())


def solution(mesh):
    in_specs = (
        P("gx", "gy", "gz", None, None),
        P("gx", "gy", "gz", None),
        P("gx", "gy", "gz", None, None),
        P("gx", "gy", "gz", None),
        P(),
        P(),
        P(),
        P(),
        P(),
    )
    out_specs = (P("gx", "gy", "gz", None, None), P())
    return jax.shard_map(body, mesh=mesh, in_specs=in_specs, out_specs=out_specs, check_vma=False)
```
